32 devices in a mesh: val: 16 (over z, y, core), qry: 2 (over x).
Axes of the slice: x: 2, y: 2, z: 4, core: 2. Of those that a mesh axis runs over, the one named last changes fastest.
Arguments:
- queries: bfloat16 [3072, 512], P('qry'), may hold values from -20 to 20
- pool_keys: bfloat16 [8192, 512], P('val'), may hold values from -20 to 20
- pool_values: bfloat16 [8192, 512], P('val'), may hold values from -6 to 6
- out_grad: bfloat16 [3072, 512], P('qry'), may hold values from -6 to 6
- lse: float32 [2, 3072], P(None, 'qry'), as said below
- compat: int32 [2, 16, 12], P(None, 'val', 'qry'), may hold values from 0 to 1, as said below
- targets: int32 [3072, 2], P('qry'), may hold values from 0 to 8191
Outputs:
- query_grad: bfloat16 [3072, 512], P('qry')
- key_grad: bfloat16 [8192, 512], P(('val', 'qry'))
- value_grad: bfloat16 [8192, 512], P(('val', 'qry'))
The draws below stay inside these ranges and needn't reach their ends.
Inputs may be any that keep to these rules, and one draw needn't show every extreme that they name: `lse`: the forward pass's value: the log of the sum over allowed j of exp(scores[h, i, j]). `compat`: 1 where a block of 512 pool values and a block of 256 queries are type-compatible for that head.
All inputs are finite; a program needn't handle non-finite values.
Results may differ from the reference program's by a relative error of at most 0.0053.
Values may be sent and summed in bfloat16 or wider, within the bound.
No kernel may reach another device: no remote copies, remote signals or barrier semaphores. Data moves between devices by JAX's collectives and lax.ppermute only.
A program may use at most 128 MiB of HBM per device.

```python
import jax
import jax.numpy as jnp
from jax import lax

HEADS = 2
HD = 256
VB = 512
QB = 256
QRY_DEV = 1536
VALUES = 8192
QUERIES = 3072
NVB = 16
NQB = 12


def shared_compat(key):
    block_level = jax.random.randint(jax.random.fold_in(key, 31), (HEADS, NVB, 1), 1, 5)
    mask_rolls = jax.random.randint(jax.random.fold_in(key, 32), (HEADS, NVB, NQB), 0, 8)
    return (mask_rolls < block_level).astype(jnp.int32)


def shared_targets(key):
    compat_table = shared_compat(key)
    query_block = jnp.arange(QUERIES, dtype=jnp.int32) // QB
    block_marks = jnp.transpose(compat_table, (2, 0, 1))[query_block]
    pick_score = jax.random.randint(jax.random.fold_in(key, 33), (QUERIES, HEADS, NVB), 0, 65536) * NVB + jnp.arange(NVB, dtype=jnp.int32)
    chosen = jnp.argmax(jnp.where(block_marks == 1, pick_score, -1), axis=2).astype(jnp.int32)
    inside = jax.random.randint(jax.random.fold_in(key, 34), (QUERIES, HEADS), 0, VB)
    target_ids = chosen * VB + inside
    target_ids = target_ids.at[0, 0].set(VALUES - 1)
    target_ids = target_ids.at[1, HEADS - 1].set(0)
    return target_ids.astype(jnp.int32)


def draw_queries(key, part):
    drawn_vals = jnp.clip(jax.random.normal(jax.random.fold_in(key, 51), (QUERIES, HEADS * HD), jnp.float32), -5.0, 5.0)
    return drawn_vals.astype(jnp.bfloat16)


def draw_pool_keys(key, part):
    normal_vals = jnp.clip(jax.random.normal(jax.random.fold_in(key, 61), (VALUES, HEADS * HD), jnp.float32), -5.0, 5.0)
    drawn_vals = 2.0 * normal_vals
    return drawn_vals.astype(jnp.bfloat16)


def draw_lse(key, part):
    query_all = draw_queries(key, part)
    key_all = draw_pool_keys(key, part)
    compat_table = shared_compat(key)
    target_ids = shared_targets(key)
    score_scale = HD ** (-0.5)
    block_index = jnp.arange(NVB, dtype=jnp.int32)
    head_rows = []
    for head_index in range(HEADS):
        col_low = head_index * HD
        query_head = query_all[:, col_low:col_low + HD].reshape(NQB, QB, HD)
        key_head = key_all[:, col_low:col_low + HD]
        target_head = target_ids[:, head_index].reshape(NQB, QB)
        marks = jnp.transpose(compat_table[head_index])

        def one_block(items):
            query_tile, target_tile, mark_row = items
            scores = score_scale * jnp.dot(query_tile, key_head.T, preferred_element_type=jnp.float32)
            scores = scores.reshape(QB, NVB, VB)
            usable = (mark_row[None, :] == 1) | ((target_tile // VB)[:, None] == block_index[None, :])
            usable_full = jnp.broadcast_to(usable[:, :, None], scores.shape)
            row_max = jnp.max(jnp.where(usable_full, scores, -1e+30), axis=(1, 2))
            total = jnp.sum(jnp.where(usable_full, jnp.exp(scores - row_max[:, None, None]), 0.0), axis=(1, 2))
            return row_max + jnp.log(total)
        head_rows.append(lax.map(one_block, (query_head, target_head, marks)).reshape(QUERIES))
    return jnp.stack(head_rows).astype(jnp.float32)


def draw_compat(key, part):
    return shared_compat(key)


def draw_targets(key, part):
    return shared_targets(key)


def levels(stream_key, extent, pieces, least, top_value):
    factor_of, own = 1.0, jax.random.fold_in(stream_key, 6)
    for dim, shards_of in pieces:
        steps = jnp.exp(jax.random.uniform(jax.random.fold_in(own, dim), (shards_of,), jnp.float32, least / len(pieces), top_value / len(pieces)))
        factor_of = factor_of * jnp.repeat(steps, extent[dim] // shards_of).reshape([-1 if axis == dim else 1 for axis in range(len(extent))])
    return factor_of


def scatter_about(own_key, dims, deviation, limit, split=(), held_as=jnp.bfloat16):
    drawn = jax.random.normal(own_key, dims, jnp.float32) * deviation
    if len(split) > 0:
        drawn = levels(own_key, dims, split, -0.22, 0.18) * drawn
    return jnp.clip(drawn, min=-limit, max=limit).astype(held_as)


def setup_inputs(seed: int = 0) -> dict:
    streams_of = jax.random.split(jax.random.key(seed), 8)
    queries = draw_queries(jax.random.fold_in(streams_of[7], 71), 0)
    pool_keys = draw_pool_keys(jax.random.fold_in(streams_of[7], 71), 0)
    pool_values = scatter_about(streams_of[2], (VALUES, HEADS * HD), 1.0, 6.0, ((0, 16),))
    out_grad = scatter_about(streams_of[3], (QUERIES, HEADS * HD), 1.0, 6.0, ((0, 2),))
    lse = draw_lse(jax.random.fold_in(streams_of[7], 71), 0)
    compat = draw_compat(jax.random.fold_in(streams_of[7], 71), 0)
    targets = draw_targets(jax.random.fold_in(streams_of[7], 71), 0)
    return {"queries": queries, "pool_keys": pool_keys, "pool_values": pool_values, "out_grad": out_grad, "lse": lse, "compat": compat, "targets": targets}


def reference(queries, pool_keys, pool_values, out_grad, lse, compat, targets):
    score_scale = HD ** -0.5
    block_count = QUERIES // QRY_DEV
    slot_ids = jnp.arange(VALUES, dtype=jnp.int32)
    block_index = jnp.arange(NVB, dtype=jnp.int32)
    query_outs = []
    key_outs = []
    value_outs = []
    for head_index in range(HEADS):
        col_low = head_index * HD
        key_head = pool_keys[:, col_low:col_low + HD]
        value_head = pool_values[:, col_low:col_low + HD]
        query_blocks = queries[:, col_low:col_low + HD].reshape(block_count, QRY_DEV, HD)
        grad_blocks = out_grad[:, col_low:col_low + HD].reshape(block_count, QRY_DEV, HD)
        target_blocks = targets[:, head_index].reshape(block_count, QRY_DEV)
        lse_blocks = lse[head_index].reshape(block_count, QRY_DEV)
        starts = jnp.arange(block_count, dtype=jnp.int32) * QRY_DEV
        head_marks = compat[head_index]

        def block_step(carried, block_items):
            key_acc, value_acc = carried
            query_tile, grad_tile, target_ids, lse_rows, start_row = block_items
            query_ids = start_row + jnp.arange(QRY_DEV, dtype=jnp.int32)
            per_query = jnp.transpose(head_marks[:, query_ids // QB])
            usable = (per_query == 1) | ((target_ids // VB)[:, None] == block_index[None, :])
            allowed = jnp.broadcast_to(usable[:, :, None], (QRY_DEV, NVB, VB)).reshape(QRY_DEV, VALUES)
            scores = score_scale * jnp.dot(query_tile, key_head.T, preferred_element_type=jnp.float32)
            soft_probs = jnp.where(allowed, jnp.exp(scores - lse_rows[:, None]), 0.0)
            dprobs = jnp.dot(grad_tile, value_head.T, preferred_element_type=jnp.float32)
            row_delta = jnp.sum(soft_probs * dprobs, axis=1, keepdims=True)
            onehot = (target_ids[:, None] == slot_ids[None, :]).astype(jnp.float32)
            dscores = soft_probs * (dprobs - row_delta + 1.0) - onehot
            probs_low = soft_probs.astype(jnp.bfloat16)
            dscores_low = dscores.astype(jnp.bfloat16)
            query_out = score_scale * jnp.dot(dscores_low, key_head, preferred_element_type=jnp.float32)
            key_acc = key_acc + score_scale * jnp.dot(dscores_low.T, query_tile, preferred_element_type=jnp.float32)
            value_acc = value_acc + jnp.dot(probs_low.T, grad_tile, preferred_element_type=jnp.float32)
            return (key_acc, value_acc), query_out

        start_carry = (jnp.zeros((VALUES, HD), jnp.float32), jnp.zeros((VALUES, HD), jnp.float32))
        final_carry, query_stack = lax.scan(block_step, start_carry, (query_blocks, grad_blocks, target_blocks, lse_blocks, starts))
        query_outs.append(query_stack.reshape(QUERIES, HD))
        key_outs.append(final_carry[0])
        value_outs.append(final_carry[1])
    query_grad = jnp.concatenate(query_outs, axis=1).astype(jnp.bfloat16)
    key_grad = jnp.concatenate(key_outs, axis=1).astype(jnp.bfloat16)
    value_grad = jnp.concatenate(value_outs, axis=1).astype(jnp.bfloat16)
    return (query_grad, key_grad, value_grad)
```

```python
import math
from functools import partial

import jax
import jax.numpy as jnp
from jax import lax
from jax.experimental import pallas as pl
from jax.experimental.pallas import tpu as pltpu
from jax.sharding import PartitionSpec as P

LOG2E = math.log2(math.e)
MASKED = 1e30
NT = (((1,), (1,)), ((), ()))
NN = (((1,), (0,)), ((), ()))
TN = (((0,), (0,)), ((), ()))
VMEM_LIMIT = 40 * 1024 * 1024


def dot(a, b, dims):
    return lax.dot_general(a, b, dims, preferred_element_type=jnp.float32)


def row_terms(place, compat, lse_ref, targets_ref, head, block, value_count):
    target = targets_ref[pl.ds(head, 1), :]
    local = target - place[0] * value_count
    hit = (local >= 0) & (local < value_count)
    usable = hit | (compat[head, 0, block] == 1)
    lse_rows = jnp.where(usable, lse_ref[pl.ds(head, 1), :], MASKED) * LOG2E
    return lse_rows, local


def scatter_rows(place, total, own_ref, send_ref, columns):
    parts = send_ref.shape[0] + 1
    share = total.shape[0] // parts
    start = pl.multiple_of(place[1] * share, share)
    own_ref[:, columns] = total[pl.ds(start, share), :]
    for step in range(1, parts):
        other = lax.rem(place[1] + step, parts)
        start = pl.multiple_of(other * share, share)
        send_ref[step - 1, :, columns] = total[pl.ds(start, share), :].astype(jnp.bfloat16)


def forward_kernel(
    place, compat, q_ref, g_ref, k_ref, v_ref, lse_ref, targets_ref,
    delta_ref, own_ref, send_ref, total, *, heads, scale,
):
    block = pl.program_id(0)
    value_count, width = k_ref.shape[0], k_ref.shape[1] // heads
    for head in range(heads):
        columns = slice(head * width, (head + 1) * width)
        lse_rows, _ = row_terms(place, compat, lse_ref, targets_ref, head, block, value_count)
        scores = dot(k_ref[:, columns], q_ref[:, columns], NT)
        probs = jnp.exp2(scores * (scale * LOG2E) - lse_rows)
        dprobs = dot(v_ref[:, columns], g_ref[:, columns], NT)
        delta_ref[head : head + 1, :] = jnp.sum(probs * dprobs, axis=0, keepdims=True)
        term = dot(probs.astype(jnp.bfloat16), g_ref[:, columns], NN)

        @pl.when(block == 0)
        def _():
            total[head] = term

        @pl.when(block > 0)
        def _():
            total[head] += term

    @pl.when(block == pl.num_programs(0) - 1)
    def _():
        for head in range(heads):
            columns = slice(head * width, (head + 1) * width)
            scatter_rows(place, total.at[head], own_ref, send_ref, columns)


def backward_kernel(
    place, compat, q_ref, g_ref, k_ref, v_ref, lse_ref, targets_ref, delta_ref,
    query_ref, own_ref, send_ref, total, *, scale,
):
    block = pl.program_id(0)
    head = place[2]
    value_count = k_ref.shape[0]
    lse_rows, local = row_terms(place, compat, lse_ref, targets_ref, head, block, value_count)
    delta_rows = delta_ref[pl.ds(head, 1), :] - 1.0
    scores = dot(k_ref[...], q_ref[...], NT)
    probs = jnp.exp2(scores * (scale * LOG2E) - lse_rows)
    dprobs = dot(v_ref[...], g_ref[...], NT)
    dscores = probs * (dprobs - delta_rows)
    slots = lax.broadcasted_iota(jnp.int32, dscores.shape, 0)
    low = jnp.where(slots == local, dscores - 1.0, dscores).astype(jnp.bfloat16)
    query_ref[...] = (scale * dot(low, k_ref[...], TN)).astype(query_ref.dtype)
    term = scale * dot(low, q_ref[...], NN)

    @pl.when(block == 0)
    def _():
        total[...] = term

    @pl.when(block > 0)
    def _():
        total[...] += term

    @pl.when(block == pl.num_programs(0) - 1)
    def _():
        scatter_rows(place, total, own_ref, send_ref, slice(None))


def cost(queries, values, width, dots):
    return pl.CostEstimate(
        flops=2 * dots * queries * values * width,
        bytes_accessed=4 * (queries + values) * width,
        transcendentals=queries * values,
    )


def forward(place, compat, queries, keys, values, grads, lse, targets, parts):
    heads, _, blocks = compat.shape
    query_count, wide = queries.shape
    value_count = keys.shape[0]
    block = query_count // blocks
    share = value_count // parts
    rows = pl.BlockSpec((block, wide), lambda i, *_: (i, 0))
    pool = pl.BlockSpec((value_count, wide), lambda i, *_: (0, 0))
    flat = pl.BlockSpec((heads, block), lambda i, *_: (0, i))
    return pl.pallas_call(
        partial(forward_kernel, heads=heads, scale=(wide // heads) ** -0.5),
        grid_spec=pltpu.PrefetchScalarGridSpec(
            num_scalar_prefetch=2,
            grid=(blocks,),
            in_specs=[rows, rows, pool, pool, flat, flat],
            out_specs=[
                flat,
                pl.BlockSpec((share, wide), lambda i, *_: (0, 0)),
                pl.BlockSpec((parts - 1, share, wide), lambda i, *_: (0, 0, 0)),
            ],
            scratch_shapes=[pltpu.VMEM((heads, value_count, wide // heads), jnp.float32)],
        ),
        out_shape=[
            jax.ShapeDtypeStruct((heads, query_count), jnp.float32),
            jax.ShapeDtypeStruct((share, wide), jnp.float32),
            jax.ShapeDtypeStruct((parts - 1, share, wide), jnp.bfloat16),
        ],
        cost_estimate=cost(query_count, value_count, wide, 3),
        compiler_params=pltpu.CompilerParams(vmem_limit_bytes=VMEM_LIMIT),
        name="forward_pass",
    )(place, compat, queries, grads, keys, values, lse, targets)


def backward(place, compat, queries, keys, values, grads, lse, targets, delta, parts, out_dtype):
    heads, _, blocks = compat.shape
    query_count, wide = queries.shape
    width = wide // heads
    value_count = keys.shape[0]
    block = query_count // blocks
    share = value_count // parts
    rows = pl.BlockSpec((block, width), lambda i, place, _: (i, place[2]))
    pool = pl.BlockSpec((value_count, width), lambda i, place, _: (0, place[2]))
    flat = pl.BlockSpec((heads, block), lambda i, *_: (0, i))
    return pl.pallas_call(
        partial(backward_kernel, scale=width ** -0.5),
        grid_spec=pltpu.PrefetchScalarGridSpec(
            num_scalar_prefetch=2,
            grid=(blocks,),
            in_specs=[rows, rows, pool, pool, flat, flat, flat],
            out_specs=[
                pl.BlockSpec((block, width), lambda i, *_: (i, 0)),
                pl.BlockSpec((share, width), lambda i, *_: (0, 0)),
                pl.BlockSpec((parts - 1, share, width), lambda i, *_: (0, 0, 0)),
            ],
            scratch_shapes=[pltpu.VMEM((value_count, width), jnp.float32)],
        ),
        out_shape=[
            jax.ShapeDtypeStruct((query_count, width), out_dtype),
            jax.ShapeDtypeStruct((share, width), jnp.float32),
            jax.ShapeDtypeStruct((parts - 1, share, width), jnp.bfloat16),
        ],
        cost_estimate=cost(query_count, value_count, width, 4),
        compiler_params=pltpu.CompilerParams(vmem_limit_bytes=VMEM_LIMIT),
        name="backward_pass",
    )(place, compat, queries, grads, keys, values, lse, targets, delta)


def assemble_kernel(place, mine_ref, theirs_ref, out_ref, sems, *, chains, radix_y, radix_z):
    core, y, z = place[0], place[1], place[2]
    piece, width = mine_ref.shape[-2:]
    pieces = radix_y * radix_z
    copies = []
    for side, ref in enumerate((mine_ref, theirs_ref)):
        columns = pl.ds(pl.multiple_of((core ^ side) * width, width), width)
        for chain in range(chains):
            for step_y in range(radix_y):
                for step_z in range(radix_z):
                    index = chain * pieces + (y ^ step_y) * radix_z + (z ^ step_z)
                    rows = pl.ds(pl.multiple_of(index * piece, piece), piece)
                    copy = pltpu.make_async_copy(
                        ref.at[chain, step_y * radix_z + step_z],
                        out_ref.at[rows, columns],
                        sems.at[len(copies)],
                    )
                    copy.start()
                    copies.append(copy)
    for copy in copies:
        copy.wait()


def assemble(place, mine, theirs, radix_y, radix_z):
    chains, pieces, piece, width = mine.shape
    return pl.pallas_call(
        partial(assemble_kernel, chains=chains, radix_y=radix_y, radix_z=radix_z),
        grid_spec=pltpu.PrefetchScalarGridSpec(
            num_scalar_prefetch=1,
            grid=(),
            in_specs=[pl.BlockSpec(memory_space=pl.ANY)] * 2,
            out_specs=pl.BlockSpec(memory_space=pl.ANY),
            scratch_shapes=[pltpu.SemaphoreType.DMA((2 * chains * pieces,))],
        ),
        out_shape=jax.ShapeDtypeStruct((chains * pieces * piece, 2 * width), mine.dtype),
        name="assemble",
    )(place, mine, theirs)


def on_device(queries, pool_keys, pool_values, out_grad, lse, compat, targets):
    heads, value_blocks, _ = compat.shape
    query_count = queries.shape[0]
    width = queries.shape[1] // heads
    value_devices, parts = lax.axis_size("val"), lax.axis_size("qry")
    assert heads == 2 and value_blocks == 1 and value_devices % 8 == 0
    val, qry = lax.axis_index("val"), lax.axis_index("qry")
    radix_z = 4
    radix_y = value_devices // (2 * radix_z)
    core, y, z = lax.rem(val, 2), lax.rem(val // 2, radix_y), val // (2 * radix_y)

    def flip(array, mask):
        return lax.ppermute(array, "val", [(i, i ^ mask) for i in range(value_devices)])

    def turn(array, step):
        return lax.ppermute(array, "qry", [(i, (i + step) % parts) for i in range(parts)])

    def swap_shares(send):
        return [turn(send[step - 1], step) for step in range(1, parts)]

    def add(own, received):
        for array in received:
            own = own + array.astype(jnp.float32)
        return own

    operands = (compat, queries, pool_keys, pool_values, out_grad, lse, jnp.transpose(targets))

    def place(head):
        return jnp.stack([val, qry, head]).astype(jnp.int32)

    delta, value_own, value_send = forward(place(core), *operands, parts)
    stride = 1
    while stride < value_devices:
        delta = add(delta, [flip(delta, stride * step) for step in range(1, 4)])
        stride *= 4
    value_received = swap_shares(value_send)

    query_send, other_own, other_send = backward(
        place(1 - core), *operands, delta, parts, jnp.bfloat16
    )
    query_received = flip(query_send, 1)
    other_received = swap_shares(other_send)
    query_own, key_own, key_send = backward(place(core), *operands, delta, parts, jnp.float32)
    key_received = swap_shares(key_send)
    query_sum = add(query_own, [query_received])

    pieces = radix_y * radix_z
    chains = 2 if query_count % (2 * pieces * 16) == 0 else 1
    mine = []
    for chain in range(chains):
        rows = query_count // chains
        part = query_sum[chain * rows : (chain + 1) * rows]
        for radix, digit, stride in ((radix_y, y, 2), (radix_z, z, 2 * radix_y)):
            split = part.reshape(radix, part.shape[0] // radix, width)

            def pick(index):
                return lax.dynamic_index_in_dim(split, index, 0, keepdims=False)

            received = [
                flip(pick(digit ^ step).astype(jnp.bfloat16), stride * step)
                for step in range(1, radix)
            ]
            part = add(pick(digit), received)
        part = part.astype(jnp.bfloat16)[None]
        for radix, stride in ((radix_z, 2 * radix_y), (radix_y, 2)):
            part = jnp.concatenate(
                [part] + [flip(part, stride * step) for step in range(1, radix)], axis=0
            )
        mine.append(part)
    mine = jnp.stack(mine)
    theirs = flip(mine, 1)
    query_grad = assemble(
        jnp.stack([core, y, z]).astype(jnp.int32), mine, theirs, radix_y, radix_z
    )

    value_grad = add(value_own, value_received).astype(jnp.bfloat16)
    key_mine = add(key_own, key_received).astype(jnp.bfloat16)
    key_other = add(other_own, other_received).astype(jnp.bfloat16)
    key_grad = jnp.where(
        core == 0,
        jnp.concatenate([key_mine, key_other], axis=1),
        jnp.concatenate([key_other, key_mine], axis=1),
    )
    return query_grad, key_grad, value_grad


def solution(mesh):
    placed = (
        P("qry", None),
        P("val", None),
        P("val", None),
        P("qry", None),
        P(None, "qry"),
        P(None, "val", "qry"),
        P("qry", None),
    )
    return jax.shard_map(
        on_device,
        mesh=mesh,
        in_specs=placed,
        out_specs=(P("qry", None), P(("val", "qry"), None), P(("val", "qry"), None)),
        check_vma=False,
    )
```

```python
import math
from functools import partial

import jax
import jax.numpy as jnp
from jax import lax
from jax.experimental import pallas as pl
from jax.experimental.pallas import tpu as pltpu
from jax.sharding import PartitionSpec as P

LOG2E = math.log2(math.e)
MASKED = 1e30
NT = (((1,), (1,)), ((), ()))
NN = (((1,), (0,)), ((), ()))
TN = (((0,), (0,)), ((), ()))
VMEM_LIMIT = 60 * 1024 * 1024


def dot(a, b, dims):
    return lax.dot_general(a, b, dims, preferred_element_type=jnp.float32)


def row_terms(place, compat, lse_ref, targets_ref, head, block, value_count):
    target = targets_ref[pl.ds(head, 1), :]
    local = target - place[0] * value_count
    hit = (local >= 0) & (local < value_count)
    usable = hit | (compat[head, 0, block] == 1)
    lse_rows = jnp.where(usable, lse_ref[pl.ds(head, 1), :], MASKED) * LOG2E
    return lse_rows, local


def scatter_rows(place, total, own_ref, send_ref, columns):
    parts = send_ref.shape[0] + 1
    share = total.shape[0] // parts
    start = pl.multiple_of(place[1] * share, share)
    own_ref[:, columns] = total[pl.ds(start, share), :]
    for step in range(1, parts):
        other = lax.rem(place[1] + step, parts)
        start = pl.multiple_of(other * share, share)
        send_ref[step - 1, :, columns] = total[pl.ds(start, share), :].astype(jnp.bfloat16)


def forward_kernel(
    place, compat, q_ref, g_ref, k_ref, v_ref, lse_ref, targets_ref,
    delta_ref, own_ref, send_ref, total, *, heads, scale,
):
    block = pl.program_id(0)
    value_count, width = k_ref.shape[0], k_ref.shape[1] // heads
    for head in range(heads):
        columns = slice(head * width, (head + 1) * width)
        lse_rows, _ = row_terms(place, compat, lse_ref, targets_ref, head, block, value_count)
        scores = dot(k_ref[:, columns], q_ref[:, columns], NT)
        probs = jnp.exp2(scores * (scale * LOG2E) - lse_rows)
        dprobs = dot(v_ref[:, columns], g_ref[:, columns], NT)
        delta_ref[head : head + 1, :] = jnp.sum(probs * dprobs, axis=0, keepdims=True)
        term = dot(probs.astype(jnp.bfloat16), g_ref[:, columns], NN)

        @pl.when(block == 0)
        def _():
            total[head] = term

        @pl.when(block > 0)
        def _():
            total[head] += term

    @pl.when(block == pl.num_programs(0) - 1)
    def _():
        for head in range(heads):
            columns = slice(head * width, (head + 1) * width)
            scatter_rows(place, total.at[head], own_ref, send_ref, columns)


def backward_kernel(
    place, compat, q_ref, g_ref, k_ref, v_ref, lse_ref, targets_ref, delta_ref, *rest, scale,
):
    *earlier, query_ref, own_ref, send_ref, total = rest
    block = pl.program_id(0)
    head = place[2]
    value_count = k_ref.shape[0]
    lse_rows, local = row_terms(place, compat, lse_ref, targets_ref, head, block, value_count)
    delta_rows = delta_ref[pl.ds(head, 1), :] - 1.0
    scores = dot(k_ref[...], q_ref[...], NT)
    probs = jnp.exp2(scores * (scale * LOG2E) - lse_rows)
    dprobs = dot(v_ref[...], g_ref[...], NT)
    dscores = probs * (dprobs - delta_rows)
    slots = lax.broadcasted_iota(jnp.int32, dscores.shape, 0)
    low = jnp.where(slots == local, dscores - 1.0, dscores).astype(jnp.bfloat16)
    query_ref[...] = (scale * dot(low, k_ref[...], TN)).astype(query_ref.dtype)
    term = scale * dot(low, q_ref[...], NN)

    @pl.when(block == 0)
    def _():
        total[...] = term

    @pl.when(block > 0)
    def _():
        total[...] += term

    @pl.when(block == pl.num_programs(0) - 1)
    def _():
        width = total.shape[1]
        if earlier:
            earlier_own, earlier_send = earlier
            columns = pl.ds(pl.multiple_of((1 - head) * width, width), width)
            own_ref[:, columns] = earlier_own[...]
            send_ref[:, :, columns] = earlier_send[...]
            columns = pl.ds(pl.multiple_of(head * width, width), width)
        else:
            columns = slice(None)
        scatter_rows(place, total, own_ref, send_ref, columns)


def cost(queries, values, width, dots):
    return pl.CostEstimate(
        flops=2 * dots * queries * values * width,
        bytes_accessed=4 * (queries + values) * width,
        transcendentals=queries * values,
    )


def forward(place, compat, queries, keys, values, grads, lse, targets, parts):
    heads, _, blocks = compat.shape
    query_count, wide = queries.shape
    value_count = keys.shape[0]
    block = query_count // blocks
    share = value_count // parts
    rows = pl.BlockSpec((block, wide), lambda i, *_: (i, 0))
    pool = pl.BlockSpec((value_count, wide), lambda i, *_: (0, 0))
    flat = pl.BlockSpec((heads, block), lambda i, *_: (0, i))
    return pl.pallas_call(
        partial(forward_kernel, heads=heads, scale=(wide // heads) ** -0.5),
        grid_spec=pltpu.PrefetchScalarGridSpec(
            num_scalar_prefetch=2,
            grid=(blocks,),
            in_specs=[rows, rows, pool, pool, flat, flat],
            out_specs=[
                flat,
                pl.BlockSpec((share, wide), lambda i, *_: (0, 0)),
                pl.BlockSpec((parts - 1, share, wide), lambda i, *_: (0, 0, 0)),
            ],
            scratch_shapes=[pltpu.VMEM((heads, value_count, wide // heads), jnp.float32)],
        ),
        out_shape=[
            jax.ShapeDtypeStruct((heads, query_count), jnp.float32),
            jax.ShapeDtypeStruct((share, wide), jnp.float32),
            jax.ShapeDtypeStruct((parts - 1, share, wide), jnp.bfloat16),
        ],
        cost_estimate=cost(query_count, value_count, wide, 3),
        compiler_params=pltpu.CompilerParams(vmem_limit_bytes=VMEM_LIMIT),
        name="forward_pass",
    )(place, compat, queries, grads, keys, values, lse, targets)


def backward(
    place, compat, queries, keys, values, grads, lse, targets, delta, parts, out_dtype, earlier=()
):
    heads, _, blocks = compat.shape
    query_count, wide = queries.shape
    width = wide // heads
    value_count = keys.shape[0]
    block = query_count // blocks
    share = value_count // parts
    rows = pl.BlockSpec((block, width), lambda i, place, _: (i, place[2]))
    pool = pl.BlockSpec((value_count, width), lambda i, place, _: (0, place[2]))
    flat = pl.BlockSpec((heads, block), lambda i, *_: (0, i))
    out_width = wide if earlier else width

    def shares(columns):
        return [
            pl.BlockSpec((share, columns), lambda i, *_: (0, 0)),
            pl.BlockSpec((parts - 1, share, columns), lambda i, *_: (0, 0, 0)),
        ]

    return pl.pallas_call(
        partial(backward_kernel, scale=width ** -0.5),
        grid_spec=pltpu.PrefetchScalarGridSpec(
            num_scalar_prefetch=2,
            grid=(blocks,),
            in_specs=[rows, rows, pool, pool, flat, flat, flat] + (shares(width) if earlier else []),
            out_specs=[pl.BlockSpec((block, width), lambda i, *_: (i, 0))] + shares(out_width),
            scratch_shapes=[pltpu.VMEM((value_count, width), jnp.float32)],
        ),
        out_shape=[
            jax.ShapeDtypeStruct((query_count, width), out_dtype),
            jax.ShapeDtypeStruct((share, out_width), jnp.float32),
            jax.ShapeDtypeStruct((parts - 1, share, out_width), jnp.bfloat16),
        ],
        cost_estimate=cost(query_count, value_count, width, 4),
        compiler_params=pltpu.CompilerParams(vmem_limit_bytes=VMEM_LIMIT),
        name="backward_pass",
    )(place, compat, queries, grads, keys, values, lse, targets, delta, *earlier)


def on_device(queries, pool_keys, pool_values, out_grad, lse, compat, targets):
    heads, value_blocks, _ = compat.shape
    query_count = queries.shape[0]
    width = queries.shape[1] // heads
    value_devices, parts = lax.axis_size("val"), lax.axis_size("qry")
    assert heads == 2 and value_blocks == 1 and value_devices % 8 == 0
    val, qry = lax.axis_index("val"), lax.axis_index("qry")
    radix_z = 4
    radix_y = value_devices // (2 * radix_z)
    core, y, z = lax.rem(val, 2), lax.rem(val // 2, radix_y), val // (2 * radix_y)

    def flip(array, mask):
        return lax.ppermute(array, "val", [(i, i ^ mask) for i in range(value_devices)])

    def turn(array, step):
        return lax.ppermute(array, "qry", [(i, (i + step) % parts) for i in range(parts)])

    def swap_shares(send):
        return [turn(send[step - 1], step) for step in range(1, parts)]

    def add(own, received):
        for array in received:
            own = own + array.astype(jnp.float32)
        return own

    operands = (compat, queries, pool_keys, pool_values, out_grad, lse, jnp.transpose(targets))

    def place(head):
        return jnp.stack([val, qry, head]).astype(jnp.int32)

    delta, value_own, value_send = forward(place(core), *operands, parts)
    delta = jnp.sum(lax.all_gather(delta, "val"), axis=0)
    value_received = swap_shares(value_send)

    query_send, *earlier = backward(place(1 - core), *operands, delta, parts, jnp.bfloat16)
    query_received = flip(query_send, 1)
    query_own, key_own, key_send = backward(
        place(core), *operands, delta, parts, jnp.float32, tuple(earlier)
    )
    key_received = swap_shares(key_send)
    query_sum = add(query_own, [query_received])

    pieces = radix_y * radix_z
    chains = 2 if query_count % (2 * pieces * 16) == 0 else 1
    piece = query_count // (pieces * chains)
    query_sum = query_sum.reshape(radix_z, radix_y, chains, piece, width)
    mine = []
    for chain in range(chains):
        part = query_sum[:, :, chain]
        for axis, radix, digit, stride in ((1, radix_y, y, 2), (0, radix_z, z, 2 * radix_y)):

            def pick(index):
                return lax.dynamic_index_in_dim(part, index, axis, keepdims=False)

            received = [
                flip(pick(digit ^ step).astype(jnp.bfloat16), stride * step)
                for step in range(1, radix)
            ]
            part = add(pick(digit), received)
        mine.append(part.astype(jnp.bfloat16))
    gathered = lax.all_gather(jnp.concatenate(mine, axis=0), "val")
    gathered = gathered.reshape(pieces, 2, chains * piece, width)
    query_grad = jnp.transpose(gathered, (0, 2, 1, 3)).reshape(query_count, 2 * width)

    value_grad = add(value_own, value_received).astype(jnp.bfloat16)
    key_grad = add(key_own, key_received).astype(jnp.bfloat16)
    return query_grad, key_grad, value_grad


def solution(mesh):
    placed = (
        P("qry", None),
        P("val", None),
        P("val", None),
        P("qry", None),
        P(None, "qry"),
        P(None, "val", "qry"),
        P("qry", None),
    )
    return jax.shard_map(
        on_device,
        mesh=mesh,
        in_specs=placed,
        out_specs=(P("qry", None), P(("val", "qry"), None), P(("val", "qry"), None)),
        check_vma=False,
    )
```

```python
import math
from functools import partial

import jax
import jax.numpy as jnp
from jax import lax
from jax.experimental import pallas as pl
from jax.experimental.pallas import tpu as pltpu
from jax.sharding import PartitionSpec as P

LOG2E = math.log2(math.e)
MASKED = 1e30
NT = (((1,), (1,)), ((), ()))
NN = (((1,), (0,)), ((), ()))
TN = (((0,), (0,)), ((), ()))
PARAMS = pltpu.CompilerParams(vmem_limit_bytes=24 * 1024 * 1024)
IN_VMEM = pl.BlockSpec(memory_space=pltpu.VMEM)
IN_SMEM = pl.BlockSpec(memory_space=pltpu.SMEM)
IN_HBM = pl.BlockSpec(memory_space=pl.ANY)


def dot(a, b, dims):
    return lax.dot_general(a, b, dims, preferred_element_type=jnp.float32)


def ways(start, size):
    return pl.ds(pl.multiple_of(start, size), size)


def forward_kernel(
    place, compat, q_hbm, g_hbm, k_hbm, v_hbm, lse_ref, targets_ref,
    delta_ref, probs_ref, score_ref, q_ref, g_ref, k_ref, v_ref, sems, *, heads, blocks, scale,
):
    value_count, width = k_ref.shape[0], k_ref.shape[1] // heads
    block = q_ref.shape[0] // blocks
    copies = [
        pltpu.make_async_copy(k_hbm, k_ref, sems.at[0]),
        pltpu.make_async_copy(v_hbm, v_ref, sems.at[1]),
    ]
    for index in range(blocks):
        rows = pl.ds(index * block, block)
        for half, (source, target) in enumerate(((q_hbm, q_ref), (g_hbm, g_ref))):
            copies.append(
                pltpu.make_async_copy(source.at[rows], target.at[rows], sems.at[2 + 2 * index + half])
            )
    for copy in copies:
        copy.start()
    copies[0].wait()
    copies[1].wait()
    for index in range(blocks):
        rows = slice(index * block, (index + 1) * block)
        copies[2 + 2 * index].wait()
        copies[3 + 2 * index].wait()
        for head in range(heads):
            columns = slice(head * width, (head + 1) * width)
            local = targets_ref[head : head + 1, rows] - place[0] * value_count
            hit = (local >= 0) & (local < value_count)
            compatible = compat[head, 0, index] == 1
            live = compatible | (jnp.max(jnp.where(hit, 1.0, 0.0)) > 0.0)

            @pl.when(live)
            def _():
                lse_rows = jnp.where(hit | compatible, lse_ref[head : head + 1, rows], MASKED) * LOG2E
                scores = dot(k_ref[:, columns], q_ref[rows, columns], NT)
                dprobs = dot(v_ref[:, columns], g_ref[rows, columns], NT)
                probs = jnp.exp2(scores * (scale * LOG2E) - lse_rows)
                delta_ref[head : head + 1, rows] = jnp.sum(probs * dprobs, axis=0, keepdims=True)
                terms = probs * (dprobs + 1.0)
                slots = lax.broadcasted_iota(jnp.int32, terms.shape, 0)
                probs_ref[head, :, rows] = probs
                score_ref[head, :, rows] = jnp.where(slots == local, terms - 1.0, terms)

            @pl.when(jnp.logical_not(live))
            def _():
                delta_ref[head : head + 1, rows] = jnp.zeros((1, block), jnp.float32)
                probs_ref[head, :, rows] = jnp.zeros((value_count, block), jnp.float32)
                score_ref[head, :, rows] = jnp.zeros((value_count, block), jnp.float32)


def value_kernel(place, probs_ref, g_ref, own_ref, send_ref):
    heads, _, _ = probs_ref.shape
    width = g_ref.shape[1] // heads
    share = own_ref.shape[0]
    parts = send_ref.shape[0] + 1
    for step in range(parts):
        rows = ways(lax.rem(place[1] + step, parts) * share, share)
        for head in range(heads):
            columns = slice(head * width, (head + 1) * width)
            term = dot(probs_ref[head, rows, :].astype(jnp.bfloat16), g_ref[:, columns], NN)
            if step == 0:
                own_ref[:, columns] = term
            else:
                send_ref[step - 1, :, columns] = term.astype(jnp.bfloat16)


def low_scores(delta_ref, probs_ref, score_ref, head, rows):
    gap = probs_ref[head, :, rows] * delta_ref[pl.ds(head, 1), rows]
    return (score_ref[head, :, rows] - gap).astype(jnp.bfloat16)


def other_kernel(
    place, delta_ref, probs_ref, score_ref, k_ref, low_ref, query_ref, *, chunk, scale
):
    head = 1 - place[2]
    width = query_ref.shape[1]
    keys = k_ref[:, ways(head * width, width)]
    for start in range(0, query_ref.shape[0], chunk):
        rows = slice(start, start + chunk)
        low = low_scores(delta_ref, probs_ref, score_ref, head, rows)
        low_ref[:, rows] = low
        query_ref[rows, :] = (scale * dot(low, keys, TN)).astype(jnp.bfloat16)


def key_kernel(
    place, delta_ref, probs_ref, score_ref, other_ref, q_ref, low_ref, own_ref, send_ref,
    *, chunk, scale,
):
    head = place[2]
    width = own_ref.shape[1] // 2
    share = own_ref.shape[0]
    parts = send_ref.shape[0] + 1
    for start in range(0, q_ref.shape[0], chunk):
        rows = slice(start, start + chunk)
        low_ref[:, rows] = low_scores(delta_ref, probs_ref, score_ref, head, rows)
    for step in range(parts - 1, -1, -1):
        rows = ways(lax.rem(place[1] + step, parts) * share, share)
        for source, index in ((other_ref, 1 - head), (low_ref, head)):
            columns = ways(index * width, width)
            term = scale * dot(source[rows, :], q_ref[:, columns], NN)
            if step == 0:
                own_ref[:, columns] = term
            else:
                send_ref[step - 1, :, columns] = term.astype(jnp.bfloat16)


def query_kernel(place, low_ref, k_ref, received_ref, keep_ref, send_ref, *, scale):
    chains, rows, width = keep_ref.shape
    keys = k_ref[:, ways(place[2] * width, width)]
    for target, other in ((send_ref, 1), (keep_ref, 0)):
        for chain in range(chains):
            start = (2 * chain + (place[3 + chain] ^ other)) * rows
            columns = ways(start, rows)
            term = scale * dot(low_ref[:, columns], keys, TN)
            total = term + received_ref[columns, :].astype(jnp.float32)
            target[chain] = total.astype(target.dtype)


def assemble_kernel(place, mine_ref, theirs_ref, out_ref, sems):
    chains, pieces, piece, width = mine_ref.shape
    copies = []
    for side, ref in enumerate((mine_ref, theirs_ref)):
        columns = ways((place[0] ^ side) * width, width)
        for chain in range(chains):
            for index in range(pieces):
                rows = ways((chain * pieces + (index ^ place[1 + chain])) * piece, piece)
                copies.append(
                    pltpu.make_async_copy(
                        ref.at[chain, index], out_ref.at[rows, columns], sems.at[len(copies)]
                    )
                )
                copies[-1].start()
    for copy in copies:
        copy.wait()


def call(kernel, name, inputs, in_specs, outputs, flops, scratch=(), out_specs=None):
    return pl.pallas_call(
        kernel,
        in_specs=in_specs,
        out_specs=[IN_VMEM] * len(outputs) if out_specs is None else out_specs,
        out_shape=outputs,
        scratch_shapes=list(scratch),
        cost_estimate=pl.CostEstimate(flops=flops, bytes_accessed=flops // 1000, transcendentals=0),
        compiler_params=PARAMS,
        name=name,
    )(*inputs)


def on_device(queries, pool_keys, pool_values, out_grad, lse, compat, targets):
    heads, value_blocks, blocks = compat.shape
    query_count, wide = queries.shape
    value_count = pool_keys.shape[0]
    width = wide // heads
    scale = width ** -0.5
    value_devices, parts = lax.axis_size("val"), lax.axis_size("qry")
    bits = value_devices.bit_length() - 1
    assert heads == 2 and value_blocks == 1 and value_devices == 1 << bits and bits >= 3
    val, qry = lax.axis_index("val"), lax.axis_index("qry")
    core = lax.rem(val, 2)
    share = value_count // parts
    f32, bf16 = jnp.float32, jnp.bfloat16

    def flip(array, mask):
        return lax.ppermute(array, "val", [(i, i ^ mask) for i in range(value_devices)])

    def swap_shares(send):
        return [
            lax.ppermute(send[step - 1], "qry", [(i, (i + step) % parts) for i in range(parts)])
            for step in range(1, parts)
        ]

    def add(own, received):
        for array in received:
            own = own + array.astype(f32)
        return own

    def bit_of(bit):
        return lax.rem(val // (1 << bit), 2)

    chains = 2 if query_count % (2 * value_devices // 2 * 16) == 0 else 1
    orders = [[1, 2], [2, 1]][:chains]
    orders = [order + list(range(3, bits)) for order in orders]
    place = jnp.stack([val, qry, core] + [bit_of(order[0]) for order in orders]).astype(jnp.int32)
    work = 2 * query_count * value_count * width

    delta, probs, terms, q_near, g_near, k_near = call(
        partial(forward_kernel, heads=heads, blocks=blocks, scale=scale),
        "forward_pass",
        (place,)
        + tuple(
            pltpu.with_memory_space_constraint(array, pltpu.HBM)
            for array in (
                compat, queries, out_grad, pool_keys, pool_values, lse, jnp.transpose(targets)
            )
        ),
        [IN_SMEM, IN_SMEM] + [IN_HBM] * 4 + [IN_VMEM] * 2,
        [
            pltpu.VMEM((heads, query_count), f32),
            pltpu.VMEM((heads, value_count, query_count), f32),
            pltpu.VMEM((heads, value_count, query_count), f32),
            pltpu.VMEM(queries.shape, bf16),
            pltpu.VMEM(queries.shape, bf16),
            pltpu.VMEM(pool_keys.shape, bf16),
        ],
        4 * work,
        [
            pltpu.VMEM(pool_values.shape, bf16),
            pltpu.SemaphoreType.DMA((2 + 2 * blocks,)),
        ],
    )
    shares = [
        pltpu.VMEM((share, wide), f32),
        pltpu.VMEM((parts - 1, share, wide), bf16),
    ]
    value_own, value_send = call(
        value_kernel, "value_terms", (place, probs, g_near), [IN_SMEM] + [IN_VMEM] * 2, shares, 2 * work
    )
    value_received = swap_shares(value_send)
    stride = 1
    while stride < value_devices:
        steps = min(4, value_devices // stride)
        delta = add(delta, [flip(delta, stride * step) for step in range(1, steps)])
        stride *= steps

    chunk = query_count // 3 if query_count % 384 == 0 else query_count
    low = pltpu.VMEM((value_count, query_count), bf16)
    low_other, query_send = call(
        partial(other_kernel, chunk=chunk, scale=scale),
        "other_head",
        (place, delta, probs, terms, k_near),
        [IN_SMEM] + [IN_VMEM] * 4,
        [low, pltpu.VMEM((query_count, width), bf16)],
        work,
    )
    query_received = flip(query_send, 1)
    low_mine, key_own, key_send = call(
        partial(key_kernel, chunk=chunk, scale=scale),
        "key_terms",
        (place, delta, probs, terms, low_other, q_near),
        [IN_SMEM] + [IN_VMEM] * 5,
        [low] + shares,
        2 * work,
    )
    key_received = swap_shares(key_send)
    half = query_count // (2 * chains)
    keep, send = call(
        partial(query_kernel, scale=scale),
        "own_head",
        (place, low_mine, k_near, query_received),
        [IN_SMEM] + [IN_VMEM] * 3,
        [pltpu.VMEM((chains, half, width), f32), pltpu.VMEM((chains, half, width), bf16)],
        work,
    )

    kept = [keep[chain] for chain in range(chains)]
    sent = [send[chain] for chain in range(chains)]
    own_piece = []
    for stage in range(bits - 1):
        received = [flip(sent[chain], 1 << orders[chain][stage]) for chain in range(chains)]
        for chain in range(chains):
            total = add(kept[chain], [received[chain]])
            if stage == bits - 2:
                kept[chain] = total.astype(bf16)
            else:
                bit = bit_of(orders[chain][stage + 1])
                split = total.reshape(2, total.shape[0] // 2, width)
                sent[chain] = lax.dynamic_index_in_dim(split, 1 - bit, 0, keepdims=False).astype(bf16)
                kept[chain] = lax.dynamic_index_in_dim(split, bit, 0, keepdims=False)
    for chain in range(chains):
        index = 0
        for bit in orders[chain]:
            index = 2 * index + bit_of(bit)
        own_piece.append(index)
    for stage in range(bits - 2, -1, -1):
        received = [flip(kept[chain], 1 << orders[chain][stage]) for chain in range(chains)]
        kept = [jnp.concatenate([kept[chain], received[chain]], axis=0) for chain in range(chains)]
    pieces = value_devices // 2
    mine = jnp.stack(kept).reshape(chains, pieces, query_count // (chains * pieces), width)
    theirs = flip(mine, 1)
    (query_grad,) = call(
        assemble_kernel,
        "assemble",
        (
            jnp.stack([core] + own_piece).astype(jnp.int32),
            pltpu.with_memory_space_constraint(mine, pltpu.VMEM),
            pltpu.with_memory_space_constraint(theirs, pltpu.VMEM),
        ),
        [IN_SMEM] + [IN_VMEM] * 2,
        [jax.ShapeDtypeStruct((query_count, wide), bf16)],
        1000 * query_count * wide,
        [pltpu.SemaphoreType.DMA((2 * chains * pieces,))],
        [IN_HBM],
    )
    value_grad = add(value_own, value_received).astype(bf16)
    key_grad = add(key_own, key_received).astype(bf16)
    return query_grad, key_grad, value_grad


def solution(mesh):
    placed = (
        P("qry", None),
        P("val", None),
        P("val", None),
        P("qry", None),
        P(None, "qry"),
        P(None, "val", "qry"),
        P("qry", None),
    )
    return jax.shard_map(
        on_device,
        mesh=mesh,
        in_specs=placed,
        out_specs=(P("qry", None), P(("val", "qry"), None), P(("val", "qry"), None)),
        check_vma=False,
    )
```

```python
import math
from functools import partial

import jax
import jax.numpy as jnp
from jax import lax
from jax.experimental import pallas as pl
from jax.experimental.pallas import tpu as pltpu
from jax.sharding import PartitionSpec as P

LOG2E = math.log2(math.e)
MASKED = 1e30
NT = (((1,), (1,)), ((), ()))
NN = (((1,), (0,)), ((), ()))
TN = (((0,), (0,)), ((), ()))
PARAMS = pltpu.CompilerParams(vmem_limit_bytes=24 * 1024 * 1024)
IN_VMEM = pl.BlockSpec(memory_space=pltpu.VMEM)
IN_SMEM = pl.BlockSpec(memory_space=pltpu.SMEM)
IN_HBM = pl.BlockSpec(memory_space=pl.ANY)


def dot(a, b, dims):
    return lax.dot_general(a, b, dims, preferred_element_type=jnp.float32)


def ways(start, size):
    return pl.ds(pl.multiple_of(start, size), size)


def forward_kernel(
    place, compat, q_hbm, g_hbm, k_hbm, v_hbm, lse_ref, targets_ref,
    delta_ref, probs_ref, dprobs_ref, q_ref, g_ref, k_ref, v_ref, sems, *, heads, blocks, scale,
):
    value_count, width = k_ref.shape[0], k_ref.shape[1] // heads
    block = q_ref.shape[0] // blocks
    copies = [
        pltpu.make_async_copy(k_hbm, k_ref, sems.at[0]),
        pltpu.make_async_copy(v_hbm, v_ref, sems.at[1]),
    ]
    for index in range(blocks):
        rows = pl.ds(index * block, block)
        for half, (source, target) in enumerate(((q_hbm, q_ref), (g_hbm, g_ref))):
            copies.append(
                pltpu.make_async_copy(source.at[rows], target.at[rows], sems.at[2 + 2 * index + half])
            )
    for copy in copies:
        copy.start()
    copies[0].wait()
    copies[1].wait()
    for index in range(blocks):
        rows = slice(index * block, (index + 1) * block)
        copies[2 + 2 * index].wait()
        copies[3 + 2 * index].wait()
        for head in range(heads):
            columns = slice(head * width, (head + 1) * width)
            local = targets_ref[head : head + 1, rows] - place[0] * value_count
            hit = (local >= 0) & (local < value_count)
            compatible = compat[head, 0, index] == 1
            live = compatible | (jnp.max(jnp.where(hit, 1.0, 0.0)) > 0.0)

            @pl.when(live)
            def _():
                lse_rows = jnp.where(hit | compatible, lse_ref[head : head + 1, rows], MASKED) * LOG2E
                scores = dot(k_ref[:, columns], q_ref[rows, columns], NT)
                dprobs = dot(v_ref[:, columns], g_ref[rows, columns], NT)
                probs = jnp.exp2(scores * (scale * LOG2E) - lse_rows)
                delta_ref[head : head + 1, rows] = jnp.sum(probs * dprobs, axis=0, keepdims=True)
                probs_ref[head, :, rows] = probs
                dprobs_ref[head, :, rows] = dprobs

            @pl.when(jnp.logical_not(live))
            def _():
                delta_ref[head : head + 1, rows] = jnp.zeros((1, block), jnp.float32)
                probs_ref[head, :, rows] = jnp.zeros((value_count, block), jnp.float32)
                dprobs_ref[head, :, rows] = jnp.zeros((value_count, block), jnp.float32)


def value_kernel(place, probs_ref, g_ref, own_ref, send_ref):
    heads, _, _ = probs_ref.shape
    width = g_ref.shape[1] // heads
    share = own_ref.shape[0]
    parts = send_ref.shape[0] + 1
    for step in range(parts):
        rows = ways(lax.rem(place[1] + step, parts) * share, share)
        for head in range(heads):
            columns = slice(head * width, (head + 1) * width)
            term = dot(probs_ref[head, rows, :].astype(jnp.bfloat16), g_ref[:, columns], NN)
            if step == 0:
                own_ref[:, columns] = term
            else:
                send_ref[step - 1, :, columns] = term.astype(jnp.bfloat16)


def onehot_less(terms, place, targets_ref, head, rows):
    local = targets_ref[pl.ds(head, 1), rows] - place[0] * terms.shape[0]
    slots = lax.broadcasted_iota(jnp.int32, terms.shape, 0)
    return jnp.where(slots == local, terms - 1.0, terms)


def pair_dot(terms, keys):
    high = terms.astype(jnp.bfloat16)
    rest = (terms - high.astype(jnp.float32)).astype(jnp.bfloat16)
    return jnp.transpose(dot(keys, high, TN) + dot(keys, rest, TN))


def query_kernel(place, probs_ref, dprobs_ref, targets_ref, k_ref, out_ref, *, own, chunk):
    head = place[2] if own else 1 - place[2]
    width = out_ref.shape[2]
    keys = k_ref[:, ways(head * width, width)]
    for start in range(0, out_ref.shape[1], chunk):
        rows = slice(start, start + chunk)
        probs = probs_ref[head, :, rows]
        terms = onehot_less(
            probs * (dprobs_ref[head, :, rows] + 1.0), place, targets_ref, head, rows
        )
        out_ref[0, rows, :] = pair_dot(terms, keys)
        out_ref[1, rows, :] = pair_dot(probs, keys)


def delta_kernel(own_ref, received_ref, terms_ref, out_ref, same_terms_ref):
    out_ref[...] = own_ref[...] + received_ref[...]


def combine_kernel(
    place, delta_ref, gone_ref, own_ref, received_ref, keep_ref, sum_ref, *send_refs, scale
):
    chains, rows, width = keep_ref.shape
    sum_ref[...] = delta_ref[...] + gone_ref[...]
    for other in (1, 0):
        for chain in range(chains):
            target = send_refs[chain] if other else keep_ref.at[chain]
            span = ways((2 * chain + (place[3 + chain] ^ other)) * rows, rows)
            delta = sum_ref[pl.ds(place[2], 1), span] * scale
            delta = jnp.transpose(jnp.broadcast_to(delta, (128, rows)))
            for start in range(0, width, 128):
                columns = slice(start, start + 128)
                direct = own_ref[0, span, columns] + received_ref[0, span, columns]
                weighted = own_ref[1, span, columns] + received_ref[1, span, columns]
                total = scale * direct - delta * weighted
                target[:, columns] = total.astype(target.dtype)


def key_kernel(
    place, delta_ref, probs_ref, dprobs_ref, targets_ref, q_ref, values_ref, own_ref, send_ref,
    low_ref, *, chunk, scale,
):
    heads = probs_ref.shape[0]
    width = own_ref.shape[1] // heads
    share = own_ref.shape[0]
    parts = send_ref.shape[0] + 1
    send_ref[:, :, heads * width :] = values_ref[...]
    for head in range(heads):
        columns = slice(head * width, (head + 1) * width)
        for start in range(0, q_ref.shape[0], chunk):
            rows = slice(start, start + chunk)
            gap = dprobs_ref[head, :, rows] - (delta_ref[head : head + 1, rows] - 1.0)
            terms = onehot_less(probs_ref[head, :, rows] * gap, place, targets_ref, head, rows)
            low_ref[head, :, rows] = terms.astype(jnp.bfloat16)
        for step in range(parts):
            rows = ways(lax.rem(place[1] + step, parts) * share, share)
            term = scale * dot(low_ref[head, rows, :], q_ref[:, columns], NN)
            if step == 0:
                own_ref[:, columns] = term
            else:
                send_ref[step - 1, :, columns] = term.astype(jnp.bfloat16)


def place_pieces(place, source, out_ref, sems, side):
    chains = len(source)
    pieces, piece, width = source[0].shape
    columns = ways((place[0] ^ side) * width, width)
    copies = []
    for chain in range(chains):
        for index in range(pieces):
            rows = ways((chain * pieces + (index ^ place[1 + chain])) * piece, piece)
            copies.append(
                pltpu.make_async_copy(
                    source[chain].at[index], out_ref.at[rows, columns], sems.at[len(copies)]
                )
            )
            copies[-1].start()
    return copies


def split_kernel(place, keep_ref, *rest):
    chains = keep_ref.shape[0]
    came_refs, kept_ref, sent_refs = rest[:chains], rest[chains + 1], rest[chains + 2 :]
    rows = kept_ref.shape[1]
    for chain in range(chains):
        for other in (1, 0):
            target = sent_refs[chain] if other else kept_ref.at[chain]
            span = ways((place[3 + chains + chain] ^ other) * rows, rows)
            total = keep_ref[chain, span, :] + came_refs[chain][span, :].astype(jnp.float32)
            target[...] = total.astype(target.dtype)


def middle_kernel(
    total_ref, came_ref, key_ref, value_ref, received_ref, key_out, value_out, *out_refs
):
    rows = total_ref.shape[1]
    for chain, out_ref in enumerate(out_refs):
        out_ref[:rows] = total_ref[chain]
        out_ref[rows:] = came_ref[chain]
    wide = key_ref.shape[1]
    key_sum, value_sum = key_ref[...], value_ref[...]
    for step in range(received_ref.shape[0]):
        key_sum += received_ref[step, :, :wide].astype(jnp.float32)
        value_sum += received_ref[step, :, wide:].astype(jnp.float32)
    key_out[...] = key_sum.astype(jnp.bfloat16)
    value_out[...] = value_sum.astype(jnp.bfloat16)


def own_columns_kernel(place, *rest):
    *mine, out_ref, sems = rest
    for copy in place_pieces(place, mine, out_ref, sems, 0):
        copy.wait()


def other_columns_kernel(place, begun_ref, *rest):
    *theirs, out_ref, sems = rest
    for copy in place_pieces(place, theirs, out_ref, sems, 1):
        copy.wait()


def call(kernel, name, inputs, in_specs, outputs, flops, scratch=(), out_specs=None, aliases={}):
    return pl.pallas_call(
        kernel,
        in_specs=in_specs,
        out_specs=[IN_VMEM] * len(outputs) if out_specs is None else out_specs,
        out_shape=outputs,
        scratch_shapes=list(scratch),
        input_output_aliases=aliases,
        cost_estimate=pl.CostEstimate(flops=flops, bytes_accessed=flops // 1000, transcendentals=0),
        compiler_params=PARAMS,
        name=name,
    )(*inputs)


def on_device(queries, pool_keys, pool_values, out_grad, lse, compat, targets):
    heads, value_blocks, blocks = compat.shape
    query_count, wide = queries.shape
    value_count = pool_keys.shape[0]
    width = wide // heads
    scale = width ** -0.5
    value_devices, parts = lax.axis_size("val"), lax.axis_size("qry")
    bits = value_devices.bit_length() - 1
    assert heads == 2 and value_blocks == 1 and value_devices == 1 << bits and bits >= 4
    val, qry = lax.axis_index("val"), lax.axis_index("qry")
    core = lax.rem(val, 2)
    share = value_count // parts
    f32, bf16 = jnp.float32, jnp.bfloat16

    def flip(array, mask):
        return lax.ppermute(array, "val", [(i, i ^ mask) for i in range(value_devices)])

    def swap_shares(send):
        return jnp.stack([
            lax.ppermute(send[step - 1], "qry", [(i, (i + step) % parts) for i in range(parts)])
            for step in range(1, parts)
        ])

    def add(own, received):
        for array in received:
            own = own + array.astype(f32)
        return own

    def bit_of(bit):
        return lax.rem(val // (1 << bit), 2)

    chains = 2 if query_count % (2 * value_devices // 2 * 16) == 0 else 1
    orders = [[1, 2], [2, 1]][:chains]
    orders = [order + list(range(3, bits)) for order in orders]
    place = jnp.stack([val, qry, core] + [bit_of(order[stage]) for stage in range(2) for order in orders]).astype(jnp.int32)
    work = 2 * query_count * value_count * width

    delta, probs, dprobs, q_near, g_near, k_near = call(
        partial(forward_kernel, heads=heads, blocks=blocks, scale=scale),
        "forward_pass",
        (place,)
        + tuple(
            pltpu.with_memory_space_constraint(array, pltpu.HBM)
            for array in (
                compat, queries, out_grad, pool_keys, pool_values, lse, jnp.transpose(targets)
            )
        ),
        [IN_SMEM, IN_SMEM] + [IN_HBM] * 4 + [IN_VMEM] * 2,
        [
            pltpu.VMEM((heads, query_count), f32),
            pltpu.VMEM((heads, value_count, query_count), f32),
            pltpu.VMEM((heads, value_count, query_count), f32),
            pltpu.VMEM(queries.shape, bf16),
            pltpu.VMEM(queries.shape, bf16),
            pltpu.VMEM(pool_keys.shape, bf16),
        ],
        4 * work,
        [
            pltpu.VMEM(pool_values.shape, bf16),
            pltpu.SemaphoreType.DMA((2 + 2 * blocks,)),
        ],
    )
    shares = [
        pltpu.VMEM((share, wide), f32),
        pltpu.VMEM((parts - 1, share, wide), bf16),
    ]
    value_own, value_send = call(
        value_kernel, "value_terms", (place, probs, g_near), [IN_SMEM] + [IN_VMEM] * 2, shares, 2 * work
    )
    chunk = query_count // 3 if query_count % 384 == 0 else query_count
    rows_of = pltpu.VMEM((2, query_count, width), f32)
    targets = jnp.transpose(targets)

    def query_terms(own, name):
        return call(
            partial(query_kernel, own=own, chunk=chunk),
            name,
            (place, probs, dprobs, targets, k_near),
            [IN_SMEM] + [IN_VMEM] * 4,
            [rows_of],
            4 * work,
        )[0]

    other = query_terms(False, "other_head")
    mine = query_terms(True, "own_head")
    received = None
    for bit in range(bits):
        came = flip(delta, 1 << bit)
        if bit < bits - 1:
            carried = {0: other, bits - 2: mine}.get(bit)
            if carried is None:
                delta = delta + came
                continue
            delta, carried = call(
                delta_kernel,
                "delta_sum",
                (delta, came, carried),
                [IN_VMEM] * 2 + [IN_HBM],
                [pltpu.VMEM((heads, query_count), f32), rows_of],
                heads * query_count,
                out_specs=[IN_VMEM, IN_HBM],
                aliases={2: 1},
            )
            if bit == 0:
                received = flip(carried, 1)
            else:
                mine = carried
    half = query_count // (2 * chains)
    keep, delta, *send = call(
        partial(combine_kernel, scale=scale),
        "combine",
        (place, delta, came, mine, received),
        [IN_SMEM] + [IN_VMEM] * 4,
        [
            pltpu.VMEM((chains, half, width), f32),
            pltpu.VMEM((heads, query_count), f32),
        ]
        + [pltpu.VMEM((half, width), bf16)] * chains,
        work // 4,
    )
    key_own, pool_send = call(
        partial(key_kernel, chunk=chunk, scale=scale),
        "key_terms",
        (place, delta, probs, dprobs, targets, q_near, value_send),
        [IN_SMEM] + [IN_VMEM] * 6,
        [shares[0], pltpu.VMEM((parts - 1, share, 2 * wide), bf16)],
        2 * work,
        [pltpu.VMEM((heads, value_count, query_count), bf16)],
    )
    pool_received = swap_shares(pool_send)

    came = [flip(send[chain], 1 << order[0]) for chain, order in enumerate(orders)]
    kept, *sent = call(
        split_kernel,
        "split",
        (place, keep, *came, pool_send),
        [IN_SMEM] + [IN_VMEM] * (1 + chains) + [IN_HBM],
        [pltpu.VMEM((chains, half // 2, width), f32)]
        + [pltpu.VMEM((half // 2, width), bf16)] * chains,
        work // 8,
    )
    total = jnp.stack(
        [
            kept[chain] + flip(sent[chain], 1 << order[1]).astype(f32)
            for chain, order in enumerate(orders)
        ]
    )
    for bit in range(3, bits):
        split = total.reshape(chains, 2, -1, width)
        pick = partial(lax.dynamic_index_in_dim, split, axis=1, keepdims=False)
        came = flip(pick(1 - bit_of(bit)).astype(bf16), 1 << bit)
        total = pick(bit_of(bit)) + came.astype(f32)
    total = total.astype(bf16)
    for bit in range(bits - 1, 3, -1):
        total = jnp.concatenate([total, flip(total, 1 << bit)], axis=1)
    key_grad, value_grad, *parts_of = call(
        middle_kernel,
        "middle",
        (total, flip(total, 8), key_own, value_own, pool_received),
        [IN_VMEM] * 5,
        [
            jax.ShapeDtypeStruct((share, wide), bf16),
            jax.ShapeDtypeStruct((share, wide), bf16),
        ]
        + [pltpu.VMEM((half // 2, width), bf16)] * chains,
        work // 8,
    )
    gathered = []
    own_piece = []
    for chain, order in enumerate(orders):
        part = parts_of[chain]
        for bit in order[1::-1]:
            part = jnp.concatenate([part, flip(part, 1 << bit)], axis=0)
        gathered.append(part)
        index = 0
        for bit in order:
            index = 2 * index + bit_of(bit)
        own_piece.append(index)
    pieces = value_devices // 2
    near = partial(pltpu.with_memory_space_constraint, memory_space=pltpu.VMEM)
    gathered = [near(part.reshape(pieces, -1, width)) for part in gathered]
    theirs = [near(flip(part, 1)) for part in gathered]
    order_place = jnp.stack([core] + own_piece).astype(jnp.int32)
    query_shape = jax.ShapeDtypeStruct((query_count, wide), bf16)
    sems = [pltpu.SemaphoreType.DMA((chains * pieces,))]
    (begun,) = call(
        own_columns_kernel,
        "own_columns",
        (order_place, *gathered),
        [IN_SMEM] + [IN_VMEM] * chains,
        [query_shape],
        work // 4,
        sems,
        [IN_HBM],
    )
    (query_grad,) = call(
        other_columns_kernel,
        "other_columns",
        (order_place, begun, *theirs),
        [IN_SMEM, IN_HBM] + [IN_VMEM] * chains,
        [query_shape],
        work // 4,
        sems,
        [IN_HBM],
        {1: 0},
    )
    return query_grad, key_grad, value_grad


def solution(mesh):
    placed = (
        P("qry", None),
        P("val", None),
        P("val", None),
        P("qry", None),
        P(None, "qry"),
        P(None, "val", "qry"),
        P("qry", None),
    )
    return jax.shard_map(
        on_device,
        mesh=mesh,
        in_specs=placed,
        out_specs=(P("qry", None), P(("val", "qry"), None), P(("val", "qry"), None)),
        check_vma=False,
    )
```

```python
import math
from functools import partial

import jax
import jax.numpy as jnp
from jax import lax
from jax.experimental import pallas as pl
from jax.experimental.pallas import tpu as pltpu
from jax.sharding import PartitionSpec as P

LOG2E = math.log2(math.e)
MASKED = 1e30
NT = (((1,), (1,)), ((), ()))
NN = (((1,), (0,)), ((), ()))
PARAMS = pltpu.CompilerParams(vmem_limit_bytes=24 * 1024 * 1024)
IN_VMEM = pl.BlockSpec(memory_space=pltpu.VMEM)
IN_SMEM = pl.BlockSpec(memory_space=pltpu.SMEM)
IN_HBM = pl.BlockSpec(memory_space=pl.ANY)


def dot(a, b, dims):
    return lax.dot_general(a, b, dims, preferred_element_type=jnp.float32)


def ways(start, size):
    return pl.ds(pl.multiple_of(start, size), size)


def forward_kernel(
    place, compat, q_hbm, g_hbm, k_hbm, v_hbm, lse_ref, targets_ref,
    delta_ref, probs_ref, dprobs_ref, q_ref, g_ref, k_ref, v_ref, sems, *, heads, blocks, scale,
):
    value_count, width = k_ref.shape[0], k_ref.shape[1] // heads
    block = q_ref.shape[0] // blocks
    copies = [
        pltpu.make_async_copy(k_hbm, k_ref, sems.at[0]),
        pltpu.make_async_copy(v_hbm, v_ref, sems.at[1]),
    ]
    for index in range(blocks):
        rows = pl.ds(index * block, block)
        for half, (source, target) in enumerate(((q_hbm, q_ref), (g_hbm, g_ref))):
            copies.append(
                pltpu.make_async_copy(source.at[rows], target.at[rows], sems.at[2 + 2 * index + half])
            )
    for copy in copies:
        copy.start()
    copies[0].wait()
    copies[1].wait()
    for index in range(blocks):
        rows = slice(index * block, (index + 1) * block)
        copies[2 + 2 * index].wait()
        copies[3 + 2 * index].wait()
        hits = []
        live = False
        for head in range(heads):
            local = targets_ref[head : head + 1, rows] - place[0] * value_count
            hit = (local >= 0) & (local < value_count)
            compatible = compat[head, 0, index] == 1
            hits.append(hit | compatible)
            live = live | compatible | (jnp.max(jnp.where(hit, 1.0, 0.0)) > 0.0)

        @pl.when(live)
        def _():
            for head in range(heads):
                columns = slice(head * width, (head + 1) * width)
                lse_rows = jnp.where(hits[head], lse_ref[head : head + 1, rows], MASKED) * LOG2E
                scores = dot(k_ref[:, columns], q_ref[rows, columns], NT)
                dprobs = dot(v_ref[:, columns], g_ref[rows, columns], NT)
                probs = jnp.exp2(scores * (scale * LOG2E) - lse_rows)
                delta_ref[head : head + 1, rows] = jnp.sum(probs * dprobs, axis=0, keepdims=True)
                probs_ref[head, :, rows] = probs
                dprobs_ref[head, :, rows] = dprobs

        @pl.when(jnp.logical_not(live))
        def _():
            for head in range(heads):
                delta_ref[head : head + 1, rows] = jnp.zeros((1, block), jnp.float32)
                probs_ref[head, :, rows] = jnp.zeros((value_count, block), jnp.float32)
                dprobs_ref[head, :, rows] = jnp.zeros((value_count, block), jnp.float32)


def value_kernel(place, probs_ref, g_ref, own_ref, send_ref):
    heads, _, _ = probs_ref.shape
    width = g_ref.shape[1] // heads
    share = own_ref.shape[0]
    parts = send_ref.shape[0] + 1
    for step in range(parts):
        rows = ways(lax.rem(place[1] + step, parts) * share, share)
        for head in range(heads):
            columns = slice(head * width, (head + 1) * width)
            term = dot(probs_ref[head, rows, :].astype(jnp.bfloat16), g_ref[:, columns], NN)
            if step == 0:
                own_ref[:, columns] = term
            else:
                send_ref[step - 1, :, columns] = term.astype(jnp.bfloat16)


def onehot_less(terms, place, targets_ref, head, rows):
    local = targets_ref[pl.ds(head, 1), rows] - place[0] * terms.shape[0]
    slots = lax.broadcasted_iota(jnp.int32, terms.shape, 0)
    return jnp.where(slots == local, terms - 1.0, terms)


def pair_dot(terms, keys):
    high = terms.astype(jnp.bfloat16)
    rest = (terms - high.astype(jnp.float32)).astype(jnp.bfloat16)
    return jnp.transpose(dot(keys, high, NN) + dot(keys, rest, NN))


def query_kernel(place, probs_ref, dprobs_ref, targets_ref, k_ref, out_ref, *, own, chunk):
    head = place[2] if own else 1 - place[2]
    width = out_ref.shape[2]
    keys = jnp.transpose(k_ref[:, ways(head * width, width)])
    for start in range(0, out_ref.shape[1], chunk):
        rows = slice(start, start + chunk)
        probs = probs_ref[head, :, rows]
        terms = onehot_less(
            probs * (dprobs_ref[head, :, rows] + 1.0), place, targets_ref, head, rows
        )
        out_ref[0, rows, :] = pair_dot(terms, keys)
        out_ref[1, rows, :] = pair_dot(probs, keys)


def delta_kernel(own_ref, received_ref, terms_ref, out_ref, same_terms_ref):
    out_ref[...] = own_ref[...] + received_ref[...]


def combine_kernel(
    place, delta_ref, gone_ref, own_ref, received_ref, keep_ref, sum_ref, send_ref, *, scale
):
    rows, width = keep_ref.shape
    sum_ref[...] = delta_ref[...] + gone_ref[...]
    for target, other in ((send_ref, 1), (keep_ref, 0)):
        span = ways((place[3] ^ other) * rows, rows)
        delta = sum_ref[pl.ds(place[2], 1), span] * scale
        delta = jnp.transpose(jnp.broadcast_to(delta, (128, rows)))
        for start in range(0, width, 128):
            columns = slice(start, start + 128)
            direct = own_ref[0, span, columns] + received_ref[0, span, columns]
            weighted = own_ref[1, span, columns] + received_ref[1, span, columns]
            target[:, columns] = (scale * direct - delta * weighted).astype(target.dtype)


def key_kernel(
    place, delta_ref, probs_ref, dprobs_ref, targets_ref, q_ref, values_ref, own_ref, send_ref,
    low_ref, *, chunk, scale,
):
    heads = probs_ref.shape[0]
    width = own_ref.shape[1] // heads
    share = own_ref.shape[0]
    parts = send_ref.shape[0] + 1
    send_ref[:, :, heads * width :] = values_ref[...]
    for head in range(heads):
        columns = slice(head * width, (head + 1) * width)
        for start in range(0, q_ref.shape[0], chunk):
            rows = slice(start, start + chunk)
            gap = dprobs_ref[head, :, rows] - (delta_ref[head : head + 1, rows] - 1.0)
            terms = onehot_less(probs_ref[head, :, rows] * gap, place, targets_ref, head, rows)
            low_ref[head, :, rows] = terms.astype(jnp.bfloat16)
        for step in range(parts):
            rows = ways(lax.rem(place[1] + step, parts) * share, share)
            term = scale * dot(low_ref[head, rows, :], q_ref[:, columns], NN)
            if step == 0:
                own_ref[:, columns] = term
            else:
                send_ref[step - 1, :, columns] = term.astype(jnp.bfloat16)


def split_kernel(place, keep_ref, came_ref, after_ref, kept_ref, sent_ref):
    rows = kept_ref.shape[0]
    for target, other in ((sent_ref, 1), (kept_ref, 0)):
        span = ways((place[4] ^ other) * rows, rows)
        total = keep_ref[span, :] + came_ref[span, :].astype(jnp.float32)
        target[...] = total.astype(target.dtype)


def middle_kernel(
    total_ref, came_ref, key_ref, value_ref, received_ref, key_out, value_out, out_ref
):
    total = total_ref[...].astype(jnp.float32) + came_ref[...].astype(jnp.float32)
    out_ref[...] = total.astype(jnp.bfloat16)
    wide = key_ref.shape[1]
    key_sum, value_sum = key_ref[...], value_ref[...]
    for step in range(received_ref.shape[0]):
        key_sum += received_ref[step, :, :wide].astype(jnp.float32)
        value_sum += received_ref[step, :, wide:].astype(jnp.float32)
    key_out[...] = key_sum.astype(jnp.bfloat16)
    value_out[...] = value_sum.astype(jnp.bfloat16)


def place_kernel(place, *rest, sources, piece):
    out_ref, sems = rest[-2:]
    copies = []
    for ref, (side, first) in zip(rest, sources):
        width = ref.shape[1]
        columns = ways((place[0] ^ side) * width, width)
        for index in range(ref.shape[0] // piece):
            rows = ways(((first + index) ^ place[1 + side]) * piece, piece)
            copies.append(
                pltpu.make_async_copy(
                    ref.at[pl.ds(index * piece, piece)], out_ref.at[rows, columns], sems.at[len(copies)]
                )
            )
            copies[-1].start()
    for copy in copies:
        copy.wait()


def call(kernel, name, inputs, in_specs, outputs, flops, scratch=(), out_specs=None, aliases={}):
    return pl.pallas_call(
        kernel,
        in_specs=in_specs,
        out_specs=[IN_VMEM] * len(outputs) if out_specs is None else out_specs,
        out_shape=outputs,
        scratch_shapes=list(scratch),
        input_output_aliases=aliases,
        cost_estimate=pl.CostEstimate(flops=flops, bytes_accessed=flops // 1000, transcendentals=0),
        compiler_params=PARAMS,
        name=name,
    )(*inputs)


def on_device(queries, pool_keys, pool_values, out_grad, lse, compat, targets):
    heads, value_blocks, blocks = compat.shape
    query_count, wide = queries.shape
    value_count = pool_keys.shape[0]
    width = wide // heads
    scale = width ** -0.5
    value_devices, parts = lax.axis_size("val"), lax.axis_size("qry")
    bits = value_devices.bit_length() - 1
    assert heads == 2 and value_blocks == 1 and value_devices == 1 << bits and bits >= 4
    val, qry = lax.axis_index("val"), lax.axis_index("qry")
    core = lax.rem(val, 2)
    share = value_count // parts
    f32, bf16 = jnp.float32, jnp.bfloat16

    def flip(array, *masks):
        pairs = [(i, i ^ masks[i % len(masks)]) for i in range(value_devices)]
        return lax.ppermute(array, "val", pairs)

    def swap_shares(send):
        return jnp.stack([
            lax.ppermute(send[step - 1], "qry", [(i, (i + step) % parts) for i in range(parts)])
            for step in range(1, parts)
        ])

    def add(own, received):
        for array in received:
            own = own + array.astype(f32)
        return own

    def bit_of(bit):
        return lax.rem(val // (1 << bit), 2)

    orders = [[1, 2], [2, 1]]
    orders = [order + list(range(3, bits - 1)) for order in orders]
    last = 1 << (bits - 1)

    def own_bits(turn):
        first, second = orders[turn], orders[1 - turn]
        return [jnp.where(core == 0, bit_of(a), bit_of(b)) for a, b in zip(first, second)]

    stages = [(1 << a, 1 << b) for a, b in zip(*orders)]
    stage_bits = own_bits(0)
    place = jnp.stack([val, qry, core] + stage_bits[:2]).astype(jnp.int32)
    work = 2 * query_count * value_count * width

    delta, probs, dprobs, q_near, g_near, k_near = call(
        partial(forward_kernel, heads=heads, blocks=blocks, scale=scale),
        "forward_pass",
        (place,)
        + tuple(
            pltpu.with_memory_space_constraint(array, pltpu.HBM)
            for array in (
                compat, queries, out_grad, pool_keys, pool_values, lse, jnp.transpose(targets)
            )
        ),
        [IN_SMEM, IN_SMEM] + [IN_HBM] * 4 + [IN_VMEM] * 2,
        [
            pltpu.VMEM((heads, query_count), f32),
            pltpu.VMEM((heads, value_count, query_count), f32),
            pltpu.VMEM((heads, value_count, query_count), f32),
            pltpu.VMEM(queries.shape, bf16),
            pltpu.VMEM(queries.shape, bf16),
            pltpu.VMEM(pool_keys.shape, bf16),
        ],
        4 * work,
        [
            pltpu.VMEM(pool_values.shape, bf16),
            pltpu.SemaphoreType.DMA((2 + 2 * blocks,)),
        ],
    )
    shares = [
        pltpu.VMEM((share, wide), f32),
        pltpu.VMEM((parts - 1, share, wide), bf16),
    ]
    value_own, value_send = call(
        value_kernel, "value_terms", (place, probs, g_near), [IN_SMEM] + [IN_VMEM] * 2, shares, 2 * work
    )
    chunk = query_count // 3 if query_count % 384 == 0 else query_count
    rows_of = pltpu.VMEM((2, query_count, width), f32)
    targets = jnp.transpose(targets)

    def query_terms(own, name):
        return call(
            partial(query_kernel, own=own, chunk=chunk),
            name,
            (place, probs, dprobs, targets, k_near),
            [IN_SMEM] + [IN_VMEM] * 4,
            [rows_of],
            4 * work,
        )[0]

    other = query_terms(False, "other_head")
    mine = query_terms(True, "own_head")
    received = None
    for bit in range(bits):
        came = flip(delta, 1 << bit)
        if bit < bits - 1:
            carried = {1: other, bits - 2: mine}.get(bit)
            if carried is None:
                delta = delta + came
                continue
            delta, carried = call(
                delta_kernel,
                "delta_sum",
                (delta, came, carried),
                [IN_VMEM] * 2 + [IN_HBM],
                [pltpu.VMEM((heads, query_count), f32), rows_of],
                heads * query_count,
                out_specs=[IN_VMEM, IN_HBM],
                aliases={2: 1},
            )
            if bit == 1:
                received = flip(carried, 1)
            else:
                mine = carried
    half = query_count // 2
    keep, delta, send = call(
        partial(combine_kernel, scale=scale),
        "combine",
        (place, delta, came, mine, received),
        [IN_SMEM] + [IN_VMEM] * 4,
        [
            pltpu.VMEM((half, width), f32),
            pltpu.VMEM((heads, query_count), f32),
            pltpu.VMEM((half, width), bf16),
        ],
        work // 4,
    )
    key_own, pool_send = call(
        partial(key_kernel, chunk=chunk, scale=scale),
        "key_terms",
        (place, delta, probs, dprobs, targets, q_near, value_send),
        [IN_SMEM] + [IN_VMEM] * 6,
        [shares[0], pltpu.VMEM((parts - 1, share, 2 * wide), bf16)],
        2 * work,
        [pltpu.VMEM((heads, value_count, query_count), bf16)],
    )
    pool_received = swap_shares(pool_send)

    kept, sent = call(
        split_kernel,
        "split",
        (place, keep, flip(send, *stages[0]), pool_send),
        [IN_SMEM] + [IN_VMEM] * 2 + [IN_HBM],
        [pltpu.VMEM((half // 2, width), f32), pltpu.VMEM((half // 2, width), bf16)],
        work // 8,
    )
    total = kept + flip(sent, *stages[1]).astype(f32)
    for stage in range(2, bits - 2):
        split = total.reshape(2, -1, width)
        pick = partial(lax.dynamic_index_in_dim, split, axis=0, keepdims=False)
        came = flip(pick(1 - stage_bits[stage]).astype(bf16), *stages[stage])
        total = pick(stage_bits[stage]) + came.astype(f32)
    total = total.astype(bf16)
    piece = total.shape[0]
    key_grad, value_grad, total = call(
        middle_kernel,
        "middle",
        (total, flip(total, last), key_own, value_own, pool_received),
        [IN_VMEM] * 5,
        [
            jax.ShapeDtypeStruct((share, wide), bf16),
            jax.ShapeDtypeStruct((share, wide), bf16),
            pltpu.VMEM((piece, width), bf16),
        ],
        work // 8,
    )
    for masks in stages[:0:-1]:
        total = jnp.concatenate([total, flip(total, *masks)], axis=0)

    def index_of(bits_of):
        index = 0
        for bit in bits_of:
            index = 2 * index + bit
        return index

    pieces_place = jnp.stack([core, index_of(own_bits(0)), index_of(own_bits(1))]).astype(jnp.int32)
    near = partial(pltpu.with_memory_space_constraint, memory_space=pltpu.VMEM)
    pieces = half // piece
    rest = flip(total, *stages[0])
    begun = ()
    for name, parts_of in (
        ("own_columns", [(total, 0, 0), (rest, 0, pieces), (flip(total, 1), 1, 0)]),
        ("other_columns", [(flip(rest, 1), 1, pieces)]),
    ):
        begun = call(
            partial(place_kernel, sources=[source[1:] for source in parts_of], piece=piece),
            name,
            (pieces_place, *[near(source[0]) for source in parts_of], *begun),
            [IN_SMEM] + [IN_VMEM] * len(parts_of) + [IN_HBM] * len(begun),
            [jax.ShapeDtypeStruct((query_count, wide), bf16)],
            work // 4,
            [pltpu.SemaphoreType.DMA((len(parts_of) * pieces,))],
            [IN_HBM],
            {1 + len(parts_of): 0} if begun else {},
        )
    return begun[0], key_grad, value_grad


def solution(mesh):
    placed = (
        P("qry", None),
        P("val", None),
        P("val", None),
        P("qry", None),
        P(None, "qry"),
        P(None, "val", "qry"),
        P("qry", None),
    )
    return jax.shard_map(
        on_device,
        mesh=mesh,
        in_specs=placed,
        out_specs=(P("qry", None), P(("val", "qry"), None), P(("val", "qry"), None)),
        check_vma=False,
    )
```

```python
import math
from functools import partial

import jax
import jax.numpy as jnp
from jax import lax
from jax.experimental import pallas as pl
from jax.experimental.pallas import tpu as pltpu
from jax.sharding import PartitionSpec as P

LOG2E = math.log2(math.e)
MASKED = 1e30
NT = (((1,), (1,)), ((), ()))
NN = (((1,), (0,)), ((), ()))
PARAMS = pltpu.CompilerParams(vmem_limit_bytes=24 * 1024 * 1024)
IN_VMEM = pl.BlockSpec(memory_space=pltpu.VMEM)
IN_SMEM = pl.BlockSpec(memory_space=pltpu.SMEM)
IN_HBM = pl.BlockSpec(memory_space=pl.ANY)


def dot(a, b, dims):
    return lax.dot_general(a, b, dims, preferred_element_type=jnp.float32)


def ways(start, size):
    return pl.ds(pl.multiple_of(start, size), size)


def forward_kernel(
    place, compat, q_hbm, g_hbm, k_hbm, v_hbm, lse_ref, targets_ref,
    delta_ref, probs_ref, dprobs_ref, q_ref, g_ref, k_ref, v_ref, sems, *, heads, blocks, scale,
):
    value_count, width = k_ref.shape[0], k_ref.shape[1] // heads
    block = q_ref.shape[0] // blocks
    copies = [
        pltpu.make_async_copy(k_hbm, k_ref, sems.at[0]),
        pltpu.make_async_copy(v_hbm, v_ref, sems.at[1]),
    ]
    for index in range(blocks):
        rows = pl.ds(index * block, block)
        for half, (source, target) in enumerate(((q_hbm, q_ref), (g_hbm, g_ref))):
            copies.append(
                pltpu.make_async_copy(source.at[rows], target.at[rows], sems.at[2 + 2 * index + half])
            )
    for copy in copies:
        copy.start()
    copies[0].wait()
    copies[1].wait()
    for index in range(blocks):
        rows = slice(index * block, (index + 1) * block)
        copies[2 + 2 * index].wait()
        copies[3 + 2 * index].wait()
        hits = []
        live = False
        for head in range(heads):
            local = targets_ref[head : head + 1, rows] - place[0] * value_count
            hit = (local >= 0) & (local < value_count)
            compatible = compat[head, 0, index] == 1
            hits.append(hit | compatible)
            live = live | compatible | (jnp.max(jnp.where(hit, 1.0, 0.0)) > 0.0)

        @pl.when(live)
        def _():
            for head in range(heads):
                columns = slice(head * width, (head + 1) * width)
                lse_rows = jnp.where(hits[head], lse_ref[head : head + 1, rows], MASKED) * LOG2E
                scores = dot(k_ref[:, columns], q_ref[rows, columns], NT)
                dprobs = dot(v_ref[:, columns], g_ref[rows, columns], NT)
                probs = jnp.exp2(scores * (scale * LOG2E) - lse_rows)
                delta_ref[head : head + 1, rows] = jnp.sum(probs * dprobs, axis=0, keepdims=True)
                probs_ref[head, :, rows] = probs
                dprobs_ref[head, :, rows] = dprobs

        @pl.when(jnp.logical_not(live))
        def _():
            for head in range(heads):
                delta_ref[head : head + 1, rows] = jnp.zeros((1, block), jnp.float32)
                probs_ref[head, :, rows] = jnp.zeros((value_count, block), jnp.float32)
                dprobs_ref[head, :, rows] = jnp.zeros((value_count, block), jnp.float32)


def value_kernel(place, probs_ref, g_ref, own_ref, send_ref):
    heads, _, _ = probs_ref.shape
    width = g_ref.shape[1] // heads
    share = own_ref.shape[0]
    parts = send_ref.shape[0] + 1
    for step in range(parts):
        rows = ways(lax.rem(place[1] + step, parts) * share, share)
        for head in range(heads):
            columns = slice(head * width, (head + 1) * width)
            term = dot(probs_ref[head, rows, :].astype(jnp.bfloat16), g_ref[:, columns], NN)
            if step == 0:
                own_ref[:, columns] = term
            else:
                send_ref[step - 1, :, columns] = term.astype(jnp.bfloat16)


def onehot_less(terms, place, targets_ref, head, rows):
    local = targets_ref[pl.ds(head, 1), rows] - place[0] * terms.shape[0]
    slots = lax.broadcasted_iota(jnp.int32, terms.shape, 0)
    return jnp.where(slots == local, terms - 1.0, terms)


def pair_dot(terms, keys):
    high = terms.astype(jnp.bfloat16)
    rest = (terms - high.astype(jnp.float32)).astype(jnp.bfloat16)
    return jnp.transpose(dot(keys, high, NN) + dot(keys, rest, NN))


def query_kernel(place, probs_ref, dprobs_ref, targets_ref, k_ref, out_ref, *, own, chunk):
    head = place[2] if own else 1 - place[2]
    width = out_ref.shape[2]
    keys = jnp.transpose(k_ref[:, ways(head * width, width)])
    for start in range(0, out_ref.shape[1], chunk):
        rows = slice(start, start + chunk)
        probs = probs_ref[head, :, rows]
        terms = onehot_less(
            probs * (dprobs_ref[head, :, rows] + 1.0), place, targets_ref, head, rows
        )
        out_ref[0, rows, :] = pair_dot(terms, keys)
        out_ref[1, rows, :] = pair_dot(probs, keys)


def delta_kernel(*refs):
    *added, terms_ref, out_ref, same_terms_ref = refs
    out_ref[...] = sum(ref[...] for ref in added)


def combine_kernel(place, own_ref, received_ref, *rest, deltas, scale):
    added, (keep_ref, sum_ref, *send_refs) = rest[:deltas], rest[deltas:]
    chains, rows, width = keep_ref.shape
    sum_ref[...] = sum(ref[...] for ref in added)
    for other in (1, 0):
        for chain in range(chains):
            target = send_refs[chain] if other else keep_ref.at[chain]
            span = ways((2 * chain + (place[3 + chain] ^ other)) * rows, rows)
            delta = sum_ref[pl.ds(place[2], 1), span] * scale
            delta = jnp.transpose(jnp.broadcast_to(delta, (128, rows)))
            for start in range(0, width, 128):
                columns = slice(start, start + 128)
                direct = own_ref[0, span, columns] + received_ref[0, span, columns]
                weighted = own_ref[1, span, columns] + received_ref[1, span, columns]
                target[:, columns] = (scale * direct - delta * weighted).astype(target.dtype)


def key_kernel(
    place, delta_ref, probs_ref, dprobs_ref, targets_ref, q_ref, values_ref, own_ref, send_ref,
    low_ref, *, chunk, scale,
):
    heads = probs_ref.shape[0]
    width = own_ref.shape[1] // heads
    share = own_ref.shape[0]
    parts = send_ref.shape[0] + 1
    send_ref[:, :, heads * width :] = values_ref[...]
    for head in range(heads):
        columns = slice(head * width, (head + 1) * width)
        for start in range(0, q_ref.shape[0], chunk):
            rows = slice(start, start + chunk)
            gap = dprobs_ref[head, :, rows] - (delta_ref[head : head + 1, rows] - 1.0)
            terms = onehot_less(probs_ref[head, :, rows] * gap, place, targets_ref, head, rows)
            low_ref[head, :, rows] = terms.astype(jnp.bfloat16)
        for step in range(parts):
            rows = ways(lax.rem(place[1] + step, parts) * share, share)
            term = scale * dot(low_ref[head, rows, :], q_ref[:, columns], NN)
            if step == 0:
                own_ref[:, columns] = term
            else:
                send_ref[step - 1, :, columns] = term.astype(jnp.bfloat16)


def split_kernel(place, keep_ref, *rest):
    chains = keep_ref.shape[0]
    came_refs, kept_ref, sent_refs = rest[:chains], rest[chains + 1], rest[chains + 2 :]
    rows = kept_ref.shape[1]
    for chain in range(chains):
        for other in (1, 0):
            target = sent_refs[chain] if other else kept_ref.at[chain]
            span = ways((place[3 + chains + chain] ^ other) * rows, rows)
            total = keep_ref[chain, span, :] + came_refs[chain][span, :].astype(jnp.float32)
            target[...] = total.astype(target.dtype)


def join_kernel(total_ref, came_ref, after_ref, *out_refs):
    for chain, out_ref in enumerate(out_refs):
        total = total_ref[chain].astype(jnp.float32) + came_ref[chain].astype(jnp.float32)
        out_ref[...] = total.astype(jnp.bfloat16)


def pool_kernel(key_ref, value_ref, received_ref, key_out, value_out):
    wide = key_ref.shape[1]
    key_sum, value_sum = key_ref[...], value_ref[...]
    for step in range(received_ref.shape[0]):
        key_sum += received_ref[step, :, :wide].astype(jnp.float32)
        value_sum += received_ref[step, :, wide:].astype(jnp.float32)
    key_out[...] = key_sum.astype(jnp.bfloat16)
    value_out[...] = value_sum.astype(jnp.bfloat16)


def place_kernel(place, *rest, sources, pieces, piece):
    out_ref, sems = rest[-2:]
    copies = []
    for ref, (side, chain, first) in zip(rest, sources):
        width = ref.shape[1]
        columns = ways((place[0] ^ side) * width, width)
        for index in range(ref.shape[0] // piece):
            natural = chain * pieces + ((first + index) ^ place[1 + chain])
            rows = ways(natural * piece, piece)
            copies.append(
                pltpu.make_async_copy(
                    ref.at[pl.ds(index * piece, piece)], out_ref.at[rows, columns], sems.at[len(copies)]
                )
            )
            copies[-1].start()
    for copy in copies:
        copy.wait()


def call(kernel, name, inputs, in_specs, outputs, flops, scratch=(), out_specs=None, aliases={}):
    return pl.pallas_call(
        kernel,
        in_specs=in_specs,
        out_specs=[IN_VMEM] * len(outputs) if out_specs is None else out_specs,
        out_shape=outputs,
        scratch_shapes=list(scratch),
        input_output_aliases=aliases,
        cost_estimate=pl.CostEstimate(flops=flops, bytes_accessed=flops // 1000, transcendentals=0),
        compiler_params=PARAMS,
        name=name,
    )(*inputs)


def on_device(queries, pool_keys, pool_values, out_grad, lse, compat, targets):
    heads, value_blocks, blocks = compat.shape
    query_count, wide = queries.shape
    value_count = pool_keys.shape[0]
    width = wide // heads
    scale = width ** -0.5
    value_devices, parts = lax.axis_size("val"), lax.axis_size("qry")
    bits = value_devices.bit_length() - 1
    assert heads == 2 and value_blocks == 1 and value_devices == 1 << bits and bits >= 4
    val, qry = lax.axis_index("val"), lax.axis_index("qry")
    core = lax.rem(val, 2)
    share = value_count // parts
    f32, bf16 = jnp.float32, jnp.bfloat16

    def flip(array, mask):
        return lax.ppermute(array, "val", [(i, i ^ mask) for i in range(value_devices)])

    def swap_shares(send):
        return jnp.stack([
            lax.ppermute(send[step - 1], "qry", [(i, (i + step) % parts) for i in range(parts)])
            for step in range(1, parts)
        ])

    def add(own, received):
        for array in received:
            own = own + array.astype(f32)
        return own

    def bit_of(bit):
        return lax.rem(val // (1 << bit), 2)

    pieces = 1 << (bits - 2)
    chains = 2 if query_count % (2 * pieces * 16) == 0 else 1
    orders = [[1, 2], [2, 1]][:chains]
    place = jnp.stack(
        [val, qry, core] + [bit_of(order[stage]) for stage in range(2) for order in orders]
    ).astype(jnp.int32)
    work = 2 * query_count * value_count * width

    delta, probs, dprobs, q_near, g_near, k_near = call(
        partial(forward_kernel, heads=heads, blocks=blocks, scale=scale),
        "forward_pass",
        (place,)
        + tuple(
            pltpu.with_memory_space_constraint(array, pltpu.HBM)
            for array in (
                compat, queries, out_grad, pool_keys, pool_values, lse, jnp.transpose(targets)
            )
        ),
        [IN_SMEM, IN_SMEM] + [IN_HBM] * 4 + [IN_VMEM] * 2,
        [
            pltpu.VMEM((heads, query_count), f32),
            pltpu.VMEM((heads, value_count, query_count), f32),
            pltpu.VMEM((heads, value_count, query_count), f32),
            pltpu.VMEM(queries.shape, bf16),
            pltpu.VMEM(queries.shape, bf16),
            pltpu.VMEM(pool_keys.shape, bf16),
        ],
        4 * work,
        [
            pltpu.VMEM(pool_values.shape, bf16),
            pltpu.SemaphoreType.DMA((2 + 2 * blocks,)),
        ],
    )
    shares = [
        pltpu.VMEM((share, wide), f32),
        pltpu.VMEM((parts - 1, share, wide), bf16),
    ]
    value_own, value_send = call(
        value_kernel, "value_terms", (place, probs, g_near), [IN_SMEM] + [IN_VMEM] * 2, shares, 2 * work
    )
    chunk = query_count // 3 if query_count % 384 == 0 else query_count
    rows_of = pltpu.VMEM((2, query_count, width), f32)
    targets = jnp.transpose(targets)

    def query_terms(own, name):
        return call(
            partial(query_kernel, own=own, chunk=chunk),
            name,
            (place, probs, dprobs, targets, k_near),
            [IN_SMEM] + [IN_VMEM] * 4,
            [rows_of],
            4 * work,
        )[0]

    other = query_terms(False, "other_head")
    received = None
    stride = 1
    added = [delta]
    while stride < value_devices:
        if stride > 1:
            terms = other if received is None else received
            delta, terms = call(
                delta_kernel,
                "delta_sum",
                (*added, terms),
                [IN_VMEM] * len(added) + [IN_HBM],
                [pltpu.VMEM((heads, query_count), f32), rows_of],
                heads * query_count,
                out_specs=[IN_VMEM, IN_HBM],
                aliases={len(added): 1},
            )
            received = flip(terms, 1) if received is None else terms
        steps = min(4, value_devices // stride)
        added = [delta] + [flip(delta, stride * step) for step in range(1, steps)]
        stride *= steps
    half = query_count // (2 * chains)
    keep, delta, *send = call(
        partial(combine_kernel, deltas=len(added), scale=scale),
        "combine",
        (place, query_terms(True, "own_head"), received, *added),
        [IN_SMEM] + [IN_VMEM] * (2 + len(added)),
        [
            pltpu.VMEM((chains, half, width), f32),
            pltpu.VMEM((heads, query_count), f32),
        ]
        + [pltpu.VMEM((half, width), bf16)] * chains,
        work // 4,
    )
    key_own, pool_send = call(
        partial(key_kernel, chunk=chunk, scale=scale),
        "key_terms",
        (place, delta, probs, dprobs, targets, q_near, value_send),
        [IN_SMEM] + [IN_VMEM] * 6,
        [shares[0], pltpu.VMEM((parts - 1, share, 2 * wide), bf16)],
        2 * work,
        [pltpu.VMEM((heads, value_count, query_count), bf16)],
    )
    pool_received = swap_shares(pool_send)

    came = [flip(send[chain], 1 << order[0]) for chain, order in enumerate(orders)]
    kept, *sent = call(
        split_kernel,
        "split",
        (place, keep, *came, pool_send),
        [IN_SMEM] + [IN_VMEM] * (1 + chains) + [IN_HBM],
        [pltpu.VMEM((chains, half // 2, width), f32)]
        + [pltpu.VMEM((half // 2, width), bf16)] * chains,
        work // 8,
    )
    total = jnp.stack(
        [
            kept[chain] + flip(sent[chain], 1 << order[1]).astype(f32)
            for chain, order in enumerate(orders)
        ]
    )
    for bit in range(3, bits - 1):
        split = total.reshape(chains, 2, -1, width)
        pick = partial(lax.dynamic_index_in_dim, split, axis=1, keepdims=False)
        came = flip(pick(1 - bit_of(bit)).astype(bf16), 1 << bit)
        total = pick(bit_of(bit)) + came.astype(f32)
    total = total.astype(bf16)
    piece = total.shape[1]
    joined = call(
        join_kernel,
        "join",
        (total, flip(total, 1 << (bits - 1)), pool_received),
        [IN_VMEM] * 2 + [IN_HBM],
        [pltpu.VMEM((piece, width), bf16)] * chains,
        work // 16,
    )
    key_grad, value_grad = call(
        pool_kernel,
        "pool_sum",
        (key_own, value_own, pool_received),
        [IN_VMEM] * 3,
        [pltpu.HBM((share, wide), bf16)] * 2,
        work // 8,
    )
    first_half, second_half, own_piece = [], [], []
    for chain, order in enumerate(orders):
        part = joined[chain]
        for bit in list(range(bits - 2, 2, -1)) + [order[1]]:
            part = jnp.concatenate([part, flip(part, 1 << bit)], axis=0)
        first_half.append(part)
        second_half.append(flip(part, 1 << order[0]))
        index = 0
        for bit in order + list(range(3, bits - 1)):
            index = 2 * index + bit_of(bit)
        own_piece.append(index)
    pieces_place = jnp.stack([core] + own_piece).astype(jnp.int32)
    near = partial(pltpu.with_memory_space_constraint, memory_space=pltpu.VMEM)
    early, late = [], []
    for chain in range(chains):
        early.append((first_half[chain], 0, chain, 0))
        early.append((second_half[chain], 0, chain, pieces // 2))
        early.append((flip(first_half[chain], 1), 1, chain, 0))
        late.append((flip(second_half[chain], 1), 1, chain, pieces // 2))
    before = (pltpu.with_memory_space_constraint(key_grad, pltpu.HBM),)
    for name, sources in (("own_columns", early), ("other_columns", late)):
        copied = len(sources)
        before = call(
            partial(
                place_kernel,
                sources=[source[1:] for source in sources],
                pieces=pieces,
                piece=piece,
            ),
            name,
            (pieces_place, *[near(source[0]) for source in sources], *before),
            [IN_SMEM] + [IN_VMEM] * copied + [IN_HBM],
            [jax.ShapeDtypeStruct((query_count, wide), bf16)],
            work // 4,
            [pltpu.SemaphoreType.DMA((copied * pieces // 2,))],
            [IN_HBM],
            {1 + copied: 0} if name == "other_columns" else {},
        )
    return before[0], key_grad, value_grad


def solution(mesh):
    placed = (
        P("qry", None),
        P("val", None),
        P("val", None),
        P("qry", None),
        P(None, "qry"),
        P(None, "val", "qry"),
        P("qry", None),
    )
    return jax.shard_map(
        on_device,
        mesh=mesh,
        in_specs=placed,
        out_specs=(P("qry", None), P(("val", "qry"), None), P(("val", "qry"), None)),
        check_vma=False,
    )
```

```python
import math
from functools import partial

import jax
import jax.numpy as jnp
from jax import lax
from jax.experimental import pallas as pl
from jax.experimental.pallas import tpu as pltpu
from jax.sharding import PartitionSpec as P

LOG2E = math.log2(math.e)
MASKED = 1e30
NT = (((1,), (1,)), ((), ()))
NN = (((1,), (0,)), ((), ()))
PARAMS = pltpu.CompilerParams(vmem_limit_bytes=24 * 1024 * 1024)
IN_VMEM = pl.BlockSpec(memory_space=pltpu.VMEM)
IN_SMEM = pl.BlockSpec(memory_space=pltpu.SMEM)
IN_HBM = pl.BlockSpec(memory_space=pl.ANY)


def dot(a, b, dims):
    return lax.dot_general(a, b, dims, preferred_element_type=jnp.float32)


def ways(start, size):
    return pl.ds(pl.multiple_of(start, size), size)


def forward_kernel(
    compat_hbm, q_hbm, g_hbm, k_hbm, v_hbm, lse_hbm, targets_hbm,
    delta_ref, probs_ref, dprobs_ref, q_ref, g_ref, k_ref,
    v_ref, lse_ref, targets_ref, compat, sems, *, heads, blocks, scale,
):
    value_count, width = k_ref.shape[0], k_ref.shape[1] // heads
    block = q_ref.shape[0] // blocks
    pairs = [
        (compat_hbm, compat), (targets_hbm, targets_ref), (lse_hbm, lse_ref),
        (k_hbm, k_ref), (v_hbm, v_ref),
    ]
    small = len(pairs)
    for index in range(blocks):
        rows = pl.ds(index * block, block)
        pairs += [(q_hbm.at[rows], q_ref.at[rows]), (g_hbm.at[rows], g_ref.at[rows])]
    copies = [pltpu.make_async_copy(*pair, sems.at[n]) for n, pair in enumerate(pairs)]
    for copy in copies:
        copy.start()
    for copy in copies[:3]:
        copy.wait()
    local = targets_ref[...] - lax.axis_index("val") * value_count
    hit = jnp.where((local >= 0) & (local < value_count), 1.0, 0.0)
    lives = []
    for index in range(blocks):
        live = jnp.max(hit[:, index * block : (index + 1) * block]) > 0.0
        for head in range(heads):
            live = live | (compat[head, 0, index] == 1)
        lives.append(live)
    for copy in copies[3:small]:
        copy.wait()
    for index in range(blocks):
        rows = slice(index * block, (index + 1) * block)
        copies[small + 2 * index].wait()
        copies[small + 2 * index + 1].wait()
        live = lives[index]

        @pl.when(live)
        def _():
            for head in range(heads):
                columns = slice(head * width, (head + 1) * width)
                usable = (hit[head : head + 1, rows] > 0.0) | (compat[head, 0, index] == 1)
                lse_rows = jnp.where(usable, lse_ref[head : head + 1, rows], MASKED) * LOG2E
                scores = dot(k_ref[:, columns], q_ref[rows, columns], NT)
                dprobs = dot(v_ref[:, columns], g_ref[rows, columns], NT)
                probs = jnp.exp2(scores * (scale * LOG2E) - lse_rows)
                delta = jnp.sum(probs * dprobs, axis=0, keepdims=True)
                weight = jnp.sum(probs, axis=0, keepdims=True)
                delta_ref[head : head + 1, rows] = delta
                centre = delta / jnp.maximum(weight, 1e-30)
                delta_ref[heads + head : heads + head + 1, rows] = centre
                probs_ref[head, :, rows] = probs
                dprobs_ref[head, :, rows] = dprobs

        @pl.when(jnp.logical_not(live))
        def _():
            for head in range(heads):
                for row in (head, heads + head):
                    delta_ref[row : row + 1, rows] = jnp.zeros((1, block), jnp.float32)
                probs_ref[head, :, rows] = jnp.zeros((value_count, block), jnp.float32)
                dprobs_ref[head, :, rows] = jnp.zeros((value_count, block), jnp.float32)


def value_kernel(place, probs_ref, g_ref, own_ref, send_ref):
    heads, _, _ = probs_ref.shape
    width = g_ref.shape[1] // heads
    share = own_ref.shape[0]
    parts = send_ref.shape[0] + 1
    for step in range(parts):
        rows = ways(lax.rem(place[1] + step, parts) * share, share)
        for head in range(heads):
            columns = slice(head * width, (head + 1) * width)
            term = dot(probs_ref[head, rows, :].astype(jnp.bfloat16), g_ref[:, columns], NN)
            if step == 0:
                own_ref[:, columns] = term
            else:
                send_ref[step - 1, :, columns] = term.astype(jnp.bfloat16)


def onehot_less(terms, place, targets_ref, head, rows):
    local = targets_ref[pl.ds(head, 1), rows] - place[0] * terms.shape[0]
    slots = lax.broadcasted_iota(jnp.int32, terms.shape, 0)
    return jnp.where(slots == local, terms - 1.0, terms)


def query_kernel(
    place, delta_ref, probs_ref, dprobs_ref, targets_ref, k_ref, out_ref, *, own, chunk
):
    head = place[2] if own else 1 - place[2]
    width = out_ref.shape[2]
    heads = probs_ref.shape[0]
    keys = jnp.transpose(k_ref[:, ways(head * width, width)])
    for start in range(0, out_ref.shape[1], chunk):
        rows = slice(start, start + chunk)
        probs = probs_ref[head, :, rows]
        gap = dprobs_ref[head, :, rows] - (delta_ref[pl.ds(heads + head, 1), rows] - 1.0)
        terms = onehot_less(probs * gap, place, targets_ref, head, rows)
        for index, factor in enumerate((terms, probs)):
            product = dot(keys, factor.astype(jnp.bfloat16), NN)
            out_ref[index, rows, :] = jnp.transpose(product)


def delta_kernel(*refs):
    *added, terms_ref, out_ref, same_terms_ref = refs
    heads = out_ref.shape[0]
    out_ref[...] = sum(ref[:heads] for ref in added)


def combine_kernel(
    place, own_ref, received_ref, centre_ref, came_ref, *rest, deltas, scale
):
    added, (keep_ref, sum_ref, *send_refs) = rest[:deltas], rest[deltas:]
    chains, rows, width = keep_ref.shape
    heads = sum_ref.shape[0]
    sum_ref[...] = sum(ref[...] for ref in added)

    def column(ref, span):
        row = sum_ref[pl.ds(place[2], 1), span] - ref[pl.ds(heads + place[2], 1), span]
        return jnp.transpose(jnp.broadcast_to(row * scale, (128, rows)))

    for other in (1, 0):
        for chain in range(chains):
            target = send_refs[chain] if other else keep_ref.at[chain]
            span = ways((2 * chain + (place[3 + chain] ^ other)) * rows, rows)
            gaps = column(centre_ref, span), column(came_ref, span)
            for start in range(0, width, 128):
                columns = slice(start, start + 128)
                direct = own_ref[0, span, columns] + received_ref[0, span, columns]
                weighted = own_ref[1, span, columns] * gaps[0]
                weighted += received_ref[1, span, columns] * gaps[1]
                target[:, columns] = (scale * direct - weighted).astype(target.dtype)


def key_kernel(
    place, delta_ref, probs_ref, dprobs_ref, targets_ref, q_ref, values_ref, own_ref, send_ref,
    low_ref, *, chunk, scale,
):
    heads = probs_ref.shape[0]
    width = own_ref.shape[1] // heads
    share = own_ref.shape[0]
    parts = send_ref.shape[0] + 1
    send_ref[:, :, heads * width :] = values_ref[...]
    for head in range(heads):
        columns = slice(head * width, (head + 1) * width)
        for start in range(0, q_ref.shape[0], chunk):
            rows = slice(start, start + chunk)
            gap = dprobs_ref[head, :, rows] - (delta_ref[head : head + 1, rows] - 1.0)
            terms = onehot_less(probs_ref[head, :, rows] * gap, place, targets_ref, head, rows)
            low_ref[head, :, rows] = terms.astype(jnp.bfloat16)
        for step in range(parts):
            rows = ways(lax.rem(place[1] + step, parts) * share, share)
            term = scale * dot(low_ref[head, rows, :], q_ref[:, columns], NN)
            if step == 0:
                own_ref[:, columns] = term
            else:
                send_ref[step - 1, :, columns] = term.astype(jnp.bfloat16)


def split_kernel(place, keep_ref, *rest):
    chains = keep_ref.shape[0]
    came_refs, kept_ref, sent_refs = rest[:chains], rest[chains + 1], rest[chains + 2 :]
    rows = kept_ref.shape[1]
    for chain in range(chains):
        for other in (1, 0):
            target = sent_refs[chain] if other else kept_ref.at[chain]
            span = ways((place[3 + chains + chain] ^ other) * rows, rows)
            total = keep_ref[chain, span, :] + came_refs[chain][span, :].astype(jnp.float32)
            target[...] = total.astype(target.dtype)


def join_kernel(total_ref, came_ref, after_ref, *out_refs):
    for chain, out_ref in enumerate(out_refs):
        total = total_ref[chain].astype(jnp.float32) + came_ref[chain].astype(jnp.float32)
        out_ref[...] = total.astype(jnp.bfloat16)


def pool_kernel(key_ref, value_ref, received_ref, key_out, value_out):
    wide = key_ref.shape[1]
    key_sum, value_sum = key_ref[...], value_ref[...]
    for step in range(received_ref.shape[0]):
        key_sum += received_ref[step, :, :wide].astype(jnp.float32)
        value_sum += received_ref[step, :, wide:].astype(jnp.float32)
    key_out[...] = key_sum.astype(jnp.bfloat16)
    value_out[...] = value_sum.astype(jnp.bfloat16)


def after_kernel(*refs):
    pass


def place_kernel(place, *rest, sources, pieces, piece):
    out_ref, sems = rest[-2:]
    copies = []
    for ref, (side, chain, first) in zip(rest, sources):
        width = ref.shape[1]
        columns = ways((place[0] ^ side) * width, width)
        for index in range(ref.shape[0] // piece):
            natural = chain * pieces + ((first + index) ^ place[1 + chain])
            rows = ways(natural * piece, piece)
            copies.append(
                pltpu.make_async_copy(
                    ref.at[pl.ds(index * piece, piece)], out_ref.at[rows, columns], sems.at[len(copies)]
                )
            )
            copies[-1].start()
    for copy in copies:
        copy.wait()


def call(kernel, name, inputs, in_specs, outputs, flops, scratch=(), out_specs=None, aliases={}):
    return pl.pallas_call(
        kernel,
        in_specs=in_specs,
        out_specs=[IN_VMEM] * len(outputs) if out_specs is None else out_specs,
        out_shape=outputs,
        scratch_shapes=list(scratch),
        input_output_aliases=aliases,
        cost_estimate=pl.CostEstimate(flops=flops, bytes_accessed=flops // 1000, transcendentals=0),
        compiler_params=PARAMS,
        name=name,
    )(*inputs)


def on_device(queries, pool_keys, pool_values, out_grad, lse, compat, targets):
    heads, value_blocks, blocks = compat.shape
    query_count, wide = queries.shape
    value_count = pool_keys.shape[0]
    width = wide // heads
    scale = width ** -0.5
    value_devices, parts = lax.axis_size("val"), lax.axis_size("qry")
    bits = value_devices.bit_length() - 1
    assert heads == 2 and value_blocks == 1 and value_devices == 1 << bits and bits >= 4
    val, qry = lax.axis_index("val"), lax.axis_index("qry")
    core = lax.rem(val, 2)
    share = value_count // parts
    f32, bf16 = jnp.float32, jnp.bfloat16

    def flip(array, mask):
        return lax.ppermute(array, "val", [(i, i ^ mask) for i in range(value_devices)])

    def swap_shares(send):
        return jnp.stack([
            lax.ppermute(send[step - 1], "qry", [(i, (i + step) % parts) for i in range(parts)])
            for step in range(1, parts)
        ])

    def add(own, received):
        for array in received:
            own = own + array.astype(f32)
        return own

    def bit_of(bit):
        return lax.rem(val // (1 << bit), 2)

    pieces = 1 << (bits - 2)
    chains = 2 if query_count % (2 * pieces * 16) == 0 else 1
    orders = [[1, 2], [2, 1]][:chains]
    place = jnp.stack(
        [val, qry, core] + [bit_of(order[stage]) for stage in range(2) for order in orders]
    ).astype(jnp.int32)
    work = 2 * query_count * value_count * width

    delta, probs, dprobs, q_near, g_near, k_near = call(
        partial(forward_kernel, heads=heads, blocks=blocks, scale=scale),
        "forward_pass",
        tuple(
            pltpu.with_memory_space_constraint(array, pltpu.HBM)
            for array in (
                compat, queries, out_grad, pool_keys, pool_values, lse, jnp.transpose(targets)
            )
        ),
        [IN_HBM] * 7,
        [
            pltpu.VMEM((2 * heads, query_count), f32),
            pltpu.VMEM((heads, value_count, query_count), f32),
            pltpu.VMEM((heads, value_count, query_count), f32),
            pltpu.VMEM(queries.shape, bf16),
            pltpu.VMEM(queries.shape, bf16),
            pltpu.VMEM(pool_keys.shape, bf16),
        ],
        4 * work,
        [
            pltpu.VMEM(pool_values.shape, bf16),
            pltpu.VMEM((heads, query_count), f32),
            pltpu.VMEM((heads, query_count), jnp.int32),
            pltpu.SMEM(compat.shape, jnp.int32),
            pltpu.SemaphoreType.DMA((5 + 2 * blocks,)),
        ],
    )
    shares = [
        pltpu.VMEM((share, wide), f32),
        pltpu.VMEM((parts - 1, share, wide), bf16),
    ]
    value_own, value_send = call(
        value_kernel, "value_terms", (place, probs, g_near), [IN_SMEM] + [IN_VMEM] * 2, shares, 2 * work
    )
    chunk = query_count // 3 if query_count % 384 == 0 else query_count
    rows_of = pltpu.VMEM((2, query_count, width), f32)
    targets = jnp.transpose(targets)

    def query_terms(own, name):
        return call(
            partial(query_kernel, own=own, chunk=chunk),
            name,
            (place, centre, probs, dprobs, targets, k_near),
            [IN_SMEM] + [IN_VMEM] * 5,
            [rows_of],
            2 * work,
        )[0]

    centre = delta
    other = query_terms(False, "other_head")
    received = None
    stride = 1
    added = [delta]
    while stride < value_devices:
        if stride > 1:
            terms = other if received is None else received
            delta, terms = call(
                delta_kernel,
                "delta_sum",
                (*added, terms),
                [IN_VMEM] * len(added) + [IN_HBM],
                [pltpu.VMEM((heads, query_count), f32), rows_of],
                heads * query_count,
                out_specs=[IN_VMEM, IN_HBM],
                aliases={len(added): 1},
            )
            received = flip(terms, 1) if received is None else terms
        steps = min(4, value_devices // stride)
        added = [delta] + [flip(delta, stride * step) for step in range(1, steps)]
        if stride == 1:
            other_centre = added[1]
        stride *= steps
    half = query_count // (2 * chains)
    keep, delta, *send = call(
        partial(combine_kernel, deltas=len(added), scale=scale),
        "combine",
        (place, query_terms(True, "own_head"), received, centre, other_centre, *added),
        [IN_SMEM] + [IN_VMEM] * (4 + len(added)),
        [
            pltpu.VMEM((chains, half, width), f32),
            pltpu.VMEM((heads, query_count), f32),
        ]
        + [pltpu.VMEM((half, width), bf16)] * chains,
        work // 4,
    )
    key_own, pool_send = call(
        partial(key_kernel, chunk=chunk, scale=scale),
        "key_terms",
        (place, delta, probs, dprobs, targets, q_near, value_send),
        [IN_SMEM] + [IN_VMEM] * 6,
        [shares[0], pltpu.VMEM((parts - 1, share, 2 * wide), bf16)],
        2 * work,
        [pltpu.VMEM((heads, value_count, query_count), bf16)],
    )
    pool_received = swap_shares(pool_send)

    came = [flip(send[chain], 1 << order[0]) for chain, order in enumerate(orders)]
    kept, *sent = call(
        split_kernel,
        "split",
        (place, keep, *came, pool_send),
        [IN_SMEM] + [IN_VMEM] * (1 + chains) + [IN_HBM],
        [pltpu.VMEM((chains, half // 2, width), f32)]
        + [pltpu.VMEM((half // 2, width), bf16)] * chains,
        work // 8,
    )
    total = jnp.stack(
        [
            kept[chain] + flip(sent[chain], 1 << order[1]).astype(f32)
            for chain, order in enumerate(orders)
        ]
    )
    for bit in range(3, bits - 1):
        split = total.reshape(chains, 2, -1, width)
        pick = partial(lax.dynamic_index_in_dim, split, axis=1, keepdims=False)
        came = flip(pick(1 - bit_of(bit)).astype(bf16), 1 << bit)
        total = pick(bit_of(bit)) + came.astype(f32)
    total = total.astype(bf16)
    piece = total.shape[1]
    joined = call(
        join_kernel,
        "join",
        (total, flip(total, 1 << (bits - 1)), pool_received),
        [IN_VMEM] * 2 + [IN_HBM],
        [pltpu.VMEM((piece, width), bf16)] * chains,
        work // 16,
    )
    key_grad, value_grad = call(
        pool_kernel,
        "pool_sum",
        (key_own, value_own, pool_received),
        [IN_VMEM] * 3,
        [pltpu.HBM((share, wide), bf16)] * 2,
        work // 8,
    )
    first_half, second_half, own_piece = [], [], []
    for chain, order in enumerate(orders):
        part = joined[chain]
        for bit in list(range(bits - 2, 2, -1)) + [order[1]]:
            part = jnp.concatenate([part, flip(part, 1 << bit)], axis=0)
        first_half.append(part)
        second_half.append(flip(part, 1 << order[0]))
        index = 0
        for bit in order + list(range(3, bits - 1)):
            index = 2 * index + bit_of(bit)
        own_piece.append(index)
    pieces_place = jnp.stack([core] + own_piece).astype(jnp.int32)
    near = partial(pltpu.with_memory_space_constraint, memory_space=pltpu.VMEM)
    far = partial(pltpu.with_memory_space_constraint, memory_space=pltpu.HBM)

    def placed(name, sources, before, aliases):
        copied = len(sources)
        return call(
            partial(
                place_kernel,
                sources=[source[1:] for source in sources],
                pieces=pieces,
                piece=piece,
            ),
            name,
            (pieces_place, *[near(source[0]) for source in sources], far(before)),
            [IN_SMEM] + [IN_VMEM] * copied + [IN_HBM],
            [pltpu.HBM((query_count, wide), bf16)],
            work // 2,
            [pltpu.SemaphoreType.DMA((copied * pieces // 2,))],
            [IN_HBM],
            {1 + copied: 0} if aliases else {},
        )[0]

    sources = [(part, 0, chain, 0) for chain, part in enumerate(first_half)]
    sources += [(flip(part, 1), 1, chain, 0) for chain, part in enumerate(first_half)]
    begun = placed("first_rows", sources, key_grad, False)
    second_half = call(
        after_kernel,
        "after",
        (*second_half, far(begun)),
        [IN_HBM] * (chains + 1),
        [pltpu.VMEM((half, width), bf16)] * chains,
        work // 1000,
        out_specs=[IN_HBM] * chains,
        aliases={chain: chain for chain in range(chains)},
    )
    sources = [(part, 0, chain, pieces // 2) for chain, part in enumerate(second_half)]
    begun = placed("own_rows", sources, begun, True)
    sources = [(flip(part, 1), 1, chain, pieces // 2) for chain, part in enumerate(second_half)]
    return placed("other_rows", sources, begun, True), key_grad, value_grad


def solution(mesh):
    placed = (
        P("qry", None),
        P("val", None),
        P("val", None),
        P("qry", None),
        P(None, "qry"),
        P(None, "val", "qry"),
        P("qry", None),
    )
    return jax.shard_map(
        on_device,
        mesh=mesh,
        in_specs=placed,
        out_specs=(P("qry", None), P(("val", "qry"), None), P(("val", "qry"), None)),
        check_vma=False,
    )
```

```python
import math
from functools import partial

import jax
import jax.numpy as jnp
from jax import lax
from jax.experimental import pallas as pl
from jax.experimental.pallas import tpu as pltpu
from jax.sharding import PartitionSpec as P

LOG2E = math.log2(math.e)
MASKED = 1e30
NT = (((1,), (1,)), ((), ()))
NN = (((1,), (0,)), ((), ()))
PARAMS = pltpu.CompilerParams(vmem_limit_bytes=16 * 1024 * 1024)
IN_VMEM = pl.BlockSpec(memory_space=pltpu.VMEM)
IN_SMEM = pl.BlockSpec(memory_space=pltpu.SMEM)
IN_HBM = pl.BlockSpec(memory_space=pl.ANY)


def dot(a, b, dims):
    return lax.dot_general(a, b, dims, preferred_element_type=jnp.float32)


def ways(start, size):
    return pl.ds(pl.multiple_of(start, size), size)


def forward_kernel(
    place, compat_hbm, q_hbm, g_hbm, k_hbm, v_hbm, lse_hbm, targets_hbm,
    delta_ref, probs_ref, dprobs_ref, q_ref, g_ref, k_ref,
    v_ref, lse_ref, targets_ref, compat, sems, *, heads, blocks, scale,
):
    value_count, width = k_ref.shape[0], k_ref.shape[1] // heads
    block = q_ref.shape[0] // blocks
    pairs = [
        (compat_hbm, compat), (targets_hbm, targets_ref), (lse_hbm, lse_ref),
        (k_hbm, k_ref), (v_hbm, v_ref),
    ]
    small = len(pairs)
    for index in range(blocks):
        rows = pl.ds(index * block, block)
        pairs += [(q_hbm.at[rows], q_ref.at[rows]), (g_hbm.at[rows], g_ref.at[rows])]
    copies = [pltpu.make_async_copy(*pair, sems.at[n]) for n, pair in enumerate(pairs)]
    for copy in copies:
        copy.start()
    for copy in copies[:3]:
        copy.wait()
    local = targets_ref[...] - lax.axis_index("val") * value_count
    hit = jnp.where((local >= 0) & (local < value_count), 1.0, 0.0)
    lives = []
    for index in range(blocks):
        live = jnp.max(hit[:, index * block : (index + 1) * block]) > 0.0
        for head in range(heads):
            live = live | (compat[head, 0, index] == 1)
        lives.append(live)
    for copy in copies[3:small]:
        copy.wait()
    for index in range(blocks):
        rows = slice(index * block, (index + 1) * block)
        copies[small + 2 * index].wait()
        copies[small + 2 * index + 1].wait()
        live = lives[index]

        @pl.when(live)
        def _():
            for head in range(heads):
                columns = slice(head * width, (head + 1) * width)
                usable = (hit[head : head + 1, rows] > 0.0) | (compat[head, 0, index] == 1)
                lse_rows = jnp.where(usable, lse_ref[head : head + 1, rows], MASKED) * LOG2E
                scores = dot(k_ref[:, columns], q_ref[rows, columns], NT)
                dprobs = dot(v_ref[:, columns], g_ref[rows, columns], NT)
                probs = jnp.exp2(scores * (scale * LOG2E) - lse_rows)
                delta = jnp.sum(probs * dprobs, axis=0, keepdims=True)
                weight = jnp.sum(probs, axis=0, keepdims=True)
                delta_ref[head : head + 1, rows] = delta
                centre = delta / jnp.maximum(weight, 1e-30)
                delta_ref[heads + head : heads + head + 1, rows] = centre
                probs_ref[head, :, rows] = probs
                dprobs_ref[head, :, rows] = dprobs

        @pl.when(jnp.logical_not(live))
        def _():
            for head in range(heads):
                for row in (head, heads + head):
                    delta_ref[row : row + 1, rows] = jnp.zeros((1, block), jnp.float32)
                probs_ref[head, :, rows] = jnp.zeros((value_count, block), jnp.float32)
                dprobs_ref[head, :, rows] = jnp.zeros((value_count, block), jnp.float32)


def value_kernel(place, probs_ref, g_ref, own_ref, send_ref):
    heads, _, _ = probs_ref.shape
    width = g_ref.shape[1] // heads
    share = own_ref.shape[0]
    parts = send_ref.shape[0] + 1
    for step in range(parts):
        rows = ways(lax.rem(place[1] + step, parts) * share, share)
        for head in range(heads):
            columns = slice(head * width, (head + 1) * width)
            term = dot(probs_ref[head, rows, :].astype(jnp.bfloat16), g_ref[:, columns], NN)
            if step == 0:
                own_ref[:, columns] = term
            else:
                send_ref[step - 1, :, columns] = term.astype(jnp.bfloat16)


def onehot_less(terms, place, targets_ref, head, rows):
    local = targets_ref[pl.ds(head, 1), rows] - place[0] * terms.shape[0]
    slots = lax.broadcasted_iota(jnp.int32, terms.shape, 0)
    return jnp.where(slots == local, terms - 1.0, terms)


def query_kernel(
    place, delta_ref, probs_ref, dprobs_ref, targets_ref, k_ref, out_ref, *, own, chunk
):
    head = place[2] if own else 1 - place[2]
    width = out_ref.shape[2]
    heads = probs_ref.shape[0]
    keys = jnp.transpose(k_ref[:, ways(head * width, width)])
    for start in range(0, out_ref.shape[1], chunk):
        rows = slice(start, start + chunk)
        probs = probs_ref[head, :, rows]
        gap = dprobs_ref[head, :, rows] - (delta_ref[pl.ds(heads + head, 1), rows] - 1.0)
        terms = onehot_less(probs * gap, place, targets_ref, head, rows)
        for index, factor in enumerate((terms, probs)):
            product = dot(keys, factor.astype(jnp.bfloat16), NN)
            out_ref[index, rows, :] = jnp.transpose(product)


def delta_kernel(*refs):
    *added, terms_ref, out_ref, same_terms_ref = refs
    heads = out_ref.shape[0]
    out_ref[...] = sum(ref[:heads] for ref in added)


def combine_kernel(
    place, own_ref, received_ref, centre_ref, came_ref, *rest, deltas, scale
):
    added, (keep_ref, sum_ref, *send_refs) = rest[:deltas], rest[deltas:]
    chains, rows, width = keep_ref.shape
    heads = sum_ref.shape[0]
    sum_ref[...] = sum(ref[...] for ref in added)

    def column(ref, span):
        row = sum_ref[pl.ds(place[2], 1), span] - ref[pl.ds(heads + place[2], 1), span]
        return jnp.transpose(jnp.broadcast_to(row * scale, (128, rows)))

    for other in (1, 0):
        for chain in range(chains):
            target = send_refs[chain] if other else keep_ref.at[chain]
            span = ways((2 * chain + (place[3 + chain] ^ other)) * rows, rows)
            gaps = column(centre_ref, span), column(came_ref, span)
            for start in range(0, width, 128):
                columns = slice(start, start + 128)
                direct = own_ref[0, span, columns] + received_ref[0, span, columns]
                weighted = own_ref[1, span, columns] * gaps[0]
                weighted += received_ref[1, span, columns] * gaps[1]
                target[:, columns] = (scale * direct - weighted).astype(target.dtype)


def key_kernel(
    place, delta_ref, probs_ref, dprobs_ref, targets_ref, q_ref, values_ref, own_ref, send_ref,
    low_ref, *, chunk, scale,
):
    heads = probs_ref.shape[0]
    width = own_ref.shape[1] // heads
    share = own_ref.shape[0]
    parts = send_ref.shape[0] + 1
    send_ref[:, :, heads * width :] = values_ref[...]
    for head in range(heads):
        columns = slice(head * width, (head + 1) * width)
        for start in range(0, q_ref.shape[0], chunk):
            rows = slice(start, start + chunk)
            gap = dprobs_ref[head, :, rows] - (delta_ref[head : head + 1, rows] - 1.0)
            terms = onehot_less(probs_ref[head, :, rows] * gap, place, targets_ref, head, rows)
            low_ref[head, :, rows] = terms.astype(jnp.bfloat16)
        for step in range(parts):
            rows = ways(lax.rem(place[1] + step, parts) * share, share)
            term = scale * dot(low_ref[head, rows, :], q_ref[:, columns], NN)
            if step == 0:
                own_ref[:, columns] = term
            else:
                send_ref[step - 1, :, columns] = term.astype(jnp.bfloat16)


def split_kernel(place, keep_ref, *rest):
    chains = keep_ref.shape[0]
    came_refs, kept_ref, sent_refs = rest[:chains], rest[chains + 1], rest[chains + 2 :]
    rows = kept_ref.shape[1]
    for chain in range(chains):
        for other in (1, 0):
            target = sent_refs[chain] if other else kept_ref.at[chain]
            span = ways((place[3 + chains + chain] ^ other) * rows, rows)
            total = keep_ref[chain, span, :] + came_refs[chain][span, :].astype(jnp.float32)
            target[...] = total.astype(target.dtype)


def join_kernel(total_ref, came_ref, after_ref, *out_refs):
    for chain, out_ref in enumerate(out_refs):
        total = total_ref[chain].astype(jnp.float32) + came_ref[chain].astype(jnp.float32)
        out_ref[...] = total.astype(jnp.bfloat16)


def pool_kernel(key_ref, value_ref, received_ref, key_out, value_out):
    wide = key_ref.shape[1]
    key_sum, value_sum = key_ref[...], value_ref[...]
    for step in range(received_ref.shape[0]):
        key_sum += received_ref[step, :, :wide].astype(jnp.float32)
        value_sum += received_ref[step, :, wide:].astype(jnp.float32)
    key_out[...] = key_sum.astype(jnp.bfloat16)
    value_out[...] = value_sum.astype(jnp.bfloat16)


def after_kernel(*refs):
    pass


def place_kernel(place, *rest, sources, pieces, piece):
    out_ref, sems = rest[-2:]
    copies = []
    for ref, (side, chain, first) in zip(rest, sources):
        width = ref.shape[1]
        columns = ways((place[0] ^ side) * width, width)
        for index in range(ref.shape[0] // piece):
            natural = chain * pieces + ((first + index) ^ place[1 + chain])
            rows = ways(natural * piece, piece)
            copies.append(
                pltpu.make_async_copy(
                    ref.at[pl.ds(index * piece, piece)], out_ref.at[rows, columns], sems.at[len(copies)]
                )
            )
            copies[-1].start()
    for copy in copies:
        copy.wait()


def call(kernel, name, inputs, in_specs, outputs, flops, scratch=(), out_specs=None, aliases={}):
    return pl.pallas_call(
        kernel,
        in_specs=in_specs,
        out_specs=[IN_VMEM] * len(outputs) if out_specs is None else out_specs,
        out_shape=outputs,
        scratch_shapes=list(scratch),
        input_output_aliases=aliases,
        cost_estimate=pl.CostEstimate(flops=flops, bytes_accessed=flops // 1000, transcendentals=0),
        compiler_params=PARAMS,
        name=name,
    )(*inputs)


def on_device(queries, pool_keys, pool_values, out_grad, lse, compat, targets):
    heads, value_blocks, blocks = compat.shape
    query_count, wide = queries.shape
    value_count = pool_keys.shape[0]
    width = wide // heads
    scale = width ** -0.5
    value_devices, parts = lax.axis_size("val"), lax.axis_size("qry")
    bits = value_devices.bit_length() - 1
    assert heads == 2 and value_blocks == 1 and value_devices == 1 << bits and bits >= 4
    val, qry = lax.axis_index("val"), lax.axis_index("qry")
    core = lax.rem(val, 2)
    share = value_count // parts
    f32, bf16 = jnp.float32, jnp.bfloat16

    def flip(array, mask):
        return lax.ppermute(array, "val", [(i, i ^ mask) for i in range(value_devices)])

    def swap_shares(send):
        return jnp.stack([
            lax.ppermute(send[step - 1], "qry", [(i, (i + step) % parts) for i in range(parts)])
            for step in range(1, parts)
        ])

    def add(own, received):
        for array in received:
            own = own + array.astype(f32)
        return own

    def bit_of(bit):
        return lax.rem(val // (1 << bit), 2)

    pieces = 1 << (bits - 2)
    chains = 2 if query_count % (2 * pieces * 16) == 0 else 1
    orders = [[1, 2], [2, 1]][:chains]
    place = jnp.stack(
        [val, qry, core] + [bit_of(order[stage]) for stage in range(2) for order in orders]
    ).astype(jnp.int32)
    work = 2 * query_count * value_count * width

    delta, probs, dprobs, q_near, g_near, k_near = call(
        partial(forward_kernel, heads=heads, blocks=blocks, scale=scale),
        "forward_pass",
        (place,)
        + tuple(
            pltpu.with_memory_space_constraint(array, pltpu.HBM)
            for array in (
                compat, queries, out_grad, pool_keys, pool_values, lse, jnp.transpose(targets)
            )
        ),
        [IN_HBM] * 8,
        [
            pltpu.VMEM((2 * heads, query_count), f32),
            pltpu.VMEM((heads, value_count, query_count), f32),
            pltpu.VMEM((heads, value_count, query_count), f32),
            pltpu.VMEM(queries.shape, bf16),
            pltpu.VMEM(queries.shape, bf16),
            pltpu.VMEM(pool_keys.shape, bf16),
        ],
        4 * work,
        [
            pltpu.VMEM(pool_values.shape, bf16),
            pltpu.VMEM((heads, query_count), f32),
            pltpu.VMEM((heads, query_count), jnp.int32),
            pltpu.SMEM(compat.shape, jnp.int32),
            pltpu.SemaphoreType.DMA((5 + 2 * blocks,)),
        ],
    )
    shares = [
        pltpu.VMEM((share, wide), f32),
        pltpu.VMEM((parts - 1, share, wide), bf16),
    ]
    value_own, value_send = call(
        value_kernel, "value_terms", (place, probs, g_near), [IN_SMEM] + [IN_VMEM] * 2, shares, 2 * work
    )
    chunk = query_count // 3 if query_count % 384 == 0 else query_count
    rows_of = pltpu.VMEM((2, query_count, width), f32)
    targets = jnp.transpose(targets)

    def query_terms(own, name):
        return call(
            partial(query_kernel, own=own, chunk=chunk),
            name,
            (place, centre, probs, dprobs, targets, k_near),
            [IN_SMEM] + [IN_VMEM] * 5,
            [rows_of],
            2 * work,
        )[0]

    centre = delta
    other = query_terms(False, "other_head")
    received = None
    stride = 1
    added = [delta]
    while stride < value_devices:
        if stride > 1:
            terms = other if received is None else received
            delta, terms = call(
                delta_kernel,
                "delta_sum",
                (*added, terms),
                [IN_VMEM] * len(added) + [IN_HBM],
                [pltpu.VMEM((heads, query_count), f32), rows_of],
                heads * query_count,
                out_specs=[IN_VMEM, IN_HBM],
                aliases={len(added): 1},
            )
            received = flip(terms, 1) if received is None else terms
        steps = min(4, value_devices // stride)
        added = [delta] + [flip(delta, stride * step) for step in range(1, steps)]
        if stride == 1:
            other_centre = added[1]
        stride *= steps
    half = query_count // (2 * chains)
    keep, delta, *send = call(
        partial(combine_kernel, deltas=len(added), scale=scale),
        "combine",
        (place, query_terms(True, "own_head"), received, centre, other_centre, *added),
        [IN_SMEM] + [IN_VMEM] * (4 + len(added)),
        [
            pltpu.VMEM((chains, half, width), f32),
            pltpu.VMEM((heads, query_count), f32),
        ]
        + [pltpu.VMEM((half, width), bf16)] * chains,
        work // 4,
    )
    key_own, pool_send = call(
        partial(key_kernel, chunk=chunk, scale=scale),
        "key_terms",
        (place, delta, probs, dprobs, targets, q_near, value_send),
        [IN_SMEM] + [IN_VMEM] * 6,
        [shares[0], pltpu.VMEM((parts - 1, share, 2 * wide), bf16)],
        2 * work,
        [pltpu.VMEM((heads, value_count, query_count), bf16)],
    )
    pool_received = swap_shares(pool_send)

    came = [flip(send[chain], 1 << order[0]) for chain, order in enumerate(orders)]
    kept, *sent = call(
        split_kernel,
        "split",
        (place, keep, *came, pool_send),
        [IN_SMEM] + [IN_VMEM] * (1 + chains) + [IN_HBM],
        [pltpu.VMEM((chains, half // 2, width), f32)]
        + [pltpu.VMEM((half // 2, width), bf16)] * chains,
        work // 8,
    )
    total = jnp.stack(
        [
            kept[chain] + flip(sent[chain], 1 << order[1]).astype(f32)
            for chain, order in enumerate(orders)
        ]
    )
    for bit in range(3, bits - 1):
        split = total.reshape(chains, 2, -1, width)
        pick = partial(lax.dynamic_index_in_dim, split, axis=1, keepdims=False)
        came = flip(pick(1 - bit_of(bit)).astype(bf16), 1 << bit)
        total = pick(bit_of(bit)) + came.astype(f32)
    total = total.astype(bf16)
    piece = total.shape[1]
    joined = call(
        join_kernel,
        "join",
        (total, flip(total, 1 << (bits - 1)), pool_received),
        [IN_VMEM] * 2 + [IN_HBM],
        [pltpu.VMEM((piece, width), bf16)] * chains,
        work // 16,
    )
    key_grad, value_grad = call(
        pool_kernel,
        "pool_sum",
        (key_own, value_own, pool_received),
        [IN_VMEM] * 3,
        [pltpu.HBM((share, wide), bf16)] * 2,
        work // 8,
    )
    first_half, second_half, own_piece = [], [], []
    for chain, order in enumerate(orders):
        part = joined[chain]
        for bit in list(range(bits - 2, 2, -1)) + [order[1]]:
            part = jnp.concatenate([part, flip(part, 1 << bit)], axis=0)
        first_half.append(part)
        second_half.append(flip(part, 1 << order[0]))
        index = 0
        for bit in order + list(range(3, bits - 1)):
            index = 2 * index + bit_of(bit)
        own_piece.append(index)
    pieces_place = jnp.stack([core] + own_piece).astype(jnp.int32)
    near = partial(pltpu.with_memory_space_constraint, memory_space=pltpu.VMEM)
    far = partial(pltpu.with_memory_space_constraint, memory_space=pltpu.HBM)

    def placed(name, sources, before, aliases):
        copied = len(sources)
        return call(
            partial(
                place_kernel,
                sources=[source[1:] for source in sources],
                pieces=pieces,
                piece=piece,
            ),
            name,
            (pieces_place, *[near(source[0]) for source in sources], far(before)),
            [IN_SMEM] + [IN_VMEM] * copied + [IN_HBM],
            [pltpu.HBM((query_count, wide), bf16)],
            work // 2,
            [pltpu.SemaphoreType.DMA((copied * pieces // 2,))],
            [IN_HBM],
            {1 + copied: 0} if aliases else {},
        )[0]

    def sources_of(first, second, side):
        rows = [(part, side, chain, 0) for chain, part in enumerate(first)]
        return rows + [(part, side, chain, pieces // 2) for chain, part in enumerate(second)]

    begun = placed("first_rows", sources_of(first_half, [], 0), key_grad, False)
    halves = call(
        after_kernel,
        "after",
        (*first_half, *second_half, far(begun)),
        [IN_HBM] * (2 * chains + 1),
        [pltpu.VMEM((half, width), bf16)] * (2 * chains),
        work // 1000,
        out_specs=[IN_HBM] * (2 * chains),
        aliases={index: index for index in range(2 * chains)},
    )
    theirs = [flip(part, 1) for part in halves]
    begun = placed("own_rows", sources_of([], halves[chains:], 0), begun, True)
    sources = sources_of(theirs[:chains], theirs[chains:], 1)
    return placed("other_rows", sources, begun, True), key_grad, value_grad


def solution(mesh):
    placed = (
        P("qry", None),
        P("val", None),
        P("val", None),
        P("qry", None),
        P(None, "qry"),
        P(None, "val", "qry"),
        P("qry", None),
    )
    return jax.shard_map(
        on_device,
        mesh=mesh,
        in_specs=placed,
        out_specs=(P("qry", None), P(("val", "qry"), None), P(("val", "qry"), None)),
        check_vma=False,
    )
```

```python
import math
from functools import partial

import jax
import jax.numpy as jnp
from jax import lax
from jax.experimental import pallas as pl
from jax.experimental.pallas import tpu as pltpu
from jax.sharding import PartitionSpec as P

LOG2E = math.log2(math.e)
MASKED = 1e30
NT = (((1,), (1,)), ((), ()))
NN = (((1,), (0,)), ((), ()))
PARAMS = pltpu.CompilerParams(vmem_limit_bytes=16 * 1024 * 1024)
IN_VMEM = pl.BlockSpec(memory_space=pltpu.VMEM)
IN_SMEM = pl.BlockSpec(memory_space=pltpu.SMEM)
IN_HBM = pl.BlockSpec(memory_space=pl.ANY)


def dot(a, b, dims):
    return lax.dot_general(a, b, dims, preferred_element_type=jnp.float32)


def ways(start, size):
    return pl.ds(pl.multiple_of(start, size), size)


def forward_kernel(
    place, compat_hbm, q_hbm, g_hbm, k_hbm, v_hbm, lse_hbm, targets_hbm,
    delta_ref, probs_ref, dprobs_ref, q_ref, g_ref, k_ref,
    v_ref, lse_ref, targets_ref, compat, sems, *, heads, blocks, scale,
):
    value_count, width = k_ref.shape[0], k_ref.shape[1] // heads
    block = q_ref.shape[0] // blocks
    pairs = [
        (compat_hbm, compat), (targets_hbm, targets_ref), (lse_hbm, lse_ref),
        (k_hbm, k_ref), (v_hbm, v_ref),
    ]
    small = len(pairs)
    for index in range(blocks):
        rows = pl.ds(index * block, block)
        pairs += [(q_hbm.at[rows], q_ref.at[rows]), (g_hbm.at[rows], g_ref.at[rows])]
    copies = [pltpu.make_async_copy(*pair, sems.at[n]) for n, pair in enumerate(pairs)]
    for copy in copies:
        copy.start()
    for copy in copies[:3]:
        copy.wait()
    local = targets_ref[...] - lax.axis_index("val") * value_count
    hit = jnp.where((local >= 0) & (local < value_count), 1.0, 0.0)
    lives = []
    for index in range(blocks):
        live = jnp.max(hit[:, index * block : (index + 1) * block]) > 0.0
        for head in range(heads):
            live = live | (compat[head, 0, index] == 1)
        lives.append(live)
    for copy in copies[3:small]:
        copy.wait()
    for index in range(blocks):
        rows = slice(index * block, (index + 1) * block)
        copies[small + 2 * index].wait()
        copies[small + 2 * index + 1].wait()
        live = lives[index]

        @pl.when(live)
        def _():
            for head in range(heads):
                columns = slice(head * width, (head + 1) * width)
                usable = (hit[head : head + 1, rows] > 0.0) | (compat[head, 0, index] == 1)
                lse_rows = jnp.where(usable, lse_ref[head : head + 1, rows], MASKED) * LOG2E
                scores = dot(k_ref[:, columns], q_ref[rows, columns], NT)
                dprobs = dot(v_ref[:, columns], g_ref[rows, columns], NT)
                probs = jnp.exp2(scores * (scale * LOG2E) - lse_rows)
                delta = jnp.sum(probs * dprobs, axis=0, keepdims=True)
                weight = jnp.sum(probs, axis=0, keepdims=True)
                delta_ref[head : head + 1, rows] = delta
                centre = delta / jnp.maximum(weight, 1e-30)
                delta_ref[heads + head : heads + head + 1, rows] = centre
                probs_ref[head, :, rows] = probs
                dprobs_ref[head, :, rows] = dprobs

        @pl.when(jnp.logical_not(live))
        def _():
            for head in range(heads):
                for row in (head, heads + head):
                    delta_ref[row : row + 1, rows] = jnp.zeros((1, block), jnp.float32)
                probs_ref[head, :, rows] = jnp.zeros((value_count, block), jnp.float32)
                dprobs_ref[head, :, rows] = jnp.zeros((value_count, block), jnp.float32)


def value_kernel(place, probs_ref, g_ref, after_ref, own_ref, send_ref):
    heads, _, _ = probs_ref.shape
    width = g_ref.shape[1] // heads
    share = own_ref.shape[0]
    parts = send_ref.shape[0] + 1
    for step in range(parts):
        rows = ways(lax.rem(place[1] + step, parts) * share, share)
        for head in range(heads):
            columns = slice(head * width, (head + 1) * width)
            term = dot(probs_ref[head, rows, :].astype(jnp.bfloat16), g_ref[:, columns], NN)
            if step == 0:
                own_ref[:, columns] = term
            else:
                send_ref[step - 1, :, columns] = term.astype(jnp.bfloat16)


def onehot_less(terms, place, targets_ref, head, rows):
    local = targets_ref[pl.ds(head, 1), rows] - place[0] * terms.shape[0]
    slots = lax.broadcasted_iota(jnp.int32, terms.shape, 0)
    return jnp.where(slots == local, terms - 1.0, terms)


def query_kernel(
    place, delta_ref, probs_ref, dprobs_ref, targets_ref, k_ref, out_ref, *, own, chunk
):
    head = place[2] if own else 1 - place[2]
    width = out_ref.shape[2]
    heads = probs_ref.shape[0]
    keys = jnp.transpose(k_ref[:, ways(head * width, width)])
    for start in range(0, out_ref.shape[1], chunk):
        rows = slice(start, start + chunk)
        probs = probs_ref[head, :, rows]
        gap = dprobs_ref[head, :, rows] - (delta_ref[pl.ds(heads + head, 1), rows] - 1.0)
        terms = onehot_less(probs * gap, place, targets_ref, head, rows)
        for index, factor in enumerate((terms, probs)):
            product = dot(keys, factor.astype(jnp.bfloat16), NN)
            out_ref[index, rows, :] = jnp.transpose(product)


def delta_kernel(*refs):
    *added, terms_ref, out_ref, same_terms_ref = refs
    heads = out_ref.shape[0]
    out_ref[...] = sum(ref[:heads] for ref in added)


def combine_kernel(
    place, own_ref, received_ref, centre_ref, came_ref, *rest, deltas, scale
):
    added, (keep_ref, sum_ref, *send_refs) = rest[:deltas], rest[deltas:]
    rows, width = keep_ref.shape
    heads = sum_ref.shape[0]
    sum_ref[...] = sum(ref[...] for ref in added)

    def column(ref, span):
        row = sum_ref[pl.ds(place[2], 1), span] - ref[pl.ds(heads + place[2], 1), span]
        return jnp.transpose(jnp.broadcast_to(row * scale, (128, rows)))

    for step in range(4):
        target = send_refs[step - 1] if step else keep_ref
        span = ways((place[3] ^ step) * rows, rows)
        gaps = column(centre_ref, span), column(came_ref, span)
        for start in range(0, width, 128):
            columns = slice(start, start + 128)
            direct = own_ref[0, span, columns] + received_ref[0, span, columns]
            weighted = own_ref[1, span, columns] * gaps[0]
            weighted += received_ref[1, span, columns] * gaps[1]
            target[:, columns] = (scale * direct - weighted).astype(target.dtype)


def key_kernel(
    place, delta_ref, probs_ref, dprobs_ref, targets_ref, q_ref, own_ref, send_ref,
    low_ref, *, chunk, scale,
):
    heads = probs_ref.shape[0]
    width = own_ref.shape[1] // heads
    share = own_ref.shape[0]
    parts = send_ref.shape[0] + 1
    for head in range(heads):
        columns = slice(head * width, (head + 1) * width)
        for start in range(0, q_ref.shape[0], chunk):
            rows = slice(start, start + chunk)
            gap = dprobs_ref[head, :, rows] - (delta_ref[head : head + 1, rows] - 1.0)
            terms = onehot_less(probs_ref[head, :, rows] * gap, place, targets_ref, head, rows)
            low_ref[head, :, rows] = terms.astype(jnp.bfloat16)
        for step in range(parts):
            rows = ways(lax.rem(place[1] + step, parts) * share, share)
            term = scale * dot(low_ref[head, rows, :], q_ref[:, columns], NN)
            if step == 0:
                own_ref[:, columns] = term
            else:
                send_ref[step - 1, :, columns] = term.astype(jnp.bfloat16)


def reduce_kernel(
    keep_ref, first_ref, second_ref, third_ref, after_value_ref, after_key_ref, out_ref
):
    total = keep_ref[...]
    for ref in (first_ref, second_ref, third_ref):
        total += ref[...].astype(jnp.float32)
    out_ref[...] = total.astype(out_ref.dtype)


def join_kernel(total_ref, came_ref, after_value_ref, after_key_ref, out_ref):
    total = total_ref[...].astype(jnp.float32) + came_ref[...].astype(jnp.float32)
    out_ref[...] = total.astype(jnp.bfloat16)


def pool_kernel(key_ref, value_ref, key_came_ref, value_came_ref, key_out, value_out):
    key_sum, value_sum = key_ref[...], value_ref[...]
    for step in range(key_came_ref.shape[0]):
        key_sum += key_came_ref[step].astype(jnp.float32)
        value_sum += value_came_ref[step].astype(jnp.float32)
    key_out[...] = key_sum.astype(jnp.bfloat16)
    value_out[...] = value_sum.astype(jnp.bfloat16)


def after_kernel(*refs):
    pass


def place_kernel(place, *rest, sources, piece):
    out_ref, sems = rest[-2:]
    copies = []
    for ref, (side, step) in zip(rest, sources):
        width = ref.shape[1]
        columns = ways((place[0] ^ side) * width, width)
        pieces = ref.shape[0] // piece
        for index in range(pieces):
            rows = ways(((place[1] ^ step) * pieces + (index ^ place[2])) * piece, piece)
            copies.append(
                pltpu.make_async_copy(
                    ref.at[pl.ds(index * piece, piece)], out_ref.at[rows, columns], sems.at[len(copies)]
                )
            )
            copies[-1].start()
    for copy in copies:
        copy.wait()


def call(kernel, name, inputs, in_specs, outputs, flops, scratch=(), out_specs=None, aliases={}):
    return pl.pallas_call(
        kernel,
        in_specs=in_specs,
        out_specs=[IN_VMEM] * len(outputs) if out_specs is None else out_specs,
        out_shape=outputs,
        scratch_shapes=list(scratch),
        input_output_aliases=aliases,
        cost_estimate=pl.CostEstimate(flops=flops, bytes_accessed=flops // 1000, transcendentals=0),
        compiler_params=PARAMS,
        name=name,
    )(*inputs)


def on_device(queries, pool_keys, pool_values, out_grad, lse, compat, targets):
    heads, value_blocks, blocks = compat.shape
    query_count, wide = queries.shape
    value_count = pool_keys.shape[0]
    width = wide // heads
    scale = width ** -0.5
    value_devices, parts = lax.axis_size("val"), lax.axis_size("qry")
    bits = value_devices.bit_length() - 1
    assert heads == 2 and value_blocks == 1 and value_devices == 1 << bits and bits >= 4
    val, qry = lax.axis_index("val"), lax.axis_index("qry")
    core = lax.rem(val, 2)
    share = value_count // parts
    f32, bf16 = jnp.float32, jnp.bfloat16

    def flip(array, mask):
        return lax.ppermute(array, "val", [(i, i ^ mask) for i in range(value_devices)])

    def swap_shares(send):
        return jnp.stack([
            lax.ppermute(send[step - 1], "qry", [(i, (i + step) % parts) for i in range(parts)])
            for step in range(1, parts)
        ])

    def add(own, received):
        for array in received:
            own = own + array.astype(f32)
        return own

    def bit_of(bit):
        return lax.rem(val // (1 << bit), 2)

    square = lax.rem(val // 2, 4)
    place = jnp.stack([val, qry, core, square]).astype(jnp.int32)
    work = 2 * query_count * value_count * width

    delta, probs, dprobs, q_near, g_near, k_near = call(
        partial(forward_kernel, heads=heads, blocks=blocks, scale=scale),
        "forward_pass",
        (place,)
        + tuple(
            pltpu.with_memory_space_constraint(array, pltpu.HBM)
            for array in (
                compat, queries, out_grad, pool_keys, pool_values, lse, jnp.transpose(targets)
            )
        ),
        [IN_HBM] * 8,
        [
            pltpu.VMEM((2 * heads, query_count), f32),
            pltpu.VMEM((heads, value_count, query_count), f32),
            pltpu.VMEM((heads, value_count, query_count), f32),
            pltpu.VMEM(queries.shape, bf16),
            pltpu.VMEM(queries.shape, bf16),
            pltpu.VMEM(pool_keys.shape, bf16),
        ],
        4 * work,
        [
            pltpu.VMEM(pool_values.shape, bf16),
            pltpu.VMEM((heads, query_count), f32),
            pltpu.VMEM((heads, query_count), jnp.int32),
            pltpu.SMEM(compat.shape, jnp.int32),
            pltpu.SemaphoreType.DMA((5 + 2 * blocks,)),
        ],
    )
    shares = [
        pltpu.VMEM((share, wide), f32),
        pltpu.VMEM((parts - 1, share, wide), bf16),
    ]
    chunk = query_count // 3 if query_count % 384 == 0 else query_count
    rows_of = pltpu.VMEM((2, query_count, width), f32)
    targets = jnp.transpose(targets)

    def query_terms(own, name):
        return call(
            partial(query_kernel, own=own, chunk=chunk),
            name,
            (place, centre, probs, dprobs, targets, k_near),
            [IN_SMEM] + [IN_VMEM] * 5,
            [rows_of],
            2 * work,
        )[0]

    centre = delta
    other = query_terms(False, "other_head")
    received = None
    stride = 1
    added = [delta]
    while stride < value_devices:
        if stride > 1:
            terms = other if received is None else received
            delta, terms = call(
                delta_kernel,
                "delta_sum",
                (*added, terms),
                [IN_VMEM] * len(added) + [IN_HBM],
                [pltpu.VMEM((heads, query_count), f32), rows_of],
                heads * query_count,
                out_specs=[IN_VMEM, IN_HBM],
                aliases={len(added): 1},
            )
            received = flip(terms, 1) if received is None else terms
        steps = min(4, value_devices // stride)
        added = [delta] + [flip(delta, stride * step) for step in range(1, steps)]
        if stride == 1:
            other_centre = added[1]
        stride *= steps
    quarter = query_count // 4
    near_part = pltpu.VMEM((quarter, width), bf16)
    keep, delta, *send = call(
        partial(combine_kernel, deltas=len(added), scale=scale),
        "combine",
        (place, query_terms(True, "own_head"), received, centre, other_centre, *added),
        [IN_SMEM] + [IN_VMEM] * (4 + len(added)),
        [
            pltpu.VMEM((quarter, width), f32),
            pltpu.VMEM((heads, query_count), f32),
        ]
        + [near_part] * 3,
        work // 4,
    )
    value_own, value_send = call(
        value_kernel,
        "value_terms",
        (place, probs, g_near, delta),
        [IN_SMEM] + [IN_VMEM] * 2 + [IN_HBM],
        shares,
        2 * work,
    )
    value_came = swap_shares(value_send)
    key_own, key_send = call(
        partial(key_kernel, chunk=chunk, scale=scale),
        "key_terms",
        (place, delta, probs, dprobs, targets, q_near),
        [IN_SMEM] + [IN_VMEM] * 5,
        shares,
        2 * work,
        [pltpu.VMEM((heads, value_count, query_count), bf16)],
    )
    key_came = swap_shares(key_send)

    came = [flip(send[step - 1], 2 * step) for step in range(1, 4)]
    (total,) = call(
        reduce_kernel,
        "reduce",
        (keep, *came, value_send, key_send),
        [IN_VMEM] * 4 + [IN_HBM] * 2,
        [near_part if bits == 4 else pltpu.VMEM((quarter, width), f32)],
        work // 8,
    )
    for bit in range(3, bits - 1):
        split = total.reshape(2, -1, width)
        pick = partial(lax.dynamic_index_in_dim, split, axis=0, keepdims=False)
        came = flip(pick(1 - bit_of(bit)).astype(bf16), 1 << bit)
        total = pick(bit_of(bit)) + came.astype(f32)
    total = total.astype(bf16)
    piece = total.shape[0]
    (part,) = call(
        join_kernel,
        "join",
        (total, flip(total, 1 << (bits - 1)), value_came, key_came),
        [IN_VMEM] * 2 + [IN_HBM] * 2,
        [pltpu.VMEM((piece, width), bf16)],
        work // 16,
    )
    inner = 0
    for bit in range(bits - 2, 2, -1):
        part = jnp.concatenate([part, flip(part, 1 << bit)], axis=0)
    for bit in range(3, bits - 1):
        inner = 2 * inner + bit_of(bit)

    key_grad, value_grad = call(
        pool_kernel,
        "pool_sum",
        (key_own, value_own, key_came, value_came),
        [IN_VMEM] * 4,
        [pltpu.HBM((share, wide), bf16)] * 2,
        work // 8,
    )
    others = [flip(part, 2 * step) for step in range(1, 4)]
    pieces_place = jnp.stack([core, square, inner]).astype(jnp.int32)
    near = partial(pltpu.with_memory_space_constraint, memory_space=pltpu.VMEM)
    far = partial(pltpu.with_memory_space_constraint, memory_space=pltpu.HBM)

    def placed(name, sources, before, aliases):
        copied = len(sources)
        return call(
            partial(place_kernel, sources=[source[1:] for source in sources], piece=piece),
            name,
            (pieces_place, *[near(source[0]) for source in sources], far(before)),
            [IN_SMEM] + [IN_VMEM] * copied + [IN_HBM],
            [pltpu.HBM((query_count, wide), bf16)],
            work // 2,
            [pltpu.SemaphoreType.DMA((copied * quarter // piece,))],
            [IN_HBM],
            {1 + copied: 0} if aliases else {},
        )[0]

    begun = placed("first_rows", [(part, 0, 0)], key_grad, False)
    part, first_other = call(
        after_kernel,
        "after",
        (part, others[0], far(begun)),
        [IN_HBM] * 3,
        [near_part] * 2,
        work // 1000,
        out_specs=[IN_HBM] * 2,
        aliases={0: 0, 1: 1},
    )
    quarters = [part, first_other] + others[1:]
    theirs = [(flip(array, 1), 1, step) for step, array in enumerate(quarters)]
    mine = [(array, 0, step) for step, array in enumerate(quarters) if step]
    begun = placed("own_rows", mine, begun, True)
    return placed("other_rows", theirs, begun, True), key_grad, value_grad


def solution(mesh):
    placed = (
        P("qry", None),
        P("val", None),
        P("val", None),
        P("qry", None),
        P(None, "qry"),
        P(None, "val", "qry"),
        P("qry", None),
    )
    return jax.shard_map(
        on_device,
        mesh=mesh,
        in_specs=placed,
        out_specs=(P("qry", None), P(("val", "qry"), None), P(("val", "qry"), None)),
        check_vma=False,
    )
```

```python
import math
from functools import partial

import jax
import jax.numpy as jnp
from jax import lax
from jax.experimental import pallas as pl
from jax.experimental.pallas import tpu as pltpu
from jax.sharding import PartitionSpec as P

LOG2E = math.log2(math.e)
MASKED = 1e30
NT = (((1,), (1,)), ((), ()))
NN = (((1,), (0,)), ((), ()))
PARAMS = pltpu.CompilerParams(vmem_limit_bytes=16 * 1024 * 1024)
IN_VMEM = pl.BlockSpec(memory_space=pltpu.VMEM)
IN_SMEM = pl.BlockSpec(memory_space=pltpu.SMEM)
IN_HBM = pl.BlockSpec(memory_space=pl.ANY)


def dot(a, b, dims):
    return lax.dot_general(a, b, dims, preferred_element_type=jnp.float32)


def ways(start, size):
    return pl.ds(pl.multiple_of(start, size), size)


def forward_kernel(
    place, compat_hbm, q_hbm, g_hbm, k_hbm, v_hbm, lse_hbm, targets_hbm,
    delta_ref, probs_ref, dprobs_ref, q_ref, g_ref, k_ref,
    v_ref, lse_ref, targets_ref, compat, sems, *, heads, blocks, scale,
):
    value_count, width = k_ref.shape[0], k_ref.shape[1] // heads
    block = q_ref.shape[0] // blocks
    pairs = [
        (compat_hbm, compat), (targets_hbm, targets_ref), (lse_hbm, lse_ref),
        (k_hbm, k_ref), (v_hbm, v_ref),
    ]
    small = len(pairs)
    for index in range(blocks):
        rows = pl.ds(index * block, block)
        pairs += [(q_hbm.at[rows], q_ref.at[rows]), (g_hbm.at[rows], g_ref.at[rows])]
    copies = [pltpu.make_async_copy(*pair, sems.at[n]) for n, pair in enumerate(pairs)]
    for copy in copies:
        copy.start()
    for copy in copies[:3]:
        copy.wait()
    local = targets_ref[...] - lax.axis_index("val") * value_count
    hit = jnp.where((local >= 0) & (local < value_count), 1.0, 0.0)
    lives = []
    for index in range(blocks):
        live = jnp.max(hit[:, index * block : (index + 1) * block]) > 0.0
        for head in range(heads):
            live = live | (compat[head, 0, index] == 1)
        lives.append(live)
    for copy in copies[3:small]:
        copy.wait()
    for index in range(blocks):
        rows = slice(index * block, (index + 1) * block)
        copies[small + 2 * index].wait()
        copies[small + 2 * index + 1].wait()
        live = lives[index]

        @pl.when(live)
        def _():
            for head in range(heads):
                columns = slice(head * width, (head + 1) * width)
                usable = (hit[head : head + 1, rows] > 0.0) | (compat[head, 0, index] == 1)
                lse_rows = jnp.where(usable, lse_ref[head : head + 1, rows], MASKED) * LOG2E
                scores = dot(k_ref[:, columns], q_ref[rows, columns], NT)
                dprobs = dot(v_ref[:, columns], g_ref[rows, columns], NT)
                probs = jnp.exp2(scores * (scale * LOG2E) - lse_rows)
                delta = jnp.sum(probs * dprobs, axis=0, keepdims=True)
                weight = jnp.sum(probs, axis=0, keepdims=True)
                delta_ref[head : head + 1, rows] = delta
                centre = delta / jnp.maximum(weight, 1e-30)
                delta_ref[heads + head : heads + head + 1, rows] = centre
                probs_ref[head, :, rows] = probs
                dprobs_ref[head, :, rows] = dprobs

        @pl.when(jnp.logical_not(live))
        def _():
            for head in range(heads):
                for row in (head, heads + head):
                    delta_ref[row : row + 1, rows] = jnp.zeros((1, block), jnp.float32)
                probs_ref[head, :, rows] = jnp.zeros((value_count, block), jnp.float32)
                dprobs_ref[head, :, rows] = jnp.zeros((value_count, block), jnp.float32)


def value_kernel(place, probs_ref, g_ref, after_ref, own_ref, send_ref):
    heads, _, _ = probs_ref.shape
    width = g_ref.shape[1] // heads
    share = own_ref.shape[0]
    parts = send_ref.shape[0] + 1
    for step in range(parts):
        rows = ways(lax.rem(place[1] + step, parts) * share, share)
        for head in range(heads):
            columns = slice(head * width, (head + 1) * width)
            term = dot(probs_ref[head, rows, :].astype(jnp.bfloat16), g_ref[:, columns], NN)
            if step == 0:
                own_ref[:, columns] = term
            else:
                send_ref[step - 1, :, columns] = term.astype(jnp.bfloat16)


def onehot_less(terms, place, targets_ref, head, rows):
    local = targets_ref[pl.ds(head, 1), rows] - place[0] * terms.shape[0]
    slots = lax.broadcasted_iota(jnp.int32, terms.shape, 0)
    return jnp.where(slots == local, terms - 1.0, terms)


def query_kernel(
    place, delta_ref, probs_ref, dprobs_ref, targets_ref, k_ref, out_ref, *, own, chunk
):
    head = place[2] if own else 1 - place[2]
    width = out_ref.shape[2]
    heads = probs_ref.shape[0]
    keys = jnp.transpose(k_ref[:, ways(head * width, width)])
    for start in range(0, out_ref.shape[1], chunk):
        rows = slice(start, start + chunk)
        probs = probs_ref[head, :, rows]
        gap = dprobs_ref[head, :, rows] - (delta_ref[pl.ds(heads + head, 1), rows] - 1.0)
        terms = onehot_less(probs * gap, place, targets_ref, head, rows)
        for index, factor in enumerate((terms, probs)):
            product = dot(keys, factor.astype(jnp.bfloat16), NN)
            out_ref[index, rows, :] = jnp.transpose(product)


def delta_kernel(*refs):
    *added, terms_ref, out_ref, same_terms_ref = refs
    heads = out_ref.shape[0]
    out_ref[...] = sum(ref[:heads] for ref in added)


def combine_kernel(
    place, own_ref, received_ref, centre_ref, came_ref, *rest, deltas, scale
):
    added, (keep_ref, sum_ref, *send_refs) = rest[:deltas], rest[deltas:]
    _, rows, width = keep_ref.shape
    heads = sum_ref.shape[0]
    sum_ref[...] = sum(ref[...] for ref in added)

    def column(ref, span):
        row = sum_ref[pl.ds(place[2], 1), span] - ref[pl.ds(heads + place[2], 1), span]
        return jnp.transpose(jnp.broadcast_to(row * scale, (128, 2 * rows)))

    for step in (3, 1, 2, 0):
        span = ways((place[3] ^ step) * 2 * rows, 2 * rows)
        own_gap, came_gap = column(centre_ref, span), column(came_ref, span)
        for part in range(2):
            target = send_refs[3 * part + step - 1] if step else keep_ref.at[part]
            span = ways((2 * (place[3] ^ step) + part) * rows, rows)
            inside = slice(part * rows, (part + 1) * rows)
            for start in range(0, width, 128):
                columns = slice(start, start + 128)
                direct = own_ref[0, span, columns] + received_ref[0, span, columns]
                weighted = own_ref[1, span, columns] * own_gap[inside]
                weighted += received_ref[1, span, columns] * came_gap[inside]
                target[:, columns] = (scale * direct - weighted).astype(target.dtype)


def key_kernel(
    place, delta_ref, probs_ref, dprobs_ref, targets_ref, q_ref, after_ref, own_ref, send_ref,
    low_ref, *, chunk, scale,
):
    heads = probs_ref.shape[0]
    width = own_ref.shape[1] // heads
    share = own_ref.shape[0]
    parts = send_ref.shape[0] + 1
    for head in range(heads):
        columns = slice(head * width, (head + 1) * width)
        for start in range(0, q_ref.shape[0], chunk):
            rows = slice(start, start + chunk)
            gap = dprobs_ref[head, :, rows] - (delta_ref[head : head + 1, rows] - 1.0)
            terms = onehot_less(probs_ref[head, :, rows] * gap, place, targets_ref, head, rows)
            low_ref[head, :, rows] = terms.astype(jnp.bfloat16)
        for step in range(parts):
            rows = ways(lax.rem(place[1] + step, parts) * share, share)
            term = scale * dot(low_ref[head, rows, :], q_ref[:, columns], NN)
            if step == 0:
                own_ref[:, columns] = term
            else:
                send_ref[step - 1, :, columns] = term.astype(jnp.bfloat16)


def reduce_kernel(keep_ref, first_ref, second_ref, third_ref, *rest, part):
    total = keep_ref[part]
    for ref in (first_ref, second_ref, third_ref):
        total += ref[...].astype(jnp.float32)
    rest[-1][...] = total.astype(rest[-1].dtype)


def join_kernel(total_ref, came_ref, out_ref):
    total = total_ref[...].astype(jnp.float32) + came_ref[...].astype(jnp.float32)
    out_ref[...] = total.astype(jnp.bfloat16)


def gather_kernel(*refs):
    out_ref = refs[-1]
    rows = refs[0].shape[0]
    for ref, step in zip(refs, (0, 3, 1, 2)):
        out_ref[step * rows : (step + 1) * rows] = ref[...]


def pool_kernel(key_ref, value_ref, key_came_ref, value_came_ref, key_out, value_out):
    key_sum, value_sum = key_ref[...], value_ref[...]
    for step in range(key_came_ref.shape[0]):
        key_sum += key_came_ref[step].astype(jnp.float32)
        value_sum += value_came_ref[step].astype(jnp.float32)
    key_out[...] = key_sum.astype(jnp.bfloat16)
    value_out[...] = value_sum.astype(jnp.bfloat16)


def place_kernel(place, *rest, sources, piece):
    out_ref, sems = rest[-2:]
    copies = []
    for ref, (side, part) in zip(rest, sources):
        width = ref.shape[1]
        columns = ways((place[0] ^ side) * width, width)
        pieces = ref.shape[0] // (4 * piece)
        for index in range(4 * pieces):
            step, inner = divmod(index, pieces)
            block = (2 * (place[1] ^ step) + part) * pieces + (inner ^ place[2])
            copies.append(
                pltpu.make_async_copy(
                    ref.at[pl.ds(index * piece, piece)],
                    out_ref.at[ways(block * piece, piece), columns],
                    sems.at[len(copies)],
                )
            )
            copies[-1].start()
    for copy in copies:
        copy.wait()


def call(kernel, name, inputs, in_specs, outputs, flops, scratch=(), out_specs=None, aliases={}):
    return pl.pallas_call(
        kernel,
        in_specs=in_specs,
        out_specs=[IN_VMEM] * len(outputs) if out_specs is None else out_specs,
        out_shape=outputs,
        scratch_shapes=list(scratch),
        input_output_aliases=aliases,
        cost_estimate=pl.CostEstimate(flops=flops, bytes_accessed=flops // 1000, transcendentals=0),
        compiler_params=PARAMS,
        name=name,
    )(*inputs)


def on_device(queries, pool_keys, pool_values, out_grad, lse, compat, targets):
    heads, value_blocks, blocks = compat.shape
    query_count, wide = queries.shape
    value_count = pool_keys.shape[0]
    width = wide // heads
    scale = width ** -0.5
    value_devices, parts = lax.axis_size("val"), lax.axis_size("qry")
    bits = value_devices.bit_length() - 1
    assert heads == 2 and value_blocks == 1 and value_devices == 1 << bits and bits >= 4
    val, qry = lax.axis_index("val"), lax.axis_index("qry")
    core = lax.rem(val, 2)
    share = value_count // parts
    f32, bf16 = jnp.float32, jnp.bfloat16

    def flip(array, mask):
        return lax.ppermute(array, "val", [(i, i ^ mask) for i in range(value_devices)])

    def swap_shares(send):
        return jnp.stack([
            lax.ppermute(send[step - 1], "qry", [(i, (i + step) % parts) for i in range(parts)])
            for step in range(1, parts)
        ])

    def add(own, received):
        for array in received:
            own = own + array.astype(f32)
        return own

    def bit_of(bit):
        return lax.rem(val // (1 << bit), 2)

    square = lax.rem(val // 2, 4)
    place = jnp.stack([val, qry, core, square]).astype(jnp.int32)
    work = 2 * query_count * value_count * width

    delta, probs, dprobs, q_near, g_near, k_near = call(
        partial(forward_kernel, heads=heads, blocks=blocks, scale=scale),
        "forward_pass",
        (place,)
        + tuple(
            pltpu.with_memory_space_constraint(array, pltpu.HBM)
            for array in (
                compat, queries, out_grad, pool_keys, pool_values, lse, jnp.transpose(targets)
            )
        ),
        [IN_HBM] * 8,
        [
            pltpu.VMEM((2 * heads, query_count), f32),
            pltpu.VMEM((heads, value_count, query_count), f32),
            pltpu.VMEM((heads, value_count, query_count), f32),
            pltpu.VMEM(queries.shape, bf16),
            pltpu.VMEM(queries.shape, bf16),
            pltpu.VMEM(pool_keys.shape, bf16),
        ],
        4 * work,
        [
            pltpu.VMEM(pool_values.shape, bf16),
            pltpu.VMEM((heads, query_count), f32),
            pltpu.VMEM((heads, query_count), jnp.int32),
            pltpu.SMEM(compat.shape, jnp.int32),
            pltpu.SemaphoreType.DMA((5 + 2 * blocks,)),
        ],
    )
    shares = [
        pltpu.VMEM((share, wide), f32),
        pltpu.VMEM((parts - 1, share, wide), bf16),
    ]
    chunk = query_count // 3 if query_count % 384 == 0 else query_count
    rows_of = pltpu.VMEM((2, query_count, width), f32)
    targets = jnp.transpose(targets)

    def query_terms(own, name):
        return call(
            partial(query_kernel, own=own, chunk=chunk),
            name,
            (place, centre, probs, dprobs, targets, k_near),
            [IN_SMEM] + [IN_VMEM] * 5,
            [rows_of],
            2 * work,
        )[0]

    centre = delta
    other = query_terms(False, "other_head")
    received = None
    stride = 1
    added = [delta]
    while stride < value_devices:
        if stride > 1:
            terms = other if received is None else received
            delta, terms = call(
                delta_kernel,
                "delta_sum",
                (*added, terms),
                [IN_VMEM] * len(added) + [IN_HBM],
                [pltpu.VMEM((heads, query_count), f32), rows_of],
                heads * query_count,
                out_specs=[IN_VMEM, IN_HBM],
                aliases={len(added): 1},
            )
            received = flip(terms, 1) if received is None else terms
        steps = min(4, value_devices // stride)
        added = [delta] + [flip(delta, stride * step) for step in range(1, steps)]
        if stride == 1:
            other_centre = added[1]
        stride *= steps
    eighth = query_count // 8
    near_part = pltpu.VMEM((eighth, width), bf16)
    keep, delta, *send = call(
        partial(combine_kernel, deltas=len(added), scale=scale),
        "combine",
        (place, query_terms(True, "own_head"), received, centre, other_centre, *added),
        [IN_SMEM] + [IN_VMEM] * (4 + len(added)),
        [
            pltpu.VMEM((2, eighth, width), f32),
            pltpu.VMEM((heads, query_count), f32),
        ]
        + [near_part] * 6,
        work // 4,
    )
    def reduced(part, after):
        came = {step: flip(send[3 * part + step - 1], 2 * step) for step in (3, 1, 2)}
        return call(
            partial(reduce_kernel, part=part),
            "reduce",
            (keep, came[3], came[1], came[2], *after),
            [IN_VMEM] * 4 + [IN_HBM] * len(after),
            [near_part if bits == 4 else pltpu.VMEM((eighth, width), f32)],
            work // 16,
        )[0]

    def joined(total):
        for bit in range(3, bits - 1):
            split = total.reshape(2, -1, width)
            pick = partial(lax.dynamic_index_in_dim, split, axis=0, keepdims=False)
            came = flip(pick(1 - bit_of(bit)).astype(bf16), 1 << bit)
            total = pick(bit_of(bit)) + came.astype(f32)
        total = total.astype(bf16)
        (whole,) = call(
            join_kernel,
            "join",
            (total, flip(total, 1 << (bits - 1))),
            [IN_VMEM] * 2,
            [pltpu.VMEM(total.shape, bf16)],
            work // 16,
        )
        for bit in range(bits - 2, 2, -1):
            whole = jnp.concatenate([whole, flip(whole, 1 << bit)], axis=0)
        return whole

    totals = [reduced(0, ())]
    value_own, value_send = call(
        value_kernel,
        "value_terms",
        (place, probs, g_near, totals[0]),
        [IN_SMEM] + [IN_VMEM] * 2 + [IN_HBM],
        shares,
        2 * work,
    )
    value_came = swap_shares(value_send)
    key_own, key_send = call(
        partial(key_kernel, chunk=chunk, scale=scale),
        "key_terms",
        (place, delta, probs, dprobs, targets, q_near, totals[0]),
        [IN_SMEM] + [IN_VMEM] * 5 + [IN_HBM],
        shares,
        2 * work,
        [pltpu.VMEM((heads, value_count, query_count), bf16)],
    )
    key_came = swap_shares(key_send)

    totals.append(reduced(1, (value_send, key_send)))
    piece = eighth >> (bits - 4)
    inner = 0
    for bit in range(3, bits - 1):
        inner = 2 * inner + bit_of(bit)

    key_grad, value_grad = call(
        pool_kernel,
        "pool_sum",
        (key_own, value_own, key_came, value_came),
        [IN_VMEM] * 4,
        [pltpu.HBM((share, wide), bf16)] * 2,
        work // 8,
    )
    pieces_place = jnp.stack([core, square, inner]).astype(jnp.int32)

    def gathered(total, after):
        whole = joined(total)
        others = {step: flip(whole, 2 * step) for step in (3, 1, 2)}
        return call(
            gather_kernel,
            "gather",
            (whole, others[3], others[1], others[2], *after),
            [IN_VMEM] * 4 + [IN_HBM] * len(after),
            [pltpu.VMEM((4 * eighth, width), bf16)],
            work // 16,
        )[0]

    near = partial(pltpu.with_memory_space_constraint, memory_space=pltpu.VMEM)
    far = partial(pltpu.with_memory_space_constraint, memory_space=pltpu.HBM)

    def placed(name, sources, before, aliases):
        copied = len(sources)
        return call(
            partial(place_kernel, sources=[source[1:] for source in sources], piece=piece),
            name,
            (pieces_place, *[near(source[0]) for source in sources], far(before)),
            [IN_SMEM] + [IN_VMEM] * copied + [IN_HBM],
            [pltpu.HBM((query_count, wide), bf16)],
            work // 2,
            [pltpu.SemaphoreType.DMA((copied * 4 * eighth // piece,))],
            [IN_HBM],
            {1 + copied: 0} if aliases else {},
        )[0]

    mine = [gathered(totals[0], ())]
    begun = placed("first_rows", [(mine[0], 0, 0)], key_grad, False)
    mine.append(gathered(totals[1], (far(begun),)))
    theirs = [flip(array, 1) for array in mine]
    begun = placed("own_rows", [(mine[1], 0, 1), (theirs[0], 1, 0)], begun, True)
    return placed("other_rows", [(theirs[1], 1, 1)], begun, True), key_grad, value_grad


def solution(mesh):
    placed = (
        P("qry", None),
        P("val", None),
        P("val", None),
        P("qry", None),
        P(None, "qry"),
        P(None, "val", "qry"),
        P("qry", None),
    )
    return jax.shard_map(
        on_device,
        mesh=mesh,
        in_specs=placed,
        out_specs=(P("qry", None), P(("val", "qry"), None), P(("val", "qry"), None)),
        check_vma=False,
    )
```

```python
import math
from functools import partial

import jax
import jax.numpy as jnp
from jax import lax
from jax.experimental import pallas as pl
from jax.experimental.pallas import tpu as pltpu
from jax.sharding import PartitionSpec as P

LOG2E = math.log2(math.e)
MASKED = 1e30
NT = (((1,), (1,)), ((), ()))
NN = (((1,), (0,)), ((), ()))
PARAMS = pltpu.CompilerParams(vmem_limit_bytes=16 * 1024 * 1024)
IN_VMEM = pl.BlockSpec(memory_space=pltpu.VMEM)
IN_SMEM = pl.BlockSpec(memory_space=pltpu.SMEM)
IN_HBM = pl.BlockSpec(memory_space=pl.ANY)


def dot(a, b, dims):
    return lax.dot_general(a, b, dims, preferred_element_type=jnp.float32)


def ways(start, size):
    return pl.ds(pl.multiple_of(start, size), size)


def forward_kernel(
    place, compat_hbm, q_hbm, g_hbm, k_hbm, v_hbm, lse_hbm, targets_hbm,
    delta_ref, probs_ref, dprobs_ref, q_ref, g_ref, k_ref,
    v_ref, lse_ref, targets_ref, compat, sems, *, heads, blocks, scale,
):
    value_count, width = k_ref.shape[0], k_ref.shape[1] // heads
    block = q_ref.shape[0] // blocks
    pairs = [
        (compat_hbm, compat), (targets_hbm, targets_ref), (lse_hbm, lse_ref),
        (k_hbm, k_ref), (v_hbm, v_ref),
    ]
    small = len(pairs)
    for index in range(blocks):
        rows = pl.ds(index * block, block)
        pairs += [(q_hbm.at[rows], q_ref.at[rows]), (g_hbm.at[rows], g_ref.at[rows])]
    copies = [pltpu.make_async_copy(*pair, sems.at[n]) for n, pair in enumerate(pairs)]
    for copy in copies:
        copy.start()
    for copy in copies[:3]:
        copy.wait()
    local = targets_ref[...] - lax.axis_index("val") * value_count
    hit = jnp.where((local >= 0) & (local < value_count), 1.0, 0.0)
    lives = []
    for index in range(blocks):
        live = jnp.max(hit[:, index * block : (index + 1) * block]) > 0.0
        for head in range(heads):
            live = live | (compat[head, 0, index] == 1)
        lives.append(live)
    for copy in copies[3:small]:
        copy.wait()
    for index in range(blocks):
        rows = slice(index * block, (index + 1) * block)
        copies[small + 2 * index].wait()
        copies[small + 2 * index + 1].wait()
        live = lives[index]

        @pl.when(live)
        def _():
            for head in range(heads):
                columns = slice(head * width, (head + 1) * width)
                usable = (hit[head : head + 1, rows] > 0.0) | (compat[head, 0, index] == 1)
                lse_rows = jnp.where(usable, lse_ref[head : head + 1, rows], MASKED) * LOG2E
                scores = dot(k_ref[:, columns], q_ref[rows, columns], NT)
                dprobs = dot(v_ref[:, columns], g_ref[rows, columns], NT)
                probs = jnp.exp2(scores * (scale * LOG2E) - lse_rows)
                delta = jnp.sum(probs * dprobs, axis=0, keepdims=True)
                weight = jnp.sum(probs, axis=0, keepdims=True)
                delta_ref[head : head + 1, rows] = delta
                centre = delta / jnp.maximum(weight, 1e-30)
                delta_ref[heads + head : heads + head + 1, rows] = centre
                probs_ref[head, :, rows] = probs
                dprobs_ref[head, :, rows] = dprobs

        @pl.when(jnp.logical_not(live))
        def _():
            for head in range(heads):
                for row in (head, heads + head):
                    delta_ref[row : row + 1, rows] = jnp.zeros((1, block), jnp.float32)
                probs_ref[head, :, rows] = jnp.zeros((value_count, block), jnp.float32)
                dprobs_ref[head, :, rows] = jnp.zeros((value_count, block), jnp.float32)


def value_kernel(place, probs_ref, g_ref, after_ref, own_ref, send_ref):
    heads, _, _ = probs_ref.shape
    width = g_ref.shape[1] // heads
    share = own_ref.shape[0]
    parts = send_ref.shape[0] + 1
    for step in range(parts):
        rows = ways(lax.rem(place[1] + step, parts) * share, share)
        for head in range(heads):
            columns = slice(head * width, (head + 1) * width)
            term = dot(probs_ref[head, rows, :].astype(jnp.bfloat16), g_ref[:, columns], NN)
            if step == 0:
                own_ref[:, columns] = term
            else:
                send_ref[step - 1, :, columns] = term.astype(jnp.bfloat16)


def onehot_less(terms, place, targets_ref, head, rows):
    local = targets_ref[pl.ds(head, 1), rows] - place[0] * terms.shape[0]
    slots = lax.broadcasted_iota(jnp.int32, terms.shape, 0)
    return jnp.where(slots == local, terms - 1.0, terms)


def query_kernel(
    place, delta_ref, probs_ref, dprobs_ref, targets_ref, k_ref, out_ref, *, own, chunk
):
    head = place[2] if own else 1 - place[2]
    width = out_ref.shape[2]
    heads = probs_ref.shape[0]
    keys = jnp.transpose(k_ref[:, ways(head * width, width)])
    for start in range(0, out_ref.shape[1], chunk):
        rows = slice(start, start + chunk)
        probs = probs_ref[head, :, rows]
        gap = dprobs_ref[head, :, rows] - (delta_ref[pl.ds(heads + head, 1), rows] - 1.0)
        terms = onehot_less(probs * gap, place, targets_ref, head, rows)
        for index, factor in enumerate((terms, probs)):
            product = dot(keys, factor.astype(jnp.bfloat16), NN)
            out_ref[index, rows, :] = jnp.transpose(product)


def delta_kernel(*refs):
    *added, terms_ref, out_ref, same_terms_ref = refs
    heads = out_ref.shape[0]
    out_ref[...] = sum(ref[:heads] for ref in added)


def combine_kernel(
    place, own_ref, received_ref, centre_ref, came_ref, *rest, deltas, scale
):
    added, (keep_ref, sum_ref, *send_refs) = rest[:deltas], rest[deltas:]
    rows, width = keep_ref.shape
    heads = sum_ref.shape[0]
    sum_ref[...] = sum(ref[...] for ref in added)

    def column(ref, span):
        row = sum_ref[pl.ds(place[2], 1), span] - ref[pl.ds(heads + place[2], 1), span]
        return jnp.transpose(jnp.broadcast_to(row * scale, (128, rows)))

    for step in (3, 1, 2, 0):
        target = send_refs[step - 1] if step else keep_ref
        span = ways((place[3] ^ step) * rows, rows)
        own_gap, came_gap = column(centre_ref, span), column(came_ref, span)
        for start in range(0, width, 128):
            columns = slice(start, start + 128)
            direct = own_ref[0, span, columns] + received_ref[0, span, columns]
            weighted = own_ref[1, span, columns] * own_gap
            weighted += received_ref[1, span, columns] * came_gap
            target[:, columns] = (scale * direct - weighted).astype(target.dtype)


def key_kernel(
    place, delta_ref, probs_ref, dprobs_ref, targets_ref, q_ref, own_ref, send_ref,
    low_ref, *, chunk, scale,
):
    heads = probs_ref.shape[0]
    width = own_ref.shape[1] // heads
    share = own_ref.shape[0]
    parts = send_ref.shape[0] + 1
    for head in range(heads):
        columns = slice(head * width, (head + 1) * width)
        for start in range(0, q_ref.shape[0], chunk):
            rows = slice(start, start + chunk)
            gap = dprobs_ref[head, :, rows] - (delta_ref[head : head + 1, rows] - 1.0)
            terms = onehot_less(probs_ref[head, :, rows] * gap, place, targets_ref, head, rows)
            low_ref[head, :, rows] = terms.astype(jnp.bfloat16)
        for step in range(parts):
            rows = ways(lax.rem(place[1] + step, parts) * share, share)
            term = scale * dot(low_ref[head, rows, :], q_ref[:, columns], NN)
            if step == 0:
                own_ref[:, columns] = term
            else:
                send_ref[step - 1, :, columns] = term.astype(jnp.bfloat16)


def reduce_kernel(keep_ref, first_ref, second_ref, third_ref, after_value, after_key, *out_refs):
    rows = out_refs[0].shape[0]
    for part, out_ref in enumerate(out_refs):
        span = slice(part * rows, (part + 1) * rows)
        total = keep_ref[span]
        for ref in (first_ref, second_ref, third_ref):
            total += ref[span].astype(jnp.float32)
        out_ref[...] = total.astype(out_ref.dtype)


def join_kernel(total_ref, came_ref, out_ref):
    total = total_ref[...].astype(jnp.float32) + came_ref[...].astype(jnp.float32)
    out_ref[...] = total.astype(jnp.bfloat16)


def gather_kernel(*refs):
    out_ref = refs[-1]
    rows = refs[0].shape[0]
    for ref, step in zip(refs, (0, 3, 1, 2)):
        out_ref[step * rows : (step + 1) * rows] = ref[...]


def pool_kernel(key_ref, value_ref, key_came_ref, value_came_ref, key_out, value_out):
    key_sum, value_sum = key_ref[...], value_ref[...]
    for step in range(key_came_ref.shape[0]):
        key_sum += key_came_ref[step].astype(jnp.float32)
        value_sum += value_came_ref[step].astype(jnp.float32)
    key_out[...] = key_sum.astype(jnp.bfloat16)
    value_out[...] = value_sum.astype(jnp.bfloat16)


def place_kernel(place, *rest, sources, piece):
    out_ref, sems = rest[-2:]
    copies = []
    for ref, (side, part) in zip(rest, sources):
        width = ref.shape[1]
        columns = ways((place[0] ^ side) * width, width)
        pieces = ref.shape[0] // (4 * piece)
        for index in range(4 * pieces):
            step, inner = divmod(index, pieces)
            block = (2 * (place[1] ^ step) + part) * pieces + (inner ^ place[2])
            copies.append(
                pltpu.make_async_copy(
                    ref.at[pl.ds(index * piece, piece)],
                    out_ref.at[ways(block * piece, piece), columns],
                    sems.at[len(copies)],
                )
            )
            copies[-1].start()
    for copy in copies:
        copy.wait()


def call(kernel, name, inputs, in_specs, outputs, flops, scratch=(), out_specs=None, aliases={}):
    return pl.pallas_call(
        kernel,
        in_specs=in_specs,
        out_specs=[IN_VMEM] * len(outputs) if out_specs is None else out_specs,
        out_shape=outputs,
        scratch_shapes=list(scratch),
        input_output_aliases=aliases,
        cost_estimate=pl.CostEstimate(flops=flops, bytes_accessed=flops // 1000, transcendentals=0),
        compiler_params=PARAMS,
        name=name,
    )(*inputs)


def on_device(queries, pool_keys, pool_values, out_grad, lse, compat, targets):
    heads, value_blocks, blocks = compat.shape
    query_count, wide = queries.shape
    value_count = pool_keys.shape[0]
    width = wide // heads
    scale = width ** -0.5
    value_devices, parts = lax.axis_size("val"), lax.axis_size("qry")
    bits = value_devices.bit_length() - 1
    assert heads == 2 and value_blocks == 1 and value_devices == 1 << bits and bits >= 4
    val, qry = lax.axis_index("val"), lax.axis_index("qry")
    core = lax.rem(val, 2)
    share = value_count // parts
    f32, bf16 = jnp.float32, jnp.bfloat16

    def flip(array, mask):
        return lax.ppermute(array, "val", [(i, i ^ mask) for i in range(value_devices)])

    def swap_shares(send):
        return jnp.stack([
            lax.ppermute(send[step - 1], "qry", [(i, (i + step) % parts) for i in range(parts)])
            for step in range(1, parts)
        ])

    def add(own, received):
        for array in received:
            own = own + array.astype(f32)
        return own

    def bit_of(bit):
        return lax.rem(val // (1 << bit), 2)

    square = lax.rem(val // 2, 4)
    place = jnp.stack([val, qry, core, square]).astype(jnp.int32)
    work = 2 * query_count * value_count * width

    delta, probs, dprobs, q_near, g_near, k_near = call(
        partial(forward_kernel, heads=heads, blocks=blocks, scale=scale),
        "forward_pass",
        (place,)
        + tuple(
            pltpu.with_memory_space_constraint(array, pltpu.HBM)
            for array in (
                compat, queries, out_grad, pool_keys, pool_values, lse, jnp.transpose(targets)
            )
        ),
        [IN_HBM] * 8,
        [
            pltpu.VMEM((2 * heads, query_count), f32),
            pltpu.VMEM((heads, value_count, query_count), f32),
            pltpu.VMEM((heads, value_count, query_count), f32),
            pltpu.VMEM(queries.shape, bf16),
            pltpu.VMEM(queries.shape, bf16),
            pltpu.VMEM(pool_keys.shape, bf16),
        ],
        4 * work,
        [
            pltpu.VMEM(pool_values.shape, bf16),
            pltpu.VMEM((heads, query_count), f32),
            pltpu.VMEM((heads, query_count), jnp.int32),
            pltpu.SMEM(compat.shape, jnp.int32),
            pltpu.SemaphoreType.DMA((5 + 2 * blocks,)),
        ],
    )
    shares = [
        pltpu.VMEM((share, wide), f32),
        pltpu.VMEM((parts - 1, share, wide), bf16),
    ]
    chunk = query_count // 3 if query_count % 384 == 0 else query_count
    rows_of = pltpu.VMEM((2, query_count, width), f32)
    targets = jnp.transpose(targets)

    def query_terms(own, name):
        return call(
            partial(query_kernel, own=own, chunk=chunk),
            name,
            (place, centre, probs, dprobs, targets, k_near),
            [IN_SMEM] + [IN_VMEM] * 5,
            [rows_of],
            2 * work,
        )[0]

    centre = delta
    other = query_terms(False, "other_head")
    received = None
    stride = 1
    added = [delta]
    while stride < value_devices:
        if stride > 1:
            terms = other if received is None else received
            delta, terms = call(
                delta_kernel,
                "delta_sum",
                (*added, terms),
                [IN_VMEM] * len(added) + [IN_HBM],
                [pltpu.VMEM((heads, query_count), f32), rows_of],
                heads * query_count,
                out_specs=[IN_VMEM, IN_HBM],
                aliases={len(added): 1},
            )
            received = flip(terms, 1) if received is None else terms
        steps = min(4, value_devices // stride)
        added = [delta] + [flip(delta, stride * step) for step in range(1, steps)]
        if stride == 1:
            other_centre = added[1]
        stride *= steps
    eighth = query_count // 8
    quarter = 2 * eighth
    keep, delta, *send = call(
        partial(combine_kernel, deltas=len(added), scale=scale),
        "combine",
        (place, query_terms(True, "own_head"), received, centre, other_centre, *added),
        [IN_SMEM] + [IN_VMEM] * (4 + len(added)),
        [
            pltpu.VMEM((quarter, width), f32),
            pltpu.VMEM((heads, query_count), f32),
        ]
        + [pltpu.VMEM((quarter, width), bf16)] * 3,
        work // 4,
    )
    def joined(total):
        for bit in range(3, bits - 1):
            split = total.reshape(2, -1, width)
            pick = partial(lax.dynamic_index_in_dim, split, axis=0, keepdims=False)
            came = flip(pick(1 - bit_of(bit)).astype(bf16), 1 << bit)
            total = pick(bit_of(bit)) + came.astype(f32)
        total = total.astype(bf16)
        (whole,) = call(
            join_kernel,
            "join",
            (total, flip(total, 1 << (bits - 1))),
            [IN_VMEM] * 2,
            [pltpu.VMEM(total.shape, bf16)],
            work // 16,
        )
        for bit in range(bits - 2, 2, -1):
            whole = jnp.concatenate([whole, flip(whole, 1 << bit)], axis=0)
        return whole

    value_own, value_send = call(
        value_kernel,
        "value_terms",
        (place, probs, g_near, delta),
        [IN_SMEM] + [IN_VMEM] * 2 + [IN_HBM],
        shares,
        2 * work,
    )
    value_came = swap_shares(value_send)
    key_own, key_send = call(
        partial(key_kernel, chunk=chunk, scale=scale),
        "key_terms",
        (place, delta, probs, dprobs, targets, q_near),
        [IN_SMEM] + [IN_VMEM] * 5,
        shares,
        2 * work,
        [pltpu.VMEM((heads, value_count, query_count), bf16)],
    )
    key_came = swap_shares(key_send)

    came = {step: flip(send[step - 1], 2 * step) for step in (3, 1, 2)}
    totals = call(
        reduce_kernel,
        "reduce",
        (keep, came[3], came[1], came[2], value_send, key_send),
        [IN_VMEM] * 4 + [IN_HBM] * 2,
        [pltpu.VMEM((eighth, width), bf16 if bits == 4 else f32)] * 2,
        work // 8,
    )
    piece = eighth >> (bits - 4)
    inner = 0
    for bit in range(3, bits - 1):
        inner = 2 * inner + bit_of(bit)

    key_grad, value_grad = call(
        pool_kernel,
        "pool_sum",
        (key_own, value_own, key_came, value_came),
        [IN_VMEM] * 4,
        [pltpu.HBM((share, wide), bf16)] * 2,
        work // 8,
    )
    pieces_place = jnp.stack([core, square, inner]).astype(jnp.int32)

    def gathered(total, after):
        whole = joined(total)
        others = {step: flip(whole, 2 * step) for step in (3, 1, 2)}
        return call(
            gather_kernel,
            "gather",
            (whole, others[3], others[1], others[2], *after),
            [IN_VMEM] * 4 + [IN_HBM] * len(after),
            [pltpu.VMEM((4 * eighth, width), bf16)],
            work // 16,
        )[0]

    near = partial(pltpu.with_memory_space_constraint, memory_space=pltpu.VMEM)
    far = partial(pltpu.with_memory_space_constraint, memory_space=pltpu.HBM)

    def placed(name, sources, before, aliases):
        copied = len(sources)
        return call(
            partial(place_kernel, sources=[source[1:] for source in sources], piece=piece),
            name,
            (pieces_place, *[near(source[0]) for source in sources], far(before)),
            [IN_SMEM] + [IN_VMEM] * copied + [IN_HBM],
            [pltpu.HBM((query_count, wide), bf16)],
            work // 2,
            [pltpu.SemaphoreType.DMA((copied * 4 * eighth // piece,))],
            [IN_HBM],
            {1 + copied: 0} if aliases else {},
        )[0]

    mine = [gathered(totals[0], ())]
    begun = placed("first_rows", [(mine[0], 0, 0)], key_grad, False)
    mine.append(gathered(totals[1], (far(begun),)))
    theirs = [flip(array, 1) for array in mine]
    begun = placed("own_rows", [(mine[1], 0, 1), (theirs[0], 1, 0)], begun, True)
    return placed("other_rows", [(theirs[1], 1, 1)], begun, True), key_grad, value_grad


def solution(mesh):
    placed = (
        P("qry", None),
        P("val", None),
        P("val", None),
        P("qry", None),
        P(None, "qry"),
        P(None, "val", "qry"),
        P("qry", None),
    )
    return jax.shard_map(
        on_device,
        mesh=mesh,
        in_specs=placed,
        out_specs=(P("qry", None), P(("val", "qry"), None), P(("val", "qry"), None)),
        check_vma=False,
    )
```

```python
import math
from functools import partial

import jax
import jax.numpy as jnp
from jax import lax
from jax.experimental import pallas as pl
from jax.experimental.pallas import tpu as pltpu
from jax.sharding import PartitionSpec as P

LOG2E = math.log2(math.e)
MASKED = 1e30
NT = (((1,), (1,)), ((), ()))
NN = (((1,), (0,)), ((), ()))
PARAMS = pltpu.CompilerParams(vmem_limit_bytes=16 * 1024 * 1024)
IN_VMEM = pl.BlockSpec(memory_space=pltpu.VMEM)
IN_SMEM = pl.BlockSpec(memory_space=pltpu.SMEM)
IN_HBM = pl.BlockSpec(memory_space=pl.ANY)


def dot(a, b, dims):
    return lax.dot_general(a, b, dims, preferred_element_type=jnp.float32)


def ways(start, size):
    return pl.ds(pl.multiple_of(start, size), size)


def forward_kernel(
    place, compat_hbm, q_hbm, g_hbm, k_hbm, v_hbm, lse_hbm, targets_hbm,
    delta_ref, probs_ref, dprobs_ref, q_ref, g_ref, k_ref,
    v_ref, lse_ref, targets_ref, compat, sems, *, heads, blocks, scale,
):
    value_count, width = k_ref.shape[0], k_ref.shape[1] // heads
    block = q_ref.shape[0] // blocks
    pairs = [
        (compat_hbm, compat), (targets_hbm, targets_ref), (lse_hbm, lse_ref),
        (k_hbm, k_ref), (v_hbm, v_ref),
    ]
    small = len(pairs)
    for index in range(blocks):
        rows = pl.ds(index * block, block)
        pairs += [(q_hbm.at[rows], q_ref.at[rows]), (g_hbm.at[rows], g_ref.at[rows])]
    copies = [pltpu.make_async_copy(*pair, sems.at[n]) for n, pair in enumerate(pairs)]
    for copy in copies:
        copy.start()
    for copy in copies[:3]:
        copy.wait()
    local = targets_ref[...] - lax.axis_index("val") * value_count
    hit = jnp.where((local >= 0) & (local < value_count), 1.0, 0.0)
    lives = []
    for index in range(blocks):
        live = jnp.max(hit[:, index * block : (index + 1) * block]) > 0.0
        for head in range(heads):
            live = live | (compat[head, 0, index] == 1)
        lives.append(live)
    for copy in copies[3:small]:
        copy.wait()
    for index in range(blocks):
        rows = slice(index * block, (index + 1) * block)
        copies[small + 2 * index].wait()
        copies[small + 2 * index + 1].wait()
        live = lives[index]

        @pl.when(live)
        def _():
            for head in range(heads):
                columns = slice(head * width, (head + 1) * width)
                usable = (hit[head : head + 1, rows] > 0.0) | (compat[head, 0, index] == 1)
                lse_rows = jnp.where(usable, lse_ref[head : head + 1, rows], MASKED) * LOG2E
                scores = dot(k_ref[:, columns], q_ref[rows, columns], NT)
                dprobs = dot(v_ref[:, columns], g_ref[rows, columns], NT)
                probs = jnp.exp2(scores * (scale * LOG2E) - lse_rows)
                delta = jnp.sum(probs * dprobs, axis=0, keepdims=True)
                weight = jnp.sum(probs, axis=0, keepdims=True)
                delta_ref[head : head + 1, rows] = delta
                centre = delta / jnp.maximum(weight, 1e-30)
                delta_ref[heads + head : heads + head + 1, rows] = centre
                probs_ref[head, :, rows] = probs
                dprobs_ref[head, :, rows] = dprobs

        @pl.when(jnp.logical_not(live))
        def _():
            for head in range(heads):
                for row in (head, heads + head):
                    delta_ref[row : row + 1, rows] = jnp.zeros((1, block), jnp.float32)
                probs_ref[head, :, rows] = jnp.zeros((value_count, block), jnp.float32)
                dprobs_ref[head, :, rows] = jnp.zeros((value_count, block), jnp.float32)


def value_kernel(place, probs_ref, g_ref, after_ref, own_ref, send_ref):
    heads, _, _ = probs_ref.shape
    width = g_ref.shape[1] // heads
    share = own_ref.shape[0]
    parts = send_ref.shape[0] + 1
    for step in range(parts):
        rows = ways(lax.rem(place[1] + step, parts) * share, share)
        for head in range(heads):
            columns = slice(head * width, (head + 1) * width)
            term = dot(probs_ref[head, rows, :].astype(jnp.bfloat16), g_ref[:, columns], NN)
            if step == 0:
                own_ref[:, columns] = term
            else:
                send_ref[step - 1, :, columns] = term.astype(jnp.bfloat16)


def onehot_less(terms, place, targets_ref, head, rows):
    local = targets_ref[pl.ds(head, 1), rows] - place[0] * terms.shape[0]
    slots = lax.broadcasted_iota(jnp.int32, terms.shape, 0)
    return jnp.where(slots == local, terms - 1.0, terms)


def query_kernel(
    place, delta_ref, probs_ref, dprobs_ref, targets_ref, k_ref, out_ref, *, own, chunk
):
    head = place[2] if own else 1 - place[2]
    width = out_ref.shape[2]
    heads = probs_ref.shape[0]
    keys = jnp.transpose(k_ref[:, ways(head * width, width)])
    for start in range(0, out_ref.shape[1], chunk):
        rows = slice(start, start + chunk)
        probs = probs_ref[head, :, rows]
        gap = dprobs_ref[head, :, rows] - (delta_ref[pl.ds(heads + head, 1), rows] - 1.0)
        terms = onehot_less(probs * gap, place, targets_ref, head, rows)
        for index, factor in enumerate((terms, probs)):
            product = dot(keys, factor.astype(jnp.bfloat16), NN)
            out_ref[index, rows, :] = jnp.transpose(product)


def delta_kernel(*refs):
    *added, terms_ref, out_ref, same_terms_ref = refs
    heads = out_ref.shape[0]
    out_ref[...] = sum(ref[:heads] for ref in added)


def combine_kernel(
    place, own_ref, received_ref, centre_ref, came_ref, *rest, deltas, scale
):
    added, (keep_ref, sum_ref, *send_refs) = rest[:deltas], rest[deltas:]
    rows, width = keep_ref.shape
    heads = sum_ref.shape[0]
    sum_ref[...] = sum(ref[...] for ref in added)

    def column(ref, span):
        row = sum_ref[pl.ds(place[2], 1), span] - ref[pl.ds(heads + place[2], 1), span]
        return jnp.transpose(jnp.broadcast_to(row * scale, (128, rows)))

    for step in (3, 1, 2, 0):
        target = send_refs[step - 1] if step else keep_ref
        span = ways((place[3] ^ step) * rows, rows)
        own_gap, came_gap = column(centre_ref, span), column(came_ref, span)
        for start in range(0, width, 128):
            columns = slice(start, start + 128)
            direct = own_ref[0, span, columns] + received_ref[0, span, columns]
            weighted = own_ref[1, span, columns] * own_gap
            weighted += received_ref[1, span, columns] * came_gap
            target[:, columns] = (scale * direct - weighted).astype(target.dtype)


def key_kernel(
    place, delta_ref, probs_ref, dprobs_ref, targets_ref, q_ref, own_ref, send_ref,
    low_ref, *, chunk, scale,
):
    heads = probs_ref.shape[0]
    width = own_ref.shape[1] // heads
    share = own_ref.shape[0]
    parts = send_ref.shape[0] + 1
    for head in range(heads):
        columns = slice(head * width, (head + 1) * width)
        for start in range(0, q_ref.shape[0], chunk):
            rows = slice(start, start + chunk)
            gap = dprobs_ref[head, :, rows] - (delta_ref[head : head + 1, rows] - 1.0)
            terms = onehot_less(probs_ref[head, :, rows] * gap, place, targets_ref, head, rows)
            low_ref[head, :, rows] = terms.astype(jnp.bfloat16)
        for step in range(parts):
            rows = ways(lax.rem(place[1] + step, parts) * share, share)
            term = scale * dot(low_ref[head, rows, :], q_ref[:, columns], NN)
            if step == 0:
                own_ref[:, columns] = term
            else:
                send_ref[step - 1, :, columns] = term.astype(jnp.bfloat16)


def reduce_kernel(keep_ref, first_ref, second_ref, third_ref, after_value, after_key, out_ref):
    total = keep_ref[...]
    for ref in (first_ref, second_ref, third_ref):
        total += ref[...].astype(jnp.float32)
    out_ref[...] = total.astype(out_ref.dtype)


def join_kernel(total_ref, came_ref, out_ref):
    total = total_ref[...].astype(jnp.float32) + came_ref[...].astype(jnp.float32)
    out_ref[...] = total.astype(jnp.bfloat16)


def gather_kernel(*refs):
    out_ref = refs[-1]
    rows = refs[0].shape[0]
    for index, ref in enumerate(refs[:3]):
        out_ref[index * rows : (index + 1) * rows] = ref[...]


def pool_kernel(key_ref, value_ref, key_came_ref, value_came_ref, key_out, value_out):
    key_sum, value_sum = key_ref[...], value_ref[...]
    for step in range(key_came_ref.shape[0]):
        key_sum += key_came_ref[step].astype(jnp.float32)
        value_sum += value_came_ref[step].astype(jnp.float32)
    key_out[...] = key_sum.astype(jnp.bfloat16)
    value_out[...] = value_sum.astype(jnp.bfloat16)


def after_kernel(*refs):
    pass


def place_kernel(place, *rest, sources, quarter, piece):
    out_ref, sems = rest[-2:]
    pieces = quarter // piece
    copies = []
    for ref, (side, steps) in zip(rest, sources):
        width = ref.shape[1]
        columns = ways((place[0] ^ side) * width, width)
        for index in range(len(steps) * pieces):
            turn, inner = divmod(index, pieces)
            block = (place[1] ^ steps[turn]) * pieces + (inner ^ place[2])
            copies.append(
                pltpu.make_async_copy(
                    ref.at[pl.ds(index * piece, piece)],
                    out_ref.at[ways(block * piece, piece), columns],
                    sems.at[len(copies)],
                )
            )
            copies[-1].start()
    for copy in copies:
        copy.wait()


def call(kernel, name, inputs, in_specs, outputs, flops, scratch=(), out_specs=None, aliases={}):
    return pl.pallas_call(
        kernel,
        in_specs=in_specs,
        out_specs=[IN_VMEM] * len(outputs) if out_specs is None else out_specs,
        out_shape=outputs,
        scratch_shapes=list(scratch),
        input_output_aliases=aliases,
        cost_estimate=pl.CostEstimate(flops=flops, bytes_accessed=flops // 1000, transcendentals=0),
        compiler_params=PARAMS,
        name=name,
    )(*inputs)


def on_device(queries, pool_keys, pool_values, out_grad, lse, compat, targets):
    heads, value_blocks, blocks = compat.shape
    query_count, wide = queries.shape
    value_count = pool_keys.shape[0]
    width = wide // heads
    scale = width ** -0.5
    value_devices, parts = lax.axis_size("val"), lax.axis_size("qry")
    bits = value_devices.bit_length() - 1
    assert heads == 2 and value_blocks == 1 and value_devices == 1 << bits and bits >= 4
    val, qry = lax.axis_index("val"), lax.axis_index("qry")
    core = lax.rem(val, 2)
    share = value_count // parts
    f32, bf16 = jnp.float32, jnp.bfloat16

    def flip(array, mask):
        return lax.ppermute(array, "val", [(i, i ^ mask) for i in range(value_devices)])

    def swap_shares(send):
        return jnp.stack([
            lax.ppermute(send[step - 1], "qry", [(i, (i + step) % parts) for i in range(parts)])
            for step in range(1, parts)
        ])

    def add(own, received):
        for array in received:
            own = own + array.astype(f32)
        return own

    def bit_of(bit):
        return lax.rem(val // (1 << bit), 2)

    square = lax.rem(val // 2, 4)
    place = jnp.stack([val, qry, core, square]).astype(jnp.int32)
    work = 2 * query_count * value_count * width

    delta, probs, dprobs, q_near, g_near, k_near = call(
        partial(forward_kernel, heads=heads, blocks=blocks, scale=scale),
        "forward_pass",
        (place,)
        + tuple(
            pltpu.with_memory_space_constraint(array, pltpu.HBM)
            for array in (
                compat, queries, out_grad, pool_keys, pool_values, lse, jnp.transpose(targets)
            )
        ),
        [IN_HBM] * 8,
        [
            pltpu.VMEM((2 * heads, query_count), f32),
            pltpu.VMEM((heads, value_count, query_count), f32),
            pltpu.VMEM((heads, value_count, query_count), f32),
            pltpu.VMEM(queries.shape, bf16),
            pltpu.VMEM(queries.shape, bf16),
            pltpu.VMEM(pool_keys.shape, bf16),
        ],
        4 * work,
        [
            pltpu.VMEM(pool_values.shape, bf16),
            pltpu.VMEM((heads, query_count), f32),
            pltpu.VMEM((heads, query_count), jnp.int32),
            pltpu.SMEM(compat.shape, jnp.int32),
            pltpu.SemaphoreType.DMA((5 + 2 * blocks,)),
        ],
    )
    shares = [
        pltpu.VMEM((share, wide), f32),
        pltpu.VMEM((parts - 1, share, wide), bf16),
    ]
    chunk = query_count // 3 if query_count % 384 == 0 else query_count
    rows_of = pltpu.VMEM((2, query_count, width), f32)
    targets = jnp.transpose(targets)

    def query_terms(own, name):
        return call(
            partial(query_kernel, own=own, chunk=chunk),
            name,
            (place, centre, probs, dprobs, targets, k_near),
            [IN_SMEM] + [IN_VMEM] * 5,
            [rows_of],
            2 * work,
        )[0]

    centre = delta
    other = query_terms(False, "other_head")
    received = None
    stride = 1
    added = [delta]
    while stride < value_devices:
        if stride > 1:
            terms = other if received is None else received
            delta, terms = call(
                delta_kernel,
                "delta_sum",
                (*added, terms),
                [IN_VMEM] * len(added) + [IN_HBM],
                [pltpu.VMEM((heads, query_count), f32), rows_of],
                heads * query_count,
                out_specs=[IN_VMEM, IN_HBM],
                aliases={len(added): 1},
            )
            received = flip(terms, 1) if received is None else terms
        steps = min(4, value_devices // stride)
        added = [delta] + [flip(delta, stride * step) for step in range(1, steps)]
        if stride == 1:
            other_centre = added[1]
        stride *= steps
    quarter = query_count // 4
    keep, delta, *send = call(
        partial(combine_kernel, deltas=len(added), scale=scale),
        "combine",
        (place, query_terms(True, "own_head"), received, centre, other_centre, *added),
        [IN_SMEM] + [IN_VMEM] * (4 + len(added)),
        [
            pltpu.VMEM((quarter, width), f32),
            pltpu.VMEM((heads, query_count), f32),
        ]
        + [pltpu.VMEM((quarter, width), bf16)] * 3,
        work // 4,
    )
    def joined(total):
        for bit in range(3, bits - 1):
            split = total.reshape(2, -1, width)
            pick = partial(lax.dynamic_index_in_dim, split, axis=0, keepdims=False)
            came = flip(pick(1 - bit_of(bit)).astype(bf16), 1 << bit)
            total = pick(bit_of(bit)) + came.astype(f32)
        total = total.astype(bf16)
        (whole,) = call(
            join_kernel,
            "join",
            (total, flip(total, 1 << (bits - 1))),
            [IN_VMEM] * 2,
            [pltpu.VMEM(total.shape, bf16)],
            work // 16,
        )
        for bit in range(bits - 2, 2, -1):
            whole = jnp.concatenate([whole, flip(whole, 1 << bit)], axis=0)
        return whole

    value_own, value_send = call(
        value_kernel,
        "value_terms",
        (place, probs, g_near, delta),
        [IN_SMEM] + [IN_VMEM] * 2 + [IN_HBM],
        shares,
        2 * work,
    )
    value_came = swap_shares(value_send)
    key_own, key_send = call(
        partial(key_kernel, chunk=chunk, scale=scale),
        "key_terms",
        (place, delta, probs, dprobs, targets, q_near),
        [IN_SMEM] + [IN_VMEM] * 5,
        shares,
        2 * work,
        [pltpu.VMEM((heads, value_count, query_count), bf16)],
    )
    key_came = swap_shares(key_send)

    came = {step: flip(send[step - 1], 2 * step) for step in (3, 1, 2)}
    (total,) = call(
        reduce_kernel,
        "reduce",
        (keep, came[3], came[1], came[2], value_send, key_send),
        [IN_VMEM] * 4 + [IN_HBM] * 2,
        [pltpu.VMEM((quarter, width), bf16 if bits == 4 else f32)],
        work // 8,
    )
    piece = quarter >> (bits - 4)
    inner = 0
    for bit in range(3, bits - 1):
        inner = 2 * inner + bit_of(bit)

    key_grad, value_grad = call(
        pool_kernel,
        "pool_sum",
        (key_own, value_own, key_came, value_came),
        [IN_VMEM] * 4,
        [pltpu.HBM((share, wide), bf16)] * 2,
        work // 8,
    )
    pieces_place = jnp.stack([core, square, inner]).astype(jnp.int32)

    near = partial(pltpu.with_memory_space_constraint, memory_space=pltpu.VMEM)
    far = partial(pltpu.with_memory_space_constraint, memory_space=pltpu.HBM)

    def placed(name, sources, before, aliases):
        copied = len(sources)
        return call(
            partial(
                place_kernel,
                sources=[source[1:] for source in sources],
                quarter=quarter,
                piece=piece,
            ),
            name,
            (pieces_place, *[near(source[0]) for source in sources], far(before)),
            [IN_SMEM] + [IN_VMEM] * copied + [IN_HBM],
            [pltpu.HBM((query_count, wide), bf16)],
            work // 2,
            [pltpu.SemaphoreType.DMA((4 * quarter // piece,))],
            [IN_HBM],
            {1 + copied: 0} if aliases else {},
        )[0]

    part = joined(total)
    steps = (3, 1, 2)
    others = [flip(part, 2 * step) for step in steps]
    begun = placed("first_rows", [(part, 0, (0,))], key_grad, False)
    (same_part,) = call(
        after_kernel,
        "after",
        (part, far(begun)),
        [IN_HBM] * 2,
        [pltpu.VMEM((quarter, width), bf16)],
        work // 1000,
        out_specs=[IN_HBM],
        aliases={0: 0},
    )
    part_came = flip(same_part, 1)
    (mine,) = call(
        gather_kernel,
        "gather",
        (*others, same_part),
        [IN_VMEM] * 3 + [IN_HBM],
        [pltpu.VMEM((3 * quarter, width), bf16)],
        work // 16,
    )
    theirs = flip(mine, 1)
    begun = placed("own_rows", [(mine, 0, steps), (part_came, 1, (0,))], begun, True)
    return placed("other_rows", [(theirs, 1, steps)], begun, True), key_grad, value_grad


def solution(mesh):
    placed = (
        P("qry", None),
        P("val", None),
        P("val", None),
        P("qry", None),
        P(None, "qry"),
        P(None, "val", "qry"),
        P("qry", None),
    )
    return jax.shard_map(
        on_device,
        mesh=mesh,
        in_specs=placed,
        out_specs=(P("qry", None), P(("val", "qry"), None), P(("val", "qry"), None)),
        check_vma=False,
    )
```

```python
import math
from functools import partial

import jax
import jax.numpy as jnp
from jax import lax
from jax.experimental import pallas as pl
from jax.experimental.pallas import tpu as pltpu
from jax.sharding import PartitionSpec as P

LOG2E = math.log2(math.e)
MASKED = 1e30
NT = (((1,), (1,)), ((), ()))
NN = (((1,), (0,)), ((), ()))
PARAMS = pltpu.CompilerParams(vmem_limit_bytes=16 * 1024 * 1024)
IN_VMEM = pl.BlockSpec(memory_space=pltpu.VMEM)
IN_SMEM = pl.BlockSpec(memory_space=pltpu.SMEM)
IN_HBM = pl.BlockSpec(memory_space=pl.ANY)


def dot(a, b, dims):
    return lax.dot_general(a, b, dims, preferred_element_type=jnp.float32)


def ways(start, size):
    return pl.ds(pl.multiple_of(start, size), size)


def forward_kernel(
    place, compat_hbm, q_hbm, g_hbm, k_hbm, v_hbm, lse_hbm, targets_hbm,
    delta_ref, probs_ref, dprobs_ref, q_ref, g_ref, k_ref,
    v_ref, lse_ref, targets_ref, compat, sems, *, heads, blocks, scale,
):
    value_count, width = k_ref.shape[0], k_ref.shape[1] // heads
    block = q_ref.shape[0] // blocks
    pairs = [
        (compat_hbm, compat), (targets_hbm, targets_ref), (lse_hbm, lse_ref),
        (k_hbm, k_ref), (v_hbm, v_ref),
    ]
    small = len(pairs)
    for index in range(blocks):
        rows = pl.ds(index * block, block)
        pairs += [(q_hbm.at[rows], q_ref.at[rows]), (g_hbm.at[rows], g_ref.at[rows])]
    copies = [pltpu.make_async_copy(*pair, sems.at[n]) for n, pair in enumerate(pairs)]
    for copy in copies:
        copy.start()
    for copy in copies[:3]:
        copy.wait()
    local = targets_ref[...] - lax.axis_index("val") * value_count
    hit = jnp.where((local >= 0) & (local < value_count), 1.0, 0.0)
    lives = []
    for index in range(blocks):
        live = jnp.max(hit[:, index * block : (index + 1) * block]) > 0.0
        for head in range(heads):
            live = live | (compat[head, 0, index] == 1)
        lives.append(live)
    for copy in copies[3:small]:
        copy.wait()
    for index in range(blocks):
        rows = slice(index * block, (index + 1) * block)
        copies[small + 2 * index].wait()
        copies[small + 2 * index + 1].wait()
        live = lives[index]

        @pl.when(live)
        def _():
            for head in range(heads):
                columns = slice(head * width, (head + 1) * width)
                usable = (hit[head : head + 1, rows] > 0.0) | (compat[head, 0, index] == 1)
                lse_rows = jnp.where(usable, lse_ref[head : head + 1, rows], MASKED) * LOG2E
                scores = dot(k_ref[:, columns], q_ref[rows, columns], NT)
                dprobs = dot(v_ref[:, columns], g_ref[rows, columns], NT)
                probs = jnp.exp2(scores * (scale * LOG2E) - lse_rows)
                delta = jnp.sum(probs * dprobs, axis=0, keepdims=True)
                weight = jnp.sum(probs, axis=0, keepdims=True)
                delta_ref[head : head + 1, rows] = delta
                centre = delta / jnp.maximum(weight, 1e-30)
                delta_ref[heads + head : heads + head + 1, rows] = centre
                probs_ref[head, :, rows] = probs
                dprobs_ref[head, :, rows] = dprobs

        @pl.when(jnp.logical_not(live))
        def _():
            for head in range(heads):
                for row in (head, heads + head):
                    delta_ref[row : row + 1, rows] = jnp.zeros((1, block), jnp.float32)
                probs_ref[head, :, rows] = jnp.zeros((value_count, block), jnp.float32)
                dprobs_ref[head, :, rows] = jnp.zeros((value_count, block), jnp.float32)


def value_kernel(place, probs_ref, g_ref, after_ref, own_ref, send_ref):
    heads, _, _ = probs_ref.shape
    width = g_ref.shape[1] // heads
    share = own_ref.shape[0]
    parts = send_ref.shape[0] + 1
    for step in range(parts):
        rows = ways(lax.rem(place[1] + step, parts) * share, share)
        for head in range(heads):
            columns = slice(head * width, (head + 1) * width)
            term = dot(probs_ref[head, rows, :].astype(jnp.bfloat16), g_ref[:, columns], NN)
            if step == 0:
                own_ref[:, columns] = term
            else:
                send_ref[step - 1, :, columns] = term.astype(jnp.bfloat16)


def onehot_less(terms, place, targets_ref, head, rows):
    local = targets_ref[pl.ds(head, 1), rows] - place[0] * terms.shape[0]
    slots = lax.broadcasted_iota(jnp.int32, terms.shape, 0)
    return jnp.where(slots == local, terms - 1.0, terms)


def query_kernel(
    place, delta_ref, probs_ref, dprobs_ref, targets_ref, k_ref, out_ref, *, own, chunk
):
    head = place[2] if own else 1 - place[2]
    width = out_ref.shape[2]
    heads = probs_ref.shape[0]
    keys = jnp.transpose(k_ref[:, ways(head * width, width)])
    for start in range(0, out_ref.shape[1], chunk):
        rows = slice(start, start + chunk)
        probs = probs_ref[head, :, rows]
        gap = dprobs_ref[head, :, rows] - (delta_ref[pl.ds(heads + head, 1), rows] - 1.0)
        terms = onehot_less(probs * gap, place, targets_ref, head, rows)
        for index, factor in enumerate((terms, probs)):
            product = dot(keys, factor.astype(jnp.bfloat16), NN)
            out_ref[index, rows, :] = jnp.transpose(product)


def delta_kernel(*refs):
    *added, terms_ref, out_ref, same_terms_ref = refs
    heads = out_ref.shape[0]
    out_ref[...] = sum(ref[:heads] for ref in added)


def combine_kernel(
    place, own_ref, received_ref, centre_ref, came_ref, *rest, deltas, scale
):
    added, (keep_ref, sum_ref, *send_refs) = rest[:deltas], rest[deltas:]
    rows, width = keep_ref.shape
    heads = sum_ref.shape[0]
    sum_ref[...] = sum(ref[...] for ref in added)

    def column(ref, span):
        row = sum_ref[pl.ds(place[2], 1), span] - ref[pl.ds(heads + place[2], 1), span]
        return jnp.transpose(jnp.broadcast_to(row * scale, (128, rows)))

    for step in (3, 1, 2, 0):
        target = send_refs[step - 1] if step else keep_ref
        span = ways((place[3] ^ step) * rows, rows)
        own_gap, came_gap = column(centre_ref, span), column(came_ref, span)
        for start in range(0, width, 128):
            columns = slice(start, start + 128)
            direct = own_ref[0, span, columns] + received_ref[0, span, columns]
            weighted = own_ref[1, span, columns] * own_gap
            weighted += received_ref[1, span, columns] * came_gap
            target[:, columns] = (scale * direct - weighted).astype(target.dtype)


def key_kernel(
    place, delta_ref, probs_ref, dprobs_ref, targets_ref, q_ref, own_ref, send_ref,
    low_ref, *, chunk, scale,
):
    heads = probs_ref.shape[0]
    width = own_ref.shape[1] // heads
    share = own_ref.shape[0]
    parts = send_ref.shape[0] + 1
    for head in range(heads):
        columns = slice(head * width, (head + 1) * width)
        for start in range(0, q_ref.shape[0], chunk):
            rows = slice(start, start + chunk)
            gap = dprobs_ref[head, :, rows] - (delta_ref[head : head + 1, rows] - 1.0)
            terms = onehot_less(probs_ref[head, :, rows] * gap, place, targets_ref, head, rows)
            low_ref[head, :, rows] = terms.astype(jnp.bfloat16)
        for step in range(parts):
            rows = ways(lax.rem(place[1] + step, parts) * share, share)
            term = scale * dot(low_ref[head, rows, :], q_ref[:, columns], NN)
            if step == 0:
                own_ref[:, columns] = term
            else:
                send_ref[step - 1, :, columns] = term.astype(jnp.bfloat16)


def reduce_kernel(keep_ref, first_ref, second_ref, third_ref, after_value, after_key, *out_refs):
    rows = out_refs[0].shape[0]
    for part, out_ref in enumerate(out_refs):
        span = slice(part * rows, (part + 1) * rows)
        total = keep_ref[span]
        for ref in (first_ref, second_ref, third_ref):
            total += ref[span].astype(jnp.float32)
        out_ref[...] = total.astype(out_ref.dtype)


def join_kernel(total_ref, came_ref, out_ref):
    total = total_ref[...].astype(jnp.float32) + came_ref[...].astype(jnp.float32)
    out_ref[...] = total.astype(jnp.bfloat16)


def gather_kernel(*refs):
    out_ref = refs[-1]
    rows = refs[0].shape[0]
    for ref, step in zip(refs, (0, 3, 1, 2)):
        out_ref[step * rows : (step + 1) * rows] = ref[...]


def after_kernel(*refs):
    pass


def pool_kernel(key_ref, value_ref, key_came_ref, value_came_ref, key_out, value_out):
    key_sum, value_sum = key_ref[...], value_ref[...]
    for step in range(key_came_ref.shape[0]):
        key_sum += key_came_ref[step].astype(jnp.float32)
        value_sum += value_came_ref[step].astype(jnp.float32)
    key_out[...] = key_sum.astype(jnp.bfloat16)
    value_out[...] = value_sum.astype(jnp.bfloat16)


def place_kernel(place, *rest, sources, piece):
    out_ref, sems = rest[-2:]
    copies = []
    for ref, (side, part) in zip(rest, sources):
        width = ref.shape[1]
        columns = ways((place[0] ^ side) * width, width)
        pieces = ref.shape[0] // (4 * piece)
        for index in range(4 * pieces):
            step, inner = divmod(index, pieces)
            block = (2 * (place[1] ^ step) + part) * pieces + (inner ^ place[2])
            copies.append(
                pltpu.make_async_copy(
                    ref.at[pl.ds(index * piece, piece)],
                    out_ref.at[ways(block * piece, piece), columns],
                    sems.at[len(copies)],
                )
            )
            copies[-1].start()
    for copy in copies:
        copy.wait()


def call(kernel, name, inputs, in_specs, outputs, flops, scratch=(), out_specs=None, aliases={}):
    return pl.pallas_call(
        kernel,
        in_specs=in_specs,
        out_specs=[IN_VMEM] * len(outputs) if out_specs is None else out_specs,
        out_shape=outputs,
        scratch_shapes=list(scratch),
        input_output_aliases=aliases,
        cost_estimate=pl.CostEstimate(flops=flops, bytes_accessed=flops // 1000, transcendentals=0),
        compiler_params=PARAMS,
        name=name,
    )(*inputs)


def on_device(queries, pool_keys, pool_values, out_grad, lse, compat, targets):
    heads, value_blocks, blocks = compat.shape
    query_count, wide = queries.shape
    value_count = pool_keys.shape[0]
    width = wide // heads
    scale = width ** -0.5
    value_devices, parts = lax.axis_size("val"), lax.axis_size("qry")
    bits = value_devices.bit_length() - 1
    assert heads == 2 and value_blocks == 1 and value_devices == 1 << bits and bits >= 4
    val, qry = lax.axis_index("val"), lax.axis_index("qry")
    core = lax.rem(val, 2)
    share = value_count // parts
    f32, bf16 = jnp.float32, jnp.bfloat16

    def flip(array, mask):
        return lax.ppermute(array, "val", [(i, i ^ mask) for i in range(value_devices)])

    def swap_shares(send):
        return jnp.stack([
            lax.ppermute(send[step - 1], "qry", [(i, (i + step) % parts) for i in range(parts)])
            for step in range(1, parts)
        ])

    def add(own, received):
        for array in received:
            own = own + array.astype(f32)
        return own

    def bit_of(bit):
        return lax.rem(val // (1 << bit), 2)

    square = lax.rem(val // 2, 4)
    place = jnp.stack([val, qry, core, square]).astype(jnp.int32)
    work = 2 * query_count * value_count * width

    delta, probs, dprobs, q_near, g_near, k_near = call(
        partial(forward_kernel, heads=heads, blocks=blocks, scale=scale),
        "forward_pass",
        (place,)
        + tuple(
            pltpu.with_memory_space_constraint(array, pltpu.HBM)
            for array in (
                compat, queries, out_grad, pool_keys, pool_values, lse, jnp.transpose(targets)
            )
        ),
        [IN_HBM] * 8,
        [
            pltpu.VMEM((2 * heads, query_count), f32),
            pltpu.VMEM((heads, value_count, query_count), f32),
            pltpu.VMEM((heads, value_count, query_count), f32),
            pltpu.VMEM(queries.shape, bf16),
            pltpu.VMEM(queries.shape, bf16),
            pltpu.VMEM(pool_keys.shape, bf16),
        ],
        4 * work,
        [
            pltpu.VMEM(pool_values.shape, bf16),
            pltpu.VMEM((heads, query_count), f32),
            pltpu.VMEM((heads, query_count), jnp.int32),
            pltpu.SMEM(compat.shape, jnp.int32),
            pltpu.SemaphoreType.DMA((5 + 2 * blocks,)),
        ],
    )
    shares = [
        pltpu.VMEM((share, wide), f32),
        pltpu.VMEM((parts - 1, share, wide), bf16),
    ]
    chunk = query_count // 3 if query_count % 384 == 0 else query_count
    rows_of = pltpu.VMEM((2, query_count, width), f32)
    targets = jnp.transpose(targets)

    def query_terms(own, name):
        return call(
            partial(query_kernel, own=own, chunk=chunk),
            name,
            (place, centre, probs, dprobs, targets, k_near),
            [IN_SMEM] + [IN_VMEM] * 5,
            [rows_of],
            2 * work,
        )[0]

    centre = delta
    other = query_terms(False, "other_head")
    received = None
    stride = 1
    added = [delta]
    while stride < value_devices:
        if stride > 1:
            terms = other if received is None else received
            delta, terms = call(
                delta_kernel,
                "delta_sum",
                (*added, terms),
                [IN_VMEM] * len(added) + [IN_HBM],
                [pltpu.VMEM((heads, query_count), f32), rows_of],
                heads * query_count,
                out_specs=[IN_VMEM, IN_HBM],
                aliases={len(added): 1},
            )
            received = flip(terms, 1) if received is None else terms
        steps = min(4, value_devices // stride)
        added = [delta] + [flip(delta, stride * step) for step in range(1, steps)]
        if stride == 1:
            other_centre = added[1]
        stride *= steps
    eighth = query_count // 8
    quarter = 2 * eighth
    keep, delta, *send = call(
        partial(combine_kernel, deltas=len(added), scale=scale),
        "combine",
        (place, query_terms(True, "own_head"), received, centre, other_centre, *added),
        [IN_SMEM] + [IN_VMEM] * (4 + len(added)),
        [
            pltpu.VMEM((quarter, width), f32),
            pltpu.VMEM((heads, query_count), f32),
        ]
        + [pltpu.VMEM((quarter, width), bf16)] * 3,
        work // 4,
    )
    swapped = []

    def joined(total):
        for bit in range(3, bits - 1):
            split = total.reshape(2, -1, width)
            pick = partial(lax.dynamic_index_in_dim, split, axis=0, keepdims=False)
            came = flip(pick(1 - bit_of(bit)).astype(bf16), 1 << bit)
            total = pick(bit_of(bit)) + came.astype(f32)
        total = total.astype(bf16)
        if swapped:
            (total,) = call(
                after_kernel,
                "after",
                (total, swapped[0]),
                [IN_HBM] * 2,
                [pltpu.VMEM(total.shape, bf16)],
                work // 1000,
                out_specs=[IN_HBM],
                aliases={0: 0},
            )
        swapped.append(flip(total, 1 << (bits - 1)))
        (whole,) = call(
            join_kernel,
            "join",
            (total, swapped[-1]),
            [IN_VMEM] * 2,
            [pltpu.VMEM(total.shape, bf16)],
            work // 16,
        )
        for bit in range(bits - 2, 2, -1):
            whole = jnp.concatenate([whole, flip(whole, 1 << bit)], axis=0)
        return whole

    value_own, value_send = call(
        value_kernel,
        "value_terms",
        (place, probs, g_near, delta),
        [IN_SMEM] + [IN_VMEM] * 2 + [IN_HBM],
        shares,
        2 * work,
    )
    value_came = swap_shares(value_send)
    key_own, key_send = call(
        partial(key_kernel, chunk=chunk, scale=scale),
        "key_terms",
        (place, delta, probs, dprobs, targets, q_near),
        [IN_SMEM] + [IN_VMEM] * 5,
        shares,
        2 * work,
        [pltpu.VMEM((heads, value_count, query_count), bf16)],
    )
    key_came = swap_shares(key_send)

    came = {step: flip(send[step - 1], 2 * step) for step in (3, 1, 2)}
    totals = call(
        reduce_kernel,
        "reduce",
        (keep, came[3], came[1], came[2], value_send, key_send),
        [IN_VMEM] * 4 + [IN_HBM] * 2,
        [pltpu.VMEM((eighth, width), bf16 if bits == 4 else f32)] * 2,
        work // 8,
    )
    piece = eighth >> (bits - 4)
    inner = 0
    for bit in range(3, bits - 1):
        inner = 2 * inner + bit_of(bit)

    key_grad, value_grad = call(
        pool_kernel,
        "pool_sum",
        (key_own, value_own, key_came, value_came),
        [IN_VMEM] * 4,
        [pltpu.HBM((share, wide), bf16)] * 2,
        work // 8,
    )
    pieces_place = jnp.stack([core, square, inner]).astype(jnp.int32)

    def gathered(total, after):
        whole = joined(total)
        others = {step: flip(whole, 2 * step) for step in (3, 1, 2)}
        return call(
            gather_kernel,
            "gather",
            (whole, others[3], others[1], others[2], *after),
            [IN_VMEM] * 4 + [IN_HBM] * len(after),
            [pltpu.VMEM((4 * eighth, width), bf16)],
            work // 16,
        )[0]

    near = partial(pltpu.with_memory_space_constraint, memory_space=pltpu.VMEM)
    far = partial(pltpu.with_memory_space_constraint, memory_space=pltpu.HBM)

    def placed(name, sources, before, aliases):
        copied = len(sources)
        return call(
            partial(place_kernel, sources=[source[1:] for source in sources], piece=piece),
            name,
            (pieces_place, *[near(source[0]) for source in sources], far(before)),
            [IN_SMEM] + [IN_VMEM] * copied + [IN_HBM],
            [pltpu.HBM((query_count, wide), bf16)],
            work // 2,
            [pltpu.SemaphoreType.DMA((copied * 4 * eighth // piece,))],
            [IN_HBM],
            {1 + copied: 0} if aliases else {},
        )[0]

    mine = [gathered(totals[0], ())]
    begun = placed("first_rows", [(mine[0], 0, 0)], key_grad, False)
    mine.append(gathered(totals[1], (far(begun),)))
    theirs = [flip(array, 1) for array in mine]
    begun = placed("own_rows", [(mine[1], 0, 1), (theirs[0], 1, 0)], begun, True)
    return placed("other_rows", [(theirs[1], 1, 1)], begun, True), key_grad, value_grad


def solution(mesh):
    placed = (
        P("qry", None),
        P("val", None),
        P("val", None),
        P("qry", None),
        P(None, "qry"),
        P(None, "val", "qry"),
        P("qry", None),
    )
    return jax.shard_map(
        on_device,
        mesh=mesh,
        in_specs=placed,
        out_specs=(P("qry", None), P(("val", "qry"), None), P(("val", "qry"), None)),
        check_vma=False,
    )
```
